32 devices in a mesh: groups: 2 (over x), dp: 16 (over z, y, core).
Axes of the slice: x: 2, y: 2, z: 4, core: 2. Of those that a mesh axis runs over, the one named last changes fastest.
Arguments:
- query_rows: bfloat16 [32, 32, 768], P(('groups', 'dp')), parts along dimension 0, may hold values from -6 to 6
- proj_weight: bfloat16 [768, 4096], replicated, may hold values from -0.21875 to 0.21875
- proj_bias: bfloat16 [4096], replicated, may hold values from -3 to 3
- candidates: int32 [32, 2], P(('groups', 'dp')), parts along dimension 0, may hold values from 0 to 15, as said below
- caption_states: bfloat16 [32, 4, 4096], P(('groups', 'dp')), parts along dimension 0, may hold values from -24 to 24
- caption_ids: int32 [32, 4], P(('groups', 'dp')), parts along dimension 0, may hold values from 0 to 32127
- caption_lengths: int32 [32], P(('groups', 'dp')), parts along dimension 0, may hold values from 1 to 4
- norm_gain: float32 [4096], replicated, may hold values from 0.5 to 1.5
- head_weight: bfloat16 [4096, 32128], P(None, 'dp'), may hold values from -0.5 to 0.5
Outputs:
- token_loglik: float32 [32, 2, 4], P(('groups', 'dp')), parts along dimension 0
The draws below stay inside these ranges and needn't reach their ends.
There are 2 independent parts, one for each index of `groups`. The reference program is written for one: setup_inputs(seed, part) draws one part's arguments, and reference() takes and returns one part's arrays. A program takes and returns all parts, laid end to end along the dimension named above; an argument that names none is the same for every part. Nothing has to cross between parts.
Inputs may be any that keep to these rules, and one draw needn't show every extreme that they name: Entry (i, k) names stored caption c, held on data shard c. The candidates of one data shard's images name distinct data shards. Each data shard's captions are named by at most 4 candidates in all, and some data shard's by exactly that many.
All inputs are finite; a program needn't handle non-finite values.
Results may differ from the reference program's by a relative error of at most 0.0006.
Values may be sent and summed in bfloat16 or wider, within the bound.
No kernel may reach another device: no remote copies, remote signals or barrier semaphores. Data moves between devices by JAX's collectives and lax.ppermute only.
A program may use at most 128 MiB of HBM per device.

```python
import math
import jax
import jax.numpy as jnp
import numpy as np
from jax import lax

D = 4096
HEAD_DIM = 64
QDIM = 768
PREFIX = 32
VOCAB = 32128
TOPK = 2
CAP_LEN = 4
IMG_DEV = 1
IMAGES = 16
CAP_DEV = 1
CAPTIONS = 16
N_DP = 16


def draw_candidates(key, part):
    devices = N_DP
    per_shard = IMG_DEV * TOPK
    key_order = jax.random.fold_in(key, 11)
    key_shift = jax.random.fold_in(key, 23)
    order = jax.random.permutation(key_order, devices)
    ranks = jnp.arange(devices)
    loads = jnp.where(ranks < devices // 4, 2 * per_shard, jnp.where(ranks < 3 * devices // 4, per_shard, 0))
    starts = jnp.cumsum(loads) - loads
    source = jnp.arange(devices)[:, None]
    within = jnp.arange(per_shard)[None, :]
    slots = within * devices + source
    block_rank = jnp.sum((starts[None, None, :] <= slots[:, :, None]).astype(jnp.int32), -1) - 1
    owners = jnp.take(order, block_rank)
    offset = slots - jnp.take(starts, block_rank)
    shifts = jax.random.randint(key_shift, (devices,), 0, CAP_DEV)
    stored_row = (offset + jnp.take(shifts, owners)) % CAP_DEV
    chosen = owners * CAP_DEV + stored_row
    return chosen.reshape(devices * IMG_DEV, TOPK).astype(jnp.int32)


def draw_caption_states(key, part):
    values = jax.random.normal(jax.random.fold_in(key, 5), (CAPTIONS, CAP_LEN, D), jnp.float32)
    values = jnp.clip(values, -6.0, 6.0)
    return values.astype(jnp.bfloat16)


def draw_head_weight(key, part):
    spread = (9.0 / D) ** 0.5
    limit = min(6.0, 0.5 / spread)
    values = jax.random.normal(jax.random.fold_in(key, 3), (D, VOCAB), jnp.float32)
    values = jnp.clip(values, -limit, limit) * spread
    return values.astype(jnp.bfloat16)


def set_ends(entries, own_key, smallest, high):
    longest = entries.shape.index(max(entries.shape))
    spots = []
    for shift in (0, 1):
        where = [jax.random.randint(jax.random.fold_in(own_key, axis), (), 0, length) for axis, length in enumerate(entries.shape)]
        where[longest] = (where[longest] + shift) % entries.shape[longest]
        spots.append(tuple(where))
    return entries.at[spots[0]].set(smallest).at[spots[1]].set(high)


def block_levels(own_key, shape, shards, smallest, high):
    level = 1.0
    for position, parts in shards:
        draws = jax.random.uniform(jax.random.fold_in(jax.random.fold_in(own_key, 6), position), (parts,), jnp.float32, smallest / len(shards), high / len(shards))
        level = level * jnp.repeat(jnp.exp(draws), shape[position] // parts).reshape((-1,) + (1,) * (len(shape) - 1 - position))
    return level


def rank_table(count, lean):
    weights = [(1 << 20) // math.isqrt(grade ** lean) + 1 for grade in range(1, count + 1)]
    scale = 1 + sum(weights) // (1 << 30)
    return np.cumsum(np.array([max(1, weight // scale) for weight in weights]))


def skewed_ids(own_key, dims, number_of, lean):
    listing = rank_table(number_of, lean)
    pick = jax.random.randint(jax.random.fold_in(own_key, 1), dims, 0, int(listing[number_of - 1]))
    rank = jnp.searchsorted(jnp.asarray(listing, jnp.int32), pick, side="right")
    return jax.random.permutation(jax.random.fold_in(own_key, 2), number_of)[rank].astype(jnp.int32)


def noise(own_key, shape, scale, bound, split=(), held_as=jnp.bfloat16):
    values = scale * jax.random.normal(own_key, shape, jnp.float32)
    if split:
        values = values * block_levels(own_key, shape, split, -0.22, 0.18)
    return jnp.clip(values, -bound, bound).astype(held_as)


def setup_inputs(seed: int = 0, part: int = 0) -> dict:
    streams_of = jax.random.split(jax.random.key(seed), 10)
    part_splits = jax.random.split(jax.random.fold_in(streams_of[9], part), 10)
    return {
        "query_rows": noise(part_splits[0], (IMAGES, PREFIX, QDIM), 1.0, 6.0, ((0, 16),)),
        "proj_weight": noise(streams_of[1], (QDIM, D), QDIM ** -0.5, 0.21875),
        "proj_bias": noise(streams_of[2], (D,), 0.5, 3.0),
        "candidates": draw_candidates(jax.random.fold_in(jax.random.fold_in(streams_of[9], part), 71), part),
        "caption_states": draw_caption_states(jax.random.fold_in(jax.random.fold_in(streams_of[9], part), 71), part),
        "caption_ids": set_ends(skewed_ids(part_splits[5], (CAPTIONS, CAP_LEN), VOCAB, 2), jax.random.fold_in(part_splits[5], 3), 0, VOCAB - 1).astype(jnp.int32),
        "caption_lengths": set_ends(jax.random.randint(part_splits[6], (CAPTIONS,), 1, CAP_LEN + 1), jax.random.fold_in(part_splits[6], 1), 1, CAP_LEN).astype(jnp.int32),
        "norm_gain": jnp.clip(1.0 + 0.1 * jax.random.normal(streams_of[7], (D,), jnp.float32), 0.5, 1.5),
        "head_weight": draw_head_weight(jax.random.fold_in(streams_of[9], 71), part),
    }


score_scale = 0.015625
eps = 1e-06

def project(rows, proj_weight, proj_bias):
    summed = jnp.dot(rows, proj_weight, preferred_element_type=jnp.float32)
    return (summed + proj_bias.astype(jnp.float32)).astype(jnp.bfloat16)

def attend(projected, states, norm_gain):
    prefix_len = projected.shape[0]
    cap_len, width = states.shape
    heads = width // HEAD_DIM
    keys = jnp.concatenate([projected, states], 0)
    query = states.reshape(cap_len, heads, HEAD_DIM).astype(jnp.float32)
    keyed = keys.reshape(prefix_len + cap_len, heads, HEAD_DIM).astype(jnp.float32)
    scores = jnp.einsum('thd,jhd->htj', query, keyed) * score_scale
    key_pos = jnp.arange(prefix_len + cap_len)[None, :]
    tok_pos = jnp.arange(cap_len)[:, None]
    allowed = (key_pos < prefix_len) | (key_pos - prefix_len <= tok_pos)
    scores = jnp.where(allowed[None], scores, -jnp.inf)
    row_max = lax.optimization_barrier(jnp.max(scores, -1, keepdims=True))
    expo = jnp.exp(scores - row_max)
    weights = (expo / lax.optimization_barrier(jnp.sum(expo, -1, keepdims=True))).astype(jnp.bfloat16)
    mixed_out = jnp.einsum('htj,jhd->thd', weights.astype(jnp.float32), keyed).reshape(cap_len, width)
    mixed = states.astype(jnp.float32) + mixed_out
    normed = mixed * lax.rsqrt(lax.optimization_barrier(jnp.mean(mixed * mixed, -1, keepdims=True)) + eps) * norm_gain
    return normed.astype(jnp.bfloat16)

def reference(query_rows, proj_weight, proj_bias, candidates, caption_states, caption_ids, caption_lengths, norm_gain, head_weight):

    def one_image(inputs):
        rows, chosen = inputs
        projected = project(rows, proj_weight, proj_bias)
        states = caption_states[chosen]
        return jax.vmap(lambda one: attend(projected, one, norm_gain))(states)
    hidden_all = lax.map(one_image, (query_rows, candidates))
    token_ids = caption_ids[candidates].reshape(-1)
    lengths = caption_lengths[candidates]
    width = hidden_all.shape[-1]
    row_blocks = hidden_all.reshape(4, -1, width)
    id_blocks = token_ids.reshape(4, -1)

    def score_block(inputs):
        block, block_ids = inputs
        logits = jnp.dot(block, head_weight, preferred_element_type=jnp.float32)
        row_max = lax.optimization_barrier(jnp.max(logits, -1))
        row_sum = lax.optimization_barrier(jnp.sum(jnp.exp(logits - row_max[:, None]), -1))
        picked = jnp.take_along_axis(logits, block_ids[:, None], 1)[:, 0]
        return picked - (row_max + jnp.log(row_sum))
    loglik = lax.map(score_block, (row_blocks, id_blocks)).reshape(lengths.shape + (CAP_LEN,))
    inside = jnp.arange(CAP_LEN)[None, None, :] < lengths[:, :, None]
    return jnp.where(inside, loglik, jnp.float32(0.0))
```

```python
import jax
import jax.numpy as jnp
from jax import lax
from jax.experimental import pallas as pl
from jax.experimental.pallas import tpu as pltpu
from jax.sharding import PartitionSpec as P

HEAD_DIM = 64
LANES = 128
DIGIT = 256
MIB = 1 << 20


score_scale = 0.015625
eps = 1e-06

VMEM = pl.BlockSpec(memory_space=pltpu.VMEM)
SMEM = pl.BlockSpec(memory_space=pltpu.SMEM)


def iota(shape, dim):
    return lax.broadcasted_iota(jnp.int32, shape, dim)


def pack_kernel(cand_ref, ids_ref, len_ref, rows_ref, states_ref, out_ref, stage):
    prefix, width = rows_ref.shape[1:]
    cap_len, model_width = states_ref.shape[1:]
    out_ref[0:prefix, :] = rows_ref[0]
    states = states_ref[0].astype(jnp.float32)
    pieces = -(-model_width // width)
    for c in range(pieces - 1):
        stage[c * cap_len : (c + 1) * cap_len, :] = states[:, c * width : (c + 1) * width]
    rest = model_width - (pieces - 1) * width
    last = (pieces - 1) * cap_len
    stage[last : last + cap_len, 0:rest] = states[:, model_width - rest :]
    token, lane = iota((cap_len, width - rest), 0), iota((cap_len, width - rest), 1)
    ids = jnp.zeros_like(token)
    for t in range(cap_len):
        ids = jnp.where(token == t, ids_ref[0, t], ids)
    digits = jnp.where(lane == 0, ids // DIGIT, jnp.where(lane == 1, ids % DIGIT, 0))
    digits = jnp.where(lane == 2, len_ref[0], digits)
    stage[last : last + cap_len, rest:] = digits.astype(jnp.float32)
    tail = stage.shape[0] - last - cap_len
    row, lane = iota((tail, width), 0), iota((tail, width), 1)
    cand = jnp.where(row < cap_len, cand_ref[0, 0], cand_ref[0, 1])
    digits = jnp.where(lane == 0, cand // DIGIT, jnp.where(lane == 1, cand % DIGIT, 0))
    stage[last + cap_len :, :] = digits.astype(jnp.float32)
    out_ref[prefix:, :] = stage[...].astype(jnp.bfloat16)


def number(digits):
    lane = iota(digits.shape, 1)
    scaled = jnp.where(lane == 0, digits * DIGIT, jnp.where(lane == 1, digits, 0.0))
    return jnp.sum(scaled, 1, keepdims=True).astype(jnp.int32)


def hidden_kernel(blocks, *refs):
    (pos_ref, *msgs), (weight_ref, bias_ref, gain_ref, out_ref, keys, caps, rows, query, mixed) = (
        refs[: 2 * blocks + 1],
        refs[2 * blocks + 1 :],
    )
    width = rows.shape[1]
    model_width = query.shape[1] - LANES
    prefix = rows.shape[0] // blocks
    held = msgs[0].shape[0] - prefix
    pair_rows = query.shape[0] // blocks
    cap_len = 4
    row_total = query.shape[0]
    for j in range(blocks):
        rows[j * prefix : (j + 1) * prefix, :] = msgs[j][0:prefix, :]
    for j in range(2 * blocks):
        caps[j * held : (j + 1) * held, :] = msgs[j][prefix:, :]
    tail = 16
    cand = jnp.concatenate(
        [msgs[j][prefix + held - tail :, 0:LANES].astype(jnp.float32)[tail - pair_rows :] for j in range(blocks)], 0
    )
    away = number(cand) ^ pos_ref[0]
    token = iota((row_total, 1), 0) % cap_len
    first = ((away & 1) * blocks + (away >> 1)) * held + token
    column = iota((row_total, 2 * blocks * held), 1)
    pieces = -(-model_width // width)
    for c in range(pieces):
        pick = jnp.where(column == first + c * cap_len, 1.0, 0.0).astype(jnp.bfloat16)
        span = min(width, query.shape[1] - c * width)
        query[:, c * width : c * width + span] = jnp.dot(
            pick, caps[:, 0:span], preferred_element_type=jnp.float32
        ).astype(jnp.bfloat16)
    step = 512

    @pl.loop(0, model_width // step)
    def _(i):
        cols = pl.ds(pl.multiple_of(i * step, step), step)
        summed = jnp.dot(rows[...], weight_ref[:, cols], preferred_element_type=jnp.float32)
        keys[:, cols] = (summed + bias_ref[:, cols].astype(jnp.float32)).astype(jnp.bfloat16)

    lane = iota((row_total, LANES), 1)
    low = lane < HEAD_DIM
    key_total = keys.shape[0]
    two = 2 * row_total
    r, k = iota((two, key_total), 0) % row_total, iota((two, key_total), 1)
    image_ok = (r // pair_rows) == (k // prefix)
    r, k = iota((two, row_total), 0) % row_total, iota((two, row_total), 1)
    own_ok = ((r // cap_len) == (k // cap_len)) & (k <= r)
    nothing = jnp.float32(-1e30)
    contract = (((1,), (1,)), ((), ()))

    def heads(i, square):
        cols = pl.ds(pl.multiple_of(i * LANES, LANES), LANES)
        q, key = query[:, cols], keys[:, cols]
        zero = jnp.zeros_like(q)
        both = jnp.concatenate([jnp.where(low, q, zero), jnp.where(low, zero, q)], 0)
        image = lax.dot_general(both, key, contract, preferred_element_type=jnp.float32) * score_scale
        own = lax.dot_general(both, q, contract, preferred_element_type=jnp.float32) * score_scale
        image, own = jnp.where(image_ok, image, nothing), jnp.where(own_ok, own, nothing)
        top = jnp.maximum(jnp.max(image, 1, keepdims=True), jnp.max(own, 1, keepdims=True))
        image, own = jnp.exp(image - top), jnp.exp(own - top)
        total = 1.0 / (jnp.sum(image, 1, keepdims=True) + jnp.sum(own, 1, keepdims=True))
        out = jnp.dot((image * total).astype(jnp.bfloat16), key, preferred_element_type=jnp.float32)
        out += jnp.dot((own * total).astype(jnp.bfloat16), q, preferred_element_type=jnp.float32)
        value = q.astype(jnp.float32) + jnp.where(low, out[:row_total], out[row_total:])
        mixed[:, cols] = value
        return square + value * value

    square = lax.fori_loop(
        0, model_width // LANES, heads, jnp.zeros((row_total, LANES), jnp.float32), unroll=4
    )
    scale = lax.rsqrt(jnp.sum(square, 1, keepdims=True) / model_width + eps)
    out_ref[:, 0:model_width] = (mixed[...] * scale * gain_ref[...]).astype(jnp.bfloat16)
    out_ref[:, model_width:] = query[:, model_width:]


def logits_kernel(pos_ref, mine_ref, other_ref, head_ref, out_ref, states, logits):
    half = mine_ref.shape[0]
    model_width, vocab = head_ref.shape
    states[0:half, :] = mine_ref[:, 0:model_width]
    states[half:, :] = other_ref[:, 0:model_width]
    row_total = 2 * half
    step = 256

    @pl.loop(0, vocab // step)
    def _(i):
        cols = pl.ds(pl.multiple_of(i * step, step), step)
        logits[:, cols] = jnp.dot(states[...], head_ref[:, cols], preferred_element_type=jnp.float32)

    done = vocab // step * step
    if done < vocab:
        logits[:, done:vocab] = jnp.dot(
            states[...], head_ref[:, done:vocab], preferred_element_type=jnp.float32
        )
    ids = jnp.concatenate(
        [number(ref[:, model_width:].astype(jnp.float32)) for ref in (mine_ref, other_ref)], 0
    )
    values = logits[:, 0:vocab]
    top = jnp.max(values, 1, keepdims=True)
    total = jnp.sum(jnp.exp(values - top), 1, keepdims=True)
    hit = iota((row_total, vocab), 1) == ids - pos_ref[0] * vocab
    target = jnp.sum(jnp.where(hit, values, 0.0), 1, keepdims=True)
    lane = iota((row_total, LANES), 1)
    packed = jnp.where(lane == 0, top, jnp.where(lane == 1, total, jnp.where(lane == 2, target, 0.0)))
    shards, rows = out_ref.shape[:2]
    for j in range(shards):
        away = (j % (shards // 2)) * 2 + j // (shards // 2)
        out_ref[pos_ref[0] ^ away] = packed[j * rows : (j + 1) * rows]


def finish_kernel(stats_ref, mine_ref, out_ref):
    stats = stats_ref[...]
    shards, rows, _ = stats.shape
    cap_len = out_ref.shape[2]
    model_width = mine_ref.shape[1] - LANES
    lane = iota((rows, LANES), 1)
    top = jnp.max(stats, 0)[:, 0:1]
    total = jnp.zeros((rows, 1), jnp.float32)
    target = jnp.zeros((rows, 1), jnp.float32)
    for e in range(shards):
        total += stats[e][:, 1:2] * jnp.exp(stats[e][:, 0:1] - top)
        target += stats[e][:, 2:3]
    loglik = target - (top + jnp.log(total))
    lengths = mine_ref[0:16, model_width:].astype(jnp.float32)[0:rows, 2:3]
    token = iota((rows, LANES), 0) % cap_len
    kept = (token == lane) & (token.astype(jnp.float32) < lengths)
    spread = jnp.where(kept, loglik, 0.0)
    for k in range(out_ref.shape[1]):
        out_ref[0, k : k + 1, :] = jnp.sum(spread[k * cap_len : (k + 1) * cap_len], 0, keepdims=True)[:, 0:cap_len]


def paired(
    query_rows, proj_weight, proj_bias, candidates, caption_states, caption_ids, caption_lengths, norm_gain, head_weight
):
    shards = lax.axis_size("dp")
    blocks = shards // 2
    _, prefix, width = query_rows.shape
    _, cap_len, model_width = caption_states.shape
    top_count = candidates.shape[1]
    pair_rows = top_count * cap_len
    held = cap_len * -(-model_width // width) + pair_rows
    row_total = blocks * pair_rows
    vocab = head_weight.shape[1]
    position = lax.axis_index("dp").astype(jnp.int32).reshape(1)

    def swap(a, away):
        return lax.ppermute(a, "dp", [(i, i ^ away) for i in range(shards)])

    message = pl.pallas_call(
        pack_kernel,
        out_shape=jax.ShapeDtypeStruct((prefix + held, width), jnp.bfloat16),
        in_specs=[SMEM, SMEM, SMEM, VMEM, VMEM],
        out_specs=VMEM,
        scratch_shapes=[pltpu.VMEM((held, width), jnp.float32)],
        compiler_params=pltpu.CompilerParams(vmem_limit_bytes=2 * MIB),
        name="pack",
    )(candidates, caption_ids, caption_lengths, query_rows, caption_states)

    got = {0: message}
    for away in (12, 8, 4, 2):
        got[away] = swap(message, away)
    for away in (4, 8, 12):
        got[away + 2] = swap(got[away], 2)
    mine = [got[2 * j] for j in range(blocks)]
    other = [swap(a, 1) for a in mine]

    hidden = pl.pallas_call(
        lambda *refs: hidden_kernel(blocks, *refs),
        out_shape=jax.ShapeDtypeStruct((row_total, model_width + LANES), jnp.bfloat16),
        in_specs=[SMEM] + [VMEM] * (2 * blocks + 3),
        out_specs=VMEM,
        scratch_shapes=[
            pltpu.VMEM((blocks * prefix, model_width), jnp.bfloat16),
            pltpu.VMEM((2 * blocks * held, width), jnp.bfloat16),
            pltpu.VMEM((blocks * prefix, width), jnp.bfloat16),
            pltpu.VMEM((row_total, model_width + LANES), jnp.bfloat16),
            pltpu.VMEM((row_total, model_width), jnp.float32),
        ],
        compiler_params=pltpu.CompilerParams(vmem_limit_bytes=20 * MIB),
        name="hidden",
    )(position, *mine, *other, proj_weight, proj_bias.reshape(1, -1), norm_gain.reshape(1, -1))

    stats = pl.pallas_call(
        logits_kernel,
        out_shape=jax.ShapeDtypeStruct((shards, pair_rows, LANES), jnp.float32),
        in_specs=[SMEM, VMEM, VMEM, VMEM],
        out_specs=VMEM,
        scratch_shapes=[
            pltpu.VMEM((2 * row_total, model_width), jnp.bfloat16),
            pltpu.VMEM((2 * row_total, -(-vocab // LANES) * LANES), jnp.float32),
        ],
        compiler_params=pltpu.CompilerParams(vmem_limit_bytes=32 * MIB),
        name="logits",
    )(position, hidden, swap(hidden, 1), head_weight)

    stats = lax.all_to_all(stats, "dp", 0, 0, tiled=True)
    return pl.pallas_call(
        finish_kernel,
        out_shape=jax.ShapeDtypeStruct((1, top_count, cap_len), jnp.float32),
        in_specs=[VMEM, VMEM],
        out_specs=VMEM,
        compiler_params=pltpu.CompilerParams(vmem_limit_bytes=2 * MIB),
        name="finish",
    )(stats, hidden)


def merged(part, axis, combine):
    gathered = jax.tree.map(lambda a: lax.all_gather(a, axis), part)

    def take(source):
        return jax.tree.map(lambda a: lax.dynamic_index_in_dim(a, source, 0, False), gathered)

    return lax.fori_loop(
        1, lax.axis_size(axis), lambda source, state: combine(state, take(source)), take(0)
    )


def project(rows, proj_weight, proj_bias):
    row_total, prefix_len, query_width = rows.shape
    summed = jnp.dot(
        rows.reshape(row_total * prefix_len, query_width),
        proj_weight,
        preferred_element_type=jnp.float32,
    )
    projected = (summed + proj_bias.astype(jnp.float32)).astype(jnp.bfloat16)
    return projected.reshape(row_total, prefix_len, proj_weight.shape[1])


def attend(projected, states, norm_gain):
    prefix_len = projected.shape[0]
    cap_len, model_width = states.shape
    heads = model_width // HEAD_DIM
    keys = jnp.concatenate([projected, states], 0)
    query = states.reshape(cap_len, heads, HEAD_DIM)
    keyed = keys.reshape(prefix_len + cap_len, heads, HEAD_DIM)
    scores = (
        jnp.einsum("thd,jhd->htj", query, keyed, preferred_element_type=jnp.float32) * score_scale
    )
    key_pos = jnp.arange(prefix_len + cap_len)[None, :]
    tok_pos = jnp.arange(cap_len)[:, None]
    allowed = (key_pos < prefix_len) | (key_pos - prefix_len <= tok_pos)
    scores = jnp.where(allowed[None], scores, -jnp.inf)
    row_max = jnp.max(scores, -1, keepdims=True)
    expo = jnp.exp(scores - row_max)
    weights = (expo / jnp.sum(expo, -1, keepdims=True)).astype(jnp.bfloat16)
    mixed_out = jnp.einsum(
        "htj,jhd->thd", weights, keyed, preferred_element_type=jnp.float32
    ).reshape(cap_len, model_width)
    mixed = states.astype(jnp.float32) + mixed_out
    normed = mixed * lax.rsqrt(jnp.mean(mixed * mixed, -1, keepdims=True) + eps) * norm_gain
    return normed.astype(jnp.bfloat16)


def merge_totals(first, second):
    larger = jnp.maximum(first[0], second[0])
    summed = first[1] * jnp.exp(first[0] - larger) + second[1] * jnp.exp(second[0] - larger)
    return (larger, summed, first[2] + second[2])


def spread(
    query_rows,
    proj_weight,
    proj_bias,
    candidates,
    caption_states,
    caption_ids,
    caption_lengths,
    norm_gain,
    head_weight,
):
    position = lax.axis_index("dp")
    img_local, top_count = candidates.shape
    pair_count = img_local * top_count
    cap_local, cap_len, model_width = caption_states.shape
    own_cand = candidates.reshape(pair_count)
    all_cand, all_len = (
        lax.all_gather(candidates, "dp", axis=0, tiled=True),
        lax.all_gather(caption_lengths, "dp", axis=0, tiled=True),
    )
    caption_total = all_len.shape[0]
    length_match = own_cand[:, None] == jnp.arange(caption_total)[None, :]
    pair_len = jnp.sum(jnp.where(length_match, all_len[None, :], 0), 1)
    piece_states = lax.all_gather(caption_states, "dp", axis=0, tiled=True)
    piece_ids = lax.all_gather(caption_ids, "dp", axis=0, tiled=True)
    piece_rows = piece_states.shape[0]
    matches = own_cand[:, None] == jnp.arange(piece_rows)[None, :]
    picked = jnp.dot(
        matches.astype(jnp.bfloat16),
        piece_states.reshape(piece_rows, cap_len * model_width),
        preferred_element_type=jnp.float32,
    )
    fetched_ids = jnp.sum(jnp.where(matches[:, :, None], piece_ids[None, :, :], 0), 1).astype(
        jnp.int32
    )
    pair_states = picked.astype(jnp.bfloat16).reshape(pair_count, cap_len, model_width)
    image_proj = project(query_rows, proj_weight, proj_bias)
    pair_proj = jnp.repeat(image_proj, top_count, axis=0)
    work_hidden = jax.vmap(lambda one, two: attend(one, two, norm_gain))(pair_proj, pair_states)
    row_base = (position * pair_count + jnp.arange(pair_count)) * cap_len
    row_count = work_hidden.shape[0] * cap_len
    hidden_rows = work_hidden.reshape(row_count, model_width)
    id_rows = fetched_ids.reshape(row_count)
    vocab_dev = head_weight.shape[1]
    vocab_start = position * vocab_dev
    every_state, every_id = (
        lax.all_gather(hidden_rows, "dp", axis=0, tiled=True),
        lax.all_gather(id_rows, "dp", axis=0, tiled=True),
    )
    logits = jnp.dot(every_state, head_weight, preferred_element_type=jnp.float32)
    local_max = jnp.max(logits, 1)
    local_sum = jnp.sum(jnp.exp(logits - local_max[:, None]), 1)
    target_hit = jnp.arange(vocab_dev)[None, :] == (every_id - vocab_start)[:, None]
    local_pick = jnp.sum(jnp.where(target_hit, logits, 0.0), 1)
    top_all, sum_all, picked_all = merged((local_max, local_sum, local_pick), "dp", merge_totals)
    row_index = row_base[:, None] + jnp.arange(cap_len)[None, :]
    own_top = jnp.take(top_all, row_index)
    own_sum = jnp.take(sum_all, row_index)
    own_picked = jnp.take(picked_all, row_index)
    loglik = own_picked - (own_top + jnp.log(own_sum))
    inside = jnp.arange(cap_len)[None, :] < pair_len[:, None]
    result = jnp.where(inside, loglik, jnp.float32(0.0))
    return result.reshape(img_local, top_count, cap_len)


def local(query_rows, proj_weight, proj_bias, candidates, caption_states, *rest):
    one_each = candidates.shape[0] == 1 and caption_states.shape[0] == 1
    fits = candidates.shape[1] == 2 and caption_states.shape[1] == 4 and query_rows.shape[1] == 32
    plan = paired if lax.axis_size("dp") == 16 and one_each and fits else spread
    return plan(query_rows, proj_weight, proj_bias, candidates, caption_states, *rest)


def solution(mesh):
    in_specs = (
        P(("groups", "dp"), None, None),
        P(),
        P(),
        P(("groups", "dp"), None),
        P(("groups", "dp"), None, None),
        P(("groups", "dp"), None),
        P(("groups", "dp")),
        P(),
        P(None, "dp"),
    )
    out_specs = P(("groups", "dp"), None, None)
    return jax.shard_map(local, mesh=mesh, in_specs=in_specs, out_specs=out_specs, check_vma=False)
```

```python
import jax
import jax.numpy as jnp
from jax import lax
from jax.experimental import pallas as pl
from jax.experimental.pallas import tpu as pltpu
from jax.sharding import PartitionSpec as P

HEAD_DIM = 64
LANES = 128
TILE = 256
DIGIT = 256
MIB = 1 << 20


score_scale = 0.015625
eps = 1e-06

VMEM = pl.BlockSpec(memory_space=pltpu.VMEM)
SMEM = pl.BlockSpec(memory_space=pltpu.SMEM)
HBM = pl.BlockSpec(memory_space=pltpu.HBM)
ROWS_BY_ROWS = (((1,), (1,)), ((), ()))


def iota(shape, dim):
    return lax.broadcasted_iota(jnp.int32, shape, dim)


def in_hbm(a):
    return pltpu.with_memory_space_constraint(a, pltpu.HBM)


def dot(a, b):
    return jnp.dot(a, b, preferred_element_type=jnp.float32)


def dot_rows(a, b):
    return lax.dot_general(a, b, ROWS_BY_ROWS, preferred_element_type=jnp.float32)


def pack_kernel(length, cand_hbm, ids_hbm, rows_hbm, states_hbm, out_ref, cand, ids, rows, states, stage, sem):
    copies = [
        pltpu.make_async_copy(src, dst, sem.at[i])
        for i, (src, dst) in enumerate(
            ((cand_hbm, cand), (ids_hbm, ids), (rows_hbm, rows), (states_hbm, states))
        )
    ]
    for copy in copies:
        copy.start()
    for copy in copies:
        copy.wait()
    width = rows.shape[2]
    cap_len, model_width = states.shape[1:]
    pieces = -(-model_width // width)
    held = pieces * cap_len
    values = states[0].astype(jnp.float32)
    for c in range(pieces - 1):
        stage[c * cap_len : (c + 1) * cap_len, :] = values[:, c * width : (c + 1) * width]
    rest = model_width - (pieces - 1) * width
    last = held - cap_len
    stage[last:held, 0:rest] = values[:, model_width - rest :]
    token, lane = iota((cap_len, width - rest), 0), iota((cap_len, width - rest), 1)
    digits = jnp.zeros_like(token)
    for t in range(cap_len):
        digits = jnp.where(token == t, jnp.where(lane == 0, ids[0, t] // DIGIT, ids[0, t] % DIGIT), digits)
    digits = jnp.where(lane < 2, digits, 0)
    digits = jnp.where(lane == 2, length[0], digits)
    for k in range(cand.shape[1]):
        digits = jnp.where(lane == 3 + 2 * k, cand[0, k] // DIGIT, digits)
        digits = jnp.where(lane == 4 + 2 * k, cand[0, k] % DIGIT, digits)
    stage[last:held, rest:] = digits.astype(jnp.float32)
    out_ref[0:held, :] = stage[...].astype(jnp.bfloat16)
    out_ref[held:, :] = rows[0]


def hidden_kernel(blocks, parts, head_parts, *refs):
    pos_ref, *msgs = refs[: 2 * blocks + 1]
    (weight_hbm, bias_ref, gain_ref, head_hbm, out_ref, head_ref) = refs[2 * blocks + 1 : 2 * blocks + 7]
    (weight, keys, caps, rows, query, mixed, sem, head_sem) = refs[2 * blocks + 7 :]
    width = rows.shape[1]
    model_width = mixed.shape[1]
    row_total = query.shape[0]
    prefix, held, pair_rows = rows.shape[0] // blocks, caps.shape[0] // (2 * blocks), row_total // blocks
    cap_len = 4
    pieces = -(-model_width // width)
    span = model_width // parts
    copies = [
        pltpu.make_async_copy(
            weight_hbm.at[:, i * span : (i + 1) * span], weight.at[:, i * span : (i + 1) * span], sem.at[i]
        )
        for i in range(parts)
    ]
    for copy in copies:
        copy.start()
    vocab = head_ref.shape[0]
    piece = -(-vocab // head_parts // 16) * 16
    head_copies = [
        pltpu.make_async_copy(
            head_hbm.at[i : min(vocab, i + piece)], head_ref.at[i : min(vocab, i + piece)], head_sem.at[i // piece]
        )
        for i in range(0, vocab, piece)
    ]

    for j in range(blocks):
        rows[j * prefix : (j + 1) * prefix, :] = msgs[j][pieces * cap_len :, :]
    for j in range(2 * blocks):
        caps[j * held : (j + 1) * held, :] = msgs[j][0:held, :]
    rest = model_width - (pieces - 1) * width
    last = (pieces - 2) * cap_len
    row, lane = iota((pair_rows, LANES), 0), iota((pair_rows, LANES), 1)
    place = 3 + 2 * (row // cap_len)
    factor = jnp.where(lane == place, float(DIGIT), jnp.where(lane == place + 1, 1.0, 0.0))
    found = []
    for j in range(blocks):
        digits = msgs[j][last : last + pair_rows, rest : rest + LANES].astype(jnp.float32)
        digits = jnp.where(row < cap_len, pltpu.roll(digits, cap_len, 0), digits)
        found.append(jnp.sum(digits * factor, 1, keepdims=True))
    away = jnp.concatenate(found, 0).astype(jnp.int32) ^ pos_ref[0]
    first = ((away & 1) * blocks + (away >> 1)) * held + iota((row_total, 1), 0) % cap_len
    column = iota((row_total, 2 * blocks * held), 1)
    pick = jnp.concatenate(
        [jnp.where(column == first + c * cap_len, 1.0, 0.0).astype(jnp.bfloat16) for c in range(pieces)], 0
    )
    picked = dot(pick, caps[...]).astype(jnp.bfloat16)
    for c in range(pieces):
        part = min(width, query.shape[1] - c * width)
        query[:, c * width : c * width + part] = picked[c * row_total : (c + 1) * row_total, 0:part]

    for i, copy in enumerate(copies):
        copy.wait()
        if i == parts - 1:
            for head_copy in head_copies:
                head_copy.start()
        cols = slice(i * span, (i + 1) * span)
        summed = dot(rows[...], weight[:, cols])
        keys[:, cols] = (summed + bias_ref[:, cols].astype(jnp.float32)).astype(jnp.bfloat16)

    heads = TILE // HEAD_DIM
    group_keys = LANES
    group_rows = group_keys // prefix * pair_rows
    groups = row_total // group_rows
    lane = iota((group_rows, TILE), 1) // HEAD_DIM
    r, k = iota((heads * group_rows, group_keys), 0) % group_rows, iota((heads * group_rows, group_keys), 1)
    image_ok = (r // pair_rows) == (k // prefix)
    r, k = iota((heads * group_rows, group_rows), 0) % group_rows, iota((heads * group_rows, group_rows), 1)
    own_ok = ((r // cap_len) == (k // cap_len)) & (k <= r)

    def attend_tile(i, square):
        cols = pl.ds(pl.multiple_of(i * TILE, TILE), TILE)
        squares = []
        for g in range(groups):
            q = query[g * group_rows : (g + 1) * group_rows, cols]
            key = keys[g * group_keys : (g + 1) * group_keys, cols]
            zero = jnp.zeros_like(q)
            every = jnp.concatenate([jnp.where(lane == h, q, zero) for h in range(heads)], 0)
            image = jnp.where(image_ok, dot_rows(every, key) * score_scale, -1e30)
            own = jnp.where(own_ok, dot_rows(every, q) * score_scale, -1e30)
            top = jnp.maximum(jnp.max(image, 1, keepdims=True), jnp.max(own, 1, keepdims=True))
            image, own = jnp.exp(image - top), jnp.exp(own - top)
            scale = 1.0 / (jnp.sum(image, 1, keepdims=True) + jnp.sum(own, 1, keepdims=True))
            out = dot((image * scale).astype(jnp.bfloat16), key) + dot((own * scale).astype(jnp.bfloat16), q)
            value = q.astype(jnp.float32)
            for h in range(heads):
                value += jnp.where(lane == h, out[h * group_rows : (h + 1) * group_rows], 0.0)
            mixed[g * group_rows : (g + 1) * group_rows, cols] = value
            squares.append(value * value)
        return square + jnp.concatenate(squares, 0)

    square = lax.fori_loop(
        0, model_width // TILE, attend_tile, jnp.zeros((row_total, TILE), jnp.float32), unroll=4
    )
    scale = lax.rsqrt(jnp.sum(square, 1, keepdims=True) / model_width + eps)
    out_ref[:, 0:model_width] = (mixed[...] * scale * gain_ref[...]).astype(jnp.bfloat16)
    out_ref[:, model_width:] = query[:, model_width:]
    for head_copy in head_copies:
        head_copy.wait()


def logits_kernel(pos_ref, mine_ref, other_ref, head_ref, out_ref, states, logits):
    half = mine_ref.shape[0]
    vocab, model_width = head_ref.shape
    row_total = 2 * half
    states[0:half, :] = mine_ref[:, 0:model_width]
    states[half:, :] = other_ref[:, 0:model_width]
    for start in range(0, vocab, TILE):
        stop = min(vocab, start + TILE)
        logits[start:stop, :] = dot_rows(head_ref[start:stop, :], states[...])
    digits = jnp.concatenate(
        [ref[:, model_width:].astype(jnp.float32) for ref in (mine_ref, other_ref)], 0
    ).T
    ids = (digits[0:1] * DIGIT + digits[1:2]).astype(jnp.int32)
    values = logits[...]
    top = jnp.max(values, 0, keepdims=True)
    total = jnp.sum(jnp.exp(values - top), 0, keepdims=True)
    hit = iota((vocab, row_total), 0) == ids - pos_ref[0] * vocab
    target = jnp.sum(jnp.where(hit, values, 0.0), 0, keepdims=True)
    packed = jnp.concatenate([top, total, target, jnp.zeros((LANES - 3, row_total), jnp.float32)], 0).T
    shards, rows = out_ref.shape[:2]
    for j in range(shards):
        away = (j % (shards // 2)) * 2 + j // (shards // 2)
        out_ref[pos_ref[0] ^ away] = packed[j * rows : (j + 1) * rows]


def finish_kernel(stats_ref, mine_ref, out_ref):
    stats = stats_ref[...]
    shards, rows, _ = stats.shape
    cap_len = out_ref.shape[2]
    model_width = mine_ref.shape[1] - LANES
    lane = iota((rows, LANES), 1)
    top = jnp.max(stats, 0)[:, 0:1]
    total = jnp.zeros((rows, 1), jnp.float32)
    target = jnp.zeros((rows, 1), jnp.float32)
    for e in range(shards):
        total += stats[e][:, 1:2] * jnp.exp(stats[e][:, 0:1] - top)
        target += stats[e][:, 2:3]
    loglik = target - (top + jnp.log(total))
    lengths = mine_ref[0:16, model_width:].astype(jnp.float32)[0:rows, 2:3]
    token = iota((rows, LANES), 0) % cap_len
    kept = (token == lane) & (token.astype(jnp.float32) < lengths)
    spread = jnp.where(kept, loglik, 0.0)
    for k in range(out_ref.shape[1]):
        out_ref[0, k : k + 1, :] = jnp.sum(spread[k * cap_len : (k + 1) * cap_len], 0, keepdims=True)[:, 0:cap_len]


def paired(
    query_rows, proj_weight, proj_bias, candidates, caption_states, caption_ids, caption_lengths, norm_gain, head_weight
):
    shards = lax.axis_size("dp")
    blocks = shards // 2
    _, prefix, width = query_rows.shape
    _, cap_len, model_width = caption_states.shape
    top_count = candidates.shape[1]
    pair_rows = top_count * cap_len
    piece_rows = cap_len * -(-model_width // width)
    held = -(-piece_rows // 16) * 16
    row_total = blocks * pair_rows
    vocab = head_weight.shape[1]
    position = lax.axis_index("dp").astype(jnp.int32).reshape(1)
    parts, head_parts = 8, 8

    def swap(a, away):
        return lax.ppermute(a, "dp", [(i, i ^ away) for i in range(shards)])

    message = pl.pallas_call(
        pack_kernel,
        out_shape=jax.ShapeDtypeStruct((piece_rows + prefix, width), jnp.bfloat16),
        in_specs=[SMEM] + [HBM] * 4,
        out_specs=VMEM,
        scratch_shapes=[
            pltpu.SMEM(candidates.shape, jnp.int32),
            pltpu.SMEM(caption_ids.shape, jnp.int32),
            pltpu.VMEM(query_rows.shape, jnp.bfloat16),
            pltpu.VMEM(caption_states.shape, jnp.bfloat16),
            pltpu.VMEM((piece_rows, width), jnp.float32),
            pltpu.SemaphoreType.DMA((4,)),
        ],
        compiler_params=pltpu.CompilerParams(vmem_limit_bytes=2 * MIB),
        name="pack",
    )(caption_lengths, *(in_hbm(a) for a in (candidates, caption_ids, query_rows, caption_states)))

    got = {0: message}
    for away in (12, 4, 2):
        got[away] = swap(message, away)
    got[8] = swap(got[12], 4)
    for away in (4, 12, 8):
        got[away + 2] = swap(got[away], 2)
    mine = [got[2 * j] for j in range(blocks)]
    other = [swap(a, 1) for a in mine]

    hidden, head = pl.pallas_call(
        lambda *refs: hidden_kernel(blocks, parts, head_parts, *refs),
        out_shape=(
            jax.ShapeDtypeStruct((row_total, model_width + LANES), jnp.bfloat16),
            pltpu.VMEM((vocab, model_width), jnp.bfloat16),
        ),
        in_specs=[SMEM] + [VMEM] * (2 * blocks) + [HBM, VMEM, VMEM, HBM],
        out_specs=(VMEM, VMEM),
        scratch_shapes=[
            pltpu.VMEM((width, model_width), jnp.bfloat16),
            pltpu.VMEM((blocks * prefix, model_width), jnp.bfloat16),
            pltpu.VMEM((2 * blocks * held, width), jnp.bfloat16),
            pltpu.VMEM((blocks * prefix, width), jnp.bfloat16),
            pltpu.VMEM((row_total, model_width + LANES), jnp.bfloat16),
            pltpu.VMEM((row_total, model_width), jnp.float32),
            pltpu.SemaphoreType.DMA((parts,)),
            pltpu.SemaphoreType.DMA((head_parts,)),
        ],
        compiler_params=pltpu.CompilerParams(vmem_limit_bytes=24 * MIB),
        name="hidden",
    )(
        position,
        *mine,
        *other,
        in_hbm(proj_weight),
        proj_bias.reshape(1, -1),
        norm_gain.reshape(1, -1),
        in_hbm(head_weight.T),
    )

    stats = pl.pallas_call(
        logits_kernel,
        out_shape=jax.ShapeDtypeStruct((shards, pair_rows, LANES), jnp.float32),
        in_specs=[SMEM, VMEM, VMEM, VMEM],
        out_specs=VMEM,
        scratch_shapes=[
            pltpu.VMEM((2 * row_total, model_width), jnp.bfloat16),
            pltpu.VMEM((vocab, 2 * row_total), jnp.float32),
        ],
        compiler_params=pltpu.CompilerParams(vmem_limit_bytes=16 * MIB),
        name="logits",
    )(position, hidden, swap(hidden, 1), head)

    stats = lax.all_to_all(stats, "dp", 0, 0, tiled=True)
    return pl.pallas_call(
        finish_kernel,
        out_shape=jax.ShapeDtypeStruct((1, top_count, cap_len), jnp.float32),
        in_specs=[VMEM, VMEM],
        out_specs=VMEM,
        compiler_params=pltpu.CompilerParams(vmem_limit_bytes=2 * MIB),
        name="finish",
    )(stats, hidden)


def merged(part, axis, combine):
    gathered = jax.tree.map(lambda a: lax.all_gather(a, axis), part)

    def take(source):
        return jax.tree.map(lambda a: lax.dynamic_index_in_dim(a, source, 0, False), gathered)

    return lax.fori_loop(
        1, lax.axis_size(axis), lambda source, state: combine(state, take(source)), take(0)
    )


def project(rows, proj_weight, proj_bias):
    row_total, prefix_len, query_width = rows.shape
    summed = jnp.dot(
        rows.reshape(row_total * prefix_len, query_width),
        proj_weight,
        preferred_element_type=jnp.float32,
    )
    projected = (summed + proj_bias.astype(jnp.float32)).astype(jnp.bfloat16)
    return projected.reshape(row_total, prefix_len, proj_weight.shape[1])


def attend(projected, states, norm_gain):
    prefix_len = projected.shape[0]
    cap_len, model_width = states.shape
    heads = model_width // HEAD_DIM
    keys = jnp.concatenate([projected, states], 0)
    query = states.reshape(cap_len, heads, HEAD_DIM)
    keyed = keys.reshape(prefix_len + cap_len, heads, HEAD_DIM)
    scores = (
        jnp.einsum("thd,jhd->htj", query, keyed, preferred_element_type=jnp.float32) * score_scale
    )
    key_pos = jnp.arange(prefix_len + cap_len)[None, :]
    tok_pos = jnp.arange(cap_len)[:, None]
    allowed = (key_pos < prefix_len) | (key_pos - prefix_len <= tok_pos)
    scores = jnp.where(allowed[None], scores, -jnp.inf)
    row_max = jnp.max(scores, -1, keepdims=True)
    expo = jnp.exp(scores - row_max)
    weights = (expo / jnp.sum(expo, -1, keepdims=True)).astype(jnp.bfloat16)
    mixed_out = jnp.einsum(
        "htj,jhd->thd", weights, keyed, preferred_element_type=jnp.float32
    ).reshape(cap_len, model_width)
    mixed = states.astype(jnp.float32) + mixed_out
    normed = mixed * lax.rsqrt(jnp.mean(mixed * mixed, -1, keepdims=True) + eps) * norm_gain
    return normed.astype(jnp.bfloat16)


def merge_totals(first, second):
    larger = jnp.maximum(first[0], second[0])
    summed = first[1] * jnp.exp(first[0] - larger) + second[1] * jnp.exp(second[0] - larger)
    return (larger, summed, first[2] + second[2])


def spread(
    query_rows,
    proj_weight,
    proj_bias,
    candidates,
    caption_states,
    caption_ids,
    caption_lengths,
    norm_gain,
    head_weight,
):
    position = lax.axis_index("dp")
    img_local, top_count = candidates.shape
    pair_count = img_local * top_count
    cap_local, cap_len, model_width = caption_states.shape
    own_cand = candidates.reshape(pair_count)
    all_cand, all_len = (
        lax.all_gather(candidates, "dp", axis=0, tiled=True),
        lax.all_gather(caption_lengths, "dp", axis=0, tiled=True),
    )
    caption_total = all_len.shape[0]
    length_match = own_cand[:, None] == jnp.arange(caption_total)[None, :]
    pair_len = jnp.sum(jnp.where(length_match, all_len[None, :], 0), 1)
    piece_states = lax.all_gather(caption_states, "dp", axis=0, tiled=True)
    piece_ids = lax.all_gather(caption_ids, "dp", axis=0, tiled=True)
    piece_rows = piece_states.shape[0]
    matches = own_cand[:, None] == jnp.arange(piece_rows)[None, :]
    picked = jnp.dot(
        matches.astype(jnp.bfloat16),
        piece_states.reshape(piece_rows, cap_len * model_width),
        preferred_element_type=jnp.float32,
    )
    fetched_ids = jnp.sum(jnp.where(matches[:, :, None], piece_ids[None, :, :], 0), 1).astype(
        jnp.int32
    )
    pair_states = picked.astype(jnp.bfloat16).reshape(pair_count, cap_len, model_width)
    image_proj = project(query_rows, proj_weight, proj_bias)
    pair_proj = jnp.repeat(image_proj, top_count, axis=0)
    work_hidden = jax.vmap(lambda one, two: attend(one, two, norm_gain))(pair_proj, pair_states)
    row_base = (position * pair_count + jnp.arange(pair_count)) * cap_len
    row_count = work_hidden.shape[0] * cap_len
    hidden_rows = work_hidden.reshape(row_count, model_width)
    id_rows = fetched_ids.reshape(row_count)
    vocab_dev = head_weight.shape[1]
    vocab_start = position * vocab_dev
    every_state, every_id = (
        lax.all_gather(hidden_rows, "dp", axis=0, tiled=True),
        lax.all_gather(id_rows, "dp", axis=0, tiled=True),
    )
    logits = jnp.dot(every_state, head_weight, preferred_element_type=jnp.float32)
    local_max = jnp.max(logits, 1)
    local_sum = jnp.sum(jnp.exp(logits - local_max[:, None]), 1)
    target_hit = jnp.arange(vocab_dev)[None, :] == (every_id - vocab_start)[:, None]
    local_pick = jnp.sum(jnp.where(target_hit, logits, 0.0), 1)
    top_all, sum_all, picked_all = merged((local_max, local_sum, local_pick), "dp", merge_totals)
    row_index = row_base[:, None] + jnp.arange(cap_len)[None, :]
    own_top = jnp.take(top_all, row_index)
    own_sum = jnp.take(sum_all, row_index)
    own_picked = jnp.take(picked_all, row_index)
    loglik = own_picked - (own_top + jnp.log(own_sum))
    inside = jnp.arange(cap_len)[None, :] < pair_len[:, None]
    result = jnp.where(inside, loglik, jnp.float32(0.0))
    return result.reshape(img_local, top_count, cap_len)


def local(query_rows, proj_weight, proj_bias, candidates, caption_states, *rest):
    one_each = candidates.shape[0] == 1 and caption_states.shape[0] == 1
    fits = candidates.shape[1] == 2 and caption_states.shape[1] == 4 and query_rows.shape[1] == 32
    plan = paired if lax.axis_size("dp") == 16 and one_each and fits else spread
    return plan(query_rows, proj_weight, proj_bias, candidates, caption_states, *rest)


def solution(mesh):
    in_specs = (
        P(("groups", "dp"), None, None),
        P(),
        P(),
        P(("groups", "dp"), None),
        P(("groups", "dp"), None, None),
        P(("groups", "dp"), None),
        P(("groups", "dp")),
        P(),
        P(None, "dp"),
    )
    out_specs = P(("groups", "dp"), None, None)
    return jax.shard_map(local, mesh=mesh, in_specs=in_specs, out_specs=out_specs, check_vma=False)
```

```python
import functools

import jax
import jax.numpy as jnp
from jax import lax
from jax.experimental import pallas as pl
from jax.experimental.pallas import tpu as pltpu
from jax.sharding import PartitionSpec as P

HEAD_DIM = 64
LANES = 128
TILE = 256
DIGIT = 256
MIB = 1 << 20


score_scale = 0.015625
eps = 1e-06

VMEM = pl.BlockSpec(memory_space=pltpu.VMEM)
SMEM = pl.BlockSpec(memory_space=pltpu.SMEM)
HBM = pl.BlockSpec(memory_space=pltpu.HBM)
ROWS_BY_ROWS = (((1,), (1,)), ((), ()))


def iota(shape, dim):
    return lax.broadcasted_iota(jnp.int32, shape, dim)


def in_hbm(a):
    return pltpu.with_memory_space_constraint(a, pltpu.HBM)


def dot(a, b):
    return jnp.dot(a, b, preferred_element_type=jnp.float32)


def dot_rows(a, b):
    return lax.dot_general(a, b, ROWS_BY_ROWS, preferred_element_type=jnp.float32)


def pack_kernel(cand_hbm, ids_hbm, rows_hbm, states_hbm, out_ref, cand, ids, rows, states, stage, sem):
    copies = [
        pltpu.make_async_copy(src, dst, sem.at[i])
        for i, (src, dst) in enumerate(
            ((cand_hbm, cand), (ids_hbm, ids), (rows_hbm, rows), (states_hbm, states))
        )
    ]
    for copy in copies:
        copy.start()
    for copy in copies:
        copy.wait()
    width = rows.shape[2]
    cap_len, model_width = states.shape[1:]
    pieces = -(-model_width // width)
    held = pieces * cap_len
    values = states[0].astype(jnp.float32)
    for c in range(pieces - 1):
        stage[c * cap_len : (c + 1) * cap_len, :] = values[:, c * width : (c + 1) * width]
    rest = model_width - (pieces - 1) * width
    last = held - cap_len
    stage[last:held, 0:rest] = values[:, model_width - rest :]
    token, lane = iota((cap_len, width - rest), 0), iota((cap_len, width - rest), 1)
    digits = jnp.zeros_like(token)
    for t in range(cap_len):
        digits = jnp.where(token == t, jnp.where(lane == 0, ids[0, t] // DIGIT, ids[0, t] % DIGIT), digits)
    digits = jnp.where(lane < 2, digits, 0)
    for k in range(cand.shape[1]):
        digits = jnp.where(lane == 2 + 2 * k, cand[0, k] // DIGIT, digits)
        digits = jnp.where(lane == 3 + 2 * k, cand[0, k] % DIGIT, digits)
    stage[last:held, rest:] = digits.astype(jnp.float32)
    out_ref[0:held, :] = stage[...].astype(jnp.bfloat16)
    out_ref[held:, :] = rows[0]


def bring_kernel(pos_ref, len_ref, weight_hbm, bias_hbm, gain_hbm, weight_ref, bias_ref, gain_ref, length_ref, bias, sem):
    pairs = ((bias_hbm, bias), (gain_hbm, gain_ref), (weight_hbm, weight_ref))
    copies = [pltpu.make_async_copy(src, dst, sem.at[i]) for i, (src, dst) in enumerate(pairs)]
    for copy in copies:
        copy.start()
    length_ref[...] = jnp.full(length_ref.shape, len_ref[0].astype(jnp.float32))
    copies[0].wait()
    bias_ref[...] = bias[...].astype(jnp.float32).reshape(bias_ref.shape)
    for copy in copies[1:]:
        copy.wait()


def copies_of(src, dst, sem, parts):
    total = src.shape[0]
    piece = -(-total // parts // 16) * 16
    return [
        pltpu.make_async_copy(src.at[i : min(total, i + piece)], dst.at[i : min(total, i + piece)], sem.at[i // piece])
        for i in range(0, total, piece)
    ]


def collect_kernel(*refs):
    *msgs, out_ref = refs
    held = out_ref.shape[0] // len(msgs)
    for i, msg in enumerate(msgs):
        out_ref[i * held : (i + 1) * held, :] = msg[0:held, :]


def keys_kernel(blocks, *refs):
    msgs, (weight, bias, keys, rows) = refs[:blocks], refs[blocks:]
    prefix = rows.shape[0] // blocks
    for j, msg in enumerate(msgs):
        rows[j * prefix : (j + 1) * prefix, :] = msg[msg.shape[0] - prefix :, :]
    step = 512
    for i in range(0, keys.shape[1], step):
        summed = dot(rows[...], weight[:, i : i + step])
        keys[:, i : i + step] = (summed + bias[:, i : i + step]).astype(jnp.bfloat16)


def hidden_kernel(order, prefix, cap_len, *refs):
    pos_ref, *cap_refs = refs[:5]
    keys, gain_ref, head_hbm, out_ref, head_ref, caps, query, mixed, bias, scores, weights, sem = refs[5:]
    head_copies = copies_of(head_hbm, head_ref, sem, sem.shape[0])
    for copy in head_copies:
        copy.start()
    blocks = len(order)
    width = caps.shape[1]
    model_width = mixed.shape[1]
    row_total = query.shape[0]
    held, pair_rows = caps.shape[0] // (2 * blocks), row_total // blocks
    pieces = -(-model_width // width)

    start = 0
    for ref in cap_refs:
        caps[start : start + ref.shape[0], :] = ref[...]
        start += ref.shape[0]
    rest = model_width - (pieces - 1) * width
    last = (pieces - 2) * cap_len
    row, lane = iota((pair_rows, LANES), 0), iota((pair_rows, LANES), 1)
    place = 2 + 2 * (row // cap_len)
    factor = jnp.where(lane == place, float(DIGIT), jnp.where(lane == place + 1, 1.0, 0.0))
    found = []
    for s in range(blocks):
        digits = caps[s * held + last : s * held + last + pair_rows, rest : rest + LANES].astype(jnp.float32)
        digits = jnp.where(row < cap_len, pltpu.roll(digits, cap_len, 0), digits)
        found.append(jnp.sum(digits * factor, 1, keepdims=True))
    found = jnp.concatenate(found, 0)
    away = found.astype(jnp.int32) ^ pos_ref[0]
    block = (away & 1) * blocks
    for s, distance in enumerate(order):
        block += jnp.where(away - (away & 1) == distance, s, 0)
    first = block * held + iota((row_total, 1), 0) % cap_len
    column = iota((row_total, 2 * blocks * held), 1)
    pick = jnp.concatenate(
        [jnp.where(column == first + c * cap_len, 1.0, 0.0).astype(jnp.bfloat16) for c in range(pieces)], 0
    )
    picked = dot(pick, caps[...]).astype(jnp.bfloat16)
    for c in range(pieces):
        part = min(width, query.shape[1] - c * width)
        query[:, c * width : c * width + part] = picked[c * row_total : (c + 1) * row_total, 0:part]

    heads = TILE // HEAD_DIM
    group_rows = bias.shape[0] // heads
    image_keys = bias.shape[1] - group_rows
    lane = iota((group_rows, TILE), 1) // HEAD_DIM
    r, k = iota(bias.shape, 0) % group_rows, iota(bias.shape, 1)
    own = k - image_keys
    allowed = ((k < image_keys) & (k // prefix == r // pair_rows)) | (
        (own >= 0) & (own <= r) & (own // cap_len == r // cap_len)
    )
    bias[...] = jnp.where(allowed, 0.0, -1e30)
    tiles = [
        (g, slice(i * TILE, (i + 1) * TILE))
        for i in range(model_width // TILE)
        for g in range(row_total // group_rows)
    ]

    def keys_of(g, cols):
        q = query[g * group_rows : (g + 1) * group_rows, cols]
        return q, jnp.concatenate([keys[g * image_keys : (g + 1) * image_keys, cols], q], 0)

    for n, (g, cols) in enumerate(tiles):
        q, key = keys_of(g, cols)
        scaled, zero = q * score_scale, jnp.zeros_like(q)
        every = jnp.concatenate([jnp.where(lane == h, scaled, zero) for h in range(heads)], 0)
        scores[n] = dot_rows(every, key)
    for n in range(len(tiles)):
        score = scores[n] + bias[...]
        expo = jnp.exp(score - jnp.max(score, 1, keepdims=True))
        weights[n] = (expo * (1.0 / jnp.sum(expo, 1, keepdims=True))).astype(jnp.bfloat16)
    squares = [jnp.zeros((group_rows, TILE), jnp.float32) for _ in range(row_total // group_rows)]
    for n, (g, cols) in enumerate(tiles):
        q, key = keys_of(g, cols)
        out = dot(weights[n], key)
        value = q.astype(jnp.float32)
        for h in range(heads):
            value += jnp.where(lane == h, out[h * group_rows : (h + 1) * group_rows], 0.0)
        mixed[g * group_rows : (g + 1) * group_rows, cols] = value
        squares[g] += value * value
    square = jnp.concatenate(squares, 0)
    scale = lax.rsqrt(jnp.sum(square, 1, keepdims=True) / model_width + eps)
    out_ref[:, 0:model_width] = (mixed[...] * scale * gain_ref[...]).astype(jnp.bfloat16)
    marks = query[:, model_width:]
    out_ref[:, model_width:] = jnp.where(iota(marks.shape, 1) == 2, found.astype(jnp.bfloat16), marks)
    for copy in head_copies:
        copy.wait()


def logits_kernel(order, pos_ref, mine_ref, other_ref, head_ref, length_ref, out_ref, states, logits):
    half = mine_ref.shape[0]
    vocab, model_width = head_ref.shape
    row_total = 2 * half
    states[0:half, :] = mine_ref[:, 0:model_width]
    states[half:, :] = other_ref[:, 0:model_width]
    for start in range(0, vocab, TILE):
        stop = min(vocab, start + TILE)
        logits[start:stop, :] = dot_rows(head_ref[start:stop, :], states[...])
    digits = jnp.concatenate(
        [ref[:, model_width:].astype(jnp.float32) for ref in (mine_ref, other_ref)], 0
    ).T
    ids = (digits[0:1] * DIGIT + digits[1:2]).astype(jnp.int32)
    values = logits[...]
    top = jnp.max(values, 0, keepdims=True)
    total = jnp.sum(jnp.exp(values - top), 0, keepdims=True)
    hit = iota((vocab, row_total), 0) == ids - pos_ref[0] * vocab
    target = jnp.sum(jnp.where(hit, values, 0.0), 0, keepdims=True)
    packed = jnp.concatenate(
        [top, total, target, length_ref[...], jnp.zeros((LANES - 4, row_total), jnp.float32)], 0
    ).T
    shards, rows = out_ref.shape[:2]
    for j in range(shards):
        away = order[j % len(order)] + j // len(order)
        out_ref[pos_ref[0] ^ away] = packed[j * rows : (j + 1) * rows]


def finish_kernel(stats_ref, mine_ref, out_ref):
    stats = stats_ref[...]
    shards, rows, _ = stats.shape
    cap_len = out_ref.shape[2]
    model_width = mine_ref.shape[1] - LANES
    lane = iota((rows, LANES), 1)
    top = jnp.max(stats, 0)[:, 0:1]
    total = jnp.zeros((rows, 1), jnp.float32)
    target = jnp.zeros((rows, 1), jnp.float32)
    length = jnp.zeros((rows, 1), jnp.float32)
    cand = mine_ref[0:16, model_width:].astype(jnp.float32)[0:rows, 2:3]
    for e in range(shards):
        total += stats[e][:, 1:2] * jnp.exp(stats[e][:, 0:1] - top)
        target += stats[e][:, 2:3]
        length += jnp.where(cand == e, stats[e][:, 3:4], 0.0)
    loglik = target - (top + jnp.log(total))
    token = iota((rows, LANES), 0) % cap_len
    kept = (token == lane) & (token.astype(jnp.float32) < length)
    spread = jnp.where(kept, loglik, 0.0)
    for k in range(out_ref.shape[1]):
        out_ref[0, k : k + 1, :] = jnp.sum(spread[k * cap_len : (k + 1) * cap_len], 0, keepdims=True)[:, 0:cap_len]


def paired(
    query_rows, proj_weight, proj_bias, candidates, caption_states, caption_ids, caption_lengths, norm_gain, head_weight
):
    shards = lax.axis_size("dp")
    blocks = shards // 2
    _, prefix, width = query_rows.shape
    _, cap_len, model_width = caption_states.shape
    top_count = candidates.shape[1]
    pair_rows = top_count * cap_len
    piece_rows = cap_len * -(-model_width // width)
    held = -(-piece_rows // 16) * 16
    row_total = blocks * pair_rows
    vocab = head_weight.shape[1]
    position = lax.axis_index("dp").astype(jnp.int32).reshape(1)
    head_parts = 8
    heads, group = TILE // HEAD_DIM, LANES // prefix
    score_tiles = model_width // TILE * blocks // group

    def swap(a, away):
        return lax.ppermute(a, "dp", [(i, i ^ away) for i in range(shards)])

    message = pl.pallas_call(
        pack_kernel,
        out_shape=jax.ShapeDtypeStruct((piece_rows + prefix, width), jnp.bfloat16),
        in_specs=[HBM] * 4,
        out_specs=VMEM,
        scratch_shapes=[
            pltpu.SMEM(candidates.shape, jnp.int32),
            pltpu.SMEM(caption_ids.shape, jnp.int32),
            pltpu.VMEM(query_rows.shape, jnp.bfloat16),
            pltpu.VMEM(caption_states.shape, jnp.bfloat16),
            pltpu.VMEM((piece_rows, width), jnp.float32),
            pltpu.SemaphoreType.DMA((4,)),
        ],
        compiler_params=pltpu.CompilerParams(vmem_limit_bytes=2 * MIB),
        name="pack",
    )(*(in_hbm(a) for a in (candidates, caption_ids, query_rows, caption_states)))

    got = {0: message}
    for away in (12, 4, 2):
        got[away] = swap(message, away)
    weight, bias, gain, length = pl.pallas_call(
        bring_kernel,
        out_shape=(
            pltpu.VMEM((width, model_width), jnp.bfloat16),
            pltpu.VMEM((1, model_width), jnp.float32),
            pltpu.VMEM((1, model_width), jnp.float32),
            pltpu.VMEM((1, LANES), jnp.float32),
        ),
        in_specs=[SMEM] * 2 + [HBM] * 3,
        out_specs=(VMEM,) * 4,
        scratch_shapes=[pltpu.VMEM((model_width,), jnp.bfloat16), pltpu.SemaphoreType.DMA((3,))],
        compiler_params=pltpu.CompilerParams(vmem_limit_bytes=2 * MIB),
        cost_estimate=pl.CostEstimate(flops=0, bytes_accessed=4 * width * model_width, transcendentals=0),
        name="bring",
    )(position, caption_lengths, *(in_hbm(a) for a in (proj_weight, proj_bias, norm_gain.reshape(1, -1))))
    got[12], got[4], got[2], length = lax.optimization_barrier((got[12], got[4], got[2], length))
    got[8] = swap(got[12], 4)
    for away in (12, 4, 8):
        got[away + 2] = swap(got[away], 2)
    order = (0, 12, 4, 2, 8, 14, 6, 10)
    mine = [got[away] for away in order]

    def collect(msgs):
        return pl.pallas_call(
            collect_kernel,
            out_shape=jax.ShapeDtypeStruct((len(msgs) * held, width), jnp.bfloat16),
            in_specs=[VMEM] * len(msgs),
            out_specs=VMEM,
            compiler_params=pltpu.CompilerParams(vmem_limit_bytes=2 * MIB),
            name="collect",
        )(*msgs)

    near, far = collect(mine[: blocks // 2]), collect(mine[blocks // 2 :])
    other_near, other_far = swap(near, 1), swap(far, 1)

    keys = pl.pallas_call(
        functools.partial(keys_kernel, blocks),
        out_shape=pltpu.VMEM((blocks * prefix, model_width), jnp.bfloat16),
        in_specs=[VMEM] * (blocks + 2),
        out_specs=VMEM,
        scratch_shapes=[pltpu.VMEM((blocks * prefix, width), jnp.bfloat16)],
        compiler_params=pltpu.CompilerParams(vmem_limit_bytes=8 * MIB),
        cost_estimate=pl.CostEstimate(
            flops=2 * blocks * prefix * width * model_width, bytes_accessed=4 * width * model_width, transcendentals=0
        ),
        name="keys",
    )(*mine, weight, bias)

    hidden, head = pl.pallas_call(
        functools.partial(hidden_kernel, order, prefix, cap_len),
        out_shape=(
            jax.ShapeDtypeStruct((row_total, model_width + LANES), jnp.bfloat16),
            pltpu.VMEM((vocab, model_width), jnp.bfloat16),
        ),
        in_specs=[SMEM] + [VMEM] * 6 + [HBM],
        out_specs=(VMEM, VMEM),
        scratch_shapes=[
            pltpu.VMEM((2 * blocks * held, width), jnp.bfloat16),
            pltpu.VMEM((row_total, model_width + LANES), jnp.bfloat16),
            pltpu.VMEM((row_total, model_width), jnp.float32),
            pltpu.VMEM((heads * group * pair_rows, group * (prefix + pair_rows)), jnp.float32),
            pltpu.VMEM((score_tiles, heads * group * pair_rows, group * (prefix + pair_rows)), jnp.float32),
            pltpu.VMEM((score_tiles, heads * group * pair_rows, group * (prefix + pair_rows)), jnp.bfloat16),
            pltpu.SemaphoreType.DMA((head_parts,)),
        ],
        compiler_params=pltpu.CompilerParams(vmem_limit_bytes=24 * MIB),
        name="hidden",
    )(position, near, far, other_near, other_far, keys, gain, in_hbm(head_weight.T))

    stats = pl.pallas_call(
        functools.partial(logits_kernel, order),
        out_shape=jax.ShapeDtypeStruct((shards, pair_rows, LANES), jnp.float32),
        in_specs=[SMEM, VMEM, VMEM, VMEM, VMEM],
        out_specs=VMEM,
        scratch_shapes=[
            pltpu.VMEM((2 * row_total, model_width), jnp.bfloat16),
            pltpu.VMEM((vocab, 2 * row_total), jnp.float32),
        ],
        compiler_params=pltpu.CompilerParams(vmem_limit_bytes=16 * MIB),
        name="logits",
    )(position, hidden, swap(hidden, 1), head, length)

    stats = lax.all_to_all(stats, "dp", 0, 0, tiled=True)
    return pl.pallas_call(
        finish_kernel,
        out_shape=jax.ShapeDtypeStruct((1, top_count, cap_len), jnp.float32),
        in_specs=[VMEM, VMEM],
        out_specs=VMEM,
        compiler_params=pltpu.CompilerParams(vmem_limit_bytes=2 * MIB),
        name="finish",
    )(stats, hidden)


def merged(part, axis, combine):
    gathered = jax.tree.map(lambda a: lax.all_gather(a, axis), part)

    def take(source):
        return jax.tree.map(lambda a: lax.dynamic_index_in_dim(a, source, 0, False), gathered)

    return lax.fori_loop(
        1, lax.axis_size(axis), lambda source, state: combine(state, take(source)), take(0)
    )


def project(rows, proj_weight, proj_bias):
    row_total, prefix_len, query_width = rows.shape
    summed = jnp.dot(
        rows.reshape(row_total * prefix_len, query_width),
        proj_weight,
        preferred_element_type=jnp.float32,
    )
    projected = (summed + proj_bias.astype(jnp.float32)).astype(jnp.bfloat16)
    return projected.reshape(row_total, prefix_len, proj_weight.shape[1])


def attend(projected, states, norm_gain):
    prefix_len = projected.shape[0]
    cap_len, model_width = states.shape
    heads = model_width // HEAD_DIM
    keys = jnp.concatenate([projected, states], 0)
    query = states.reshape(cap_len, heads, HEAD_DIM)
    keyed = keys.reshape(prefix_len + cap_len, heads, HEAD_DIM)
    scores = (
        jnp.einsum("thd,jhd->htj", query, keyed, preferred_element_type=jnp.float32) * score_scale
    )
    key_pos = jnp.arange(prefix_len + cap_len)[None, :]
    tok_pos = jnp.arange(cap_len)[:, None]
    allowed = (key_pos < prefix_len) | (key_pos - prefix_len <= tok_pos)
    scores = jnp.where(allowed[None], scores, -jnp.inf)
    row_max = jnp.max(scores, -1, keepdims=True)
    expo = jnp.exp(scores - row_max)
    weights = (expo / jnp.sum(expo, -1, keepdims=True)).astype(jnp.bfloat16)
    mixed_out = jnp.einsum(
        "htj,jhd->thd", weights, keyed, preferred_element_type=jnp.float32
    ).reshape(cap_len, model_width)
    mixed = states.astype(jnp.float32) + mixed_out
    normed = mixed * lax.rsqrt(jnp.mean(mixed * mixed, -1, keepdims=True) + eps) * norm_gain
    return normed.astype(jnp.bfloat16)


def merge_totals(first, second):
    larger = jnp.maximum(first[0], second[0])
    summed = first[1] * jnp.exp(first[0] - larger) + second[1] * jnp.exp(second[0] - larger)
    return (larger, summed, first[2] + second[2])


def spread(
    query_rows,
    proj_weight,
    proj_bias,
    candidates,
    caption_states,
    caption_ids,
    caption_lengths,
    norm_gain,
    head_weight,
):
    position = lax.axis_index("dp")
    img_local, top_count = candidates.shape
    pair_count = img_local * top_count
    cap_local, cap_len, model_width = caption_states.shape
    own_cand = candidates.reshape(pair_count)
    all_cand, all_len = (
        lax.all_gather(candidates, "dp", axis=0, tiled=True),
        lax.all_gather(caption_lengths, "dp", axis=0, tiled=True),
    )
    caption_total = all_len.shape[0]
    length_match = own_cand[:, None] == jnp.arange(caption_total)[None, :]
    pair_len = jnp.sum(jnp.where(length_match, all_len[None, :], 0), 1)
    piece_states = lax.all_gather(caption_states, "dp", axis=0, tiled=True)
    piece_ids = lax.all_gather(caption_ids, "dp", axis=0, tiled=True)
    piece_rows = piece_states.shape[0]
    matches = own_cand[:, None] == jnp.arange(piece_rows)[None, :]
    picked = jnp.dot(
        matches.astype(jnp.bfloat16),
        piece_states.reshape(piece_rows, cap_len * model_width),
        preferred_element_type=jnp.float32,
    )
    fetched_ids = jnp.sum(jnp.where(matches[:, :, None], piece_ids[None, :, :], 0), 1).astype(
        jnp.int32
    )
    pair_states = picked.astype(jnp.bfloat16).reshape(pair_count, cap_len, model_width)
    image_proj = project(query_rows, proj_weight, proj_bias)
    pair_proj = jnp.repeat(image_proj, top_count, axis=0)
    work_hidden = jax.vmap(lambda one, two: attend(one, two, norm_gain))(pair_proj, pair_states)
    row_base = (position * pair_count + jnp.arange(pair_count)) * cap_len
    row_count = work_hidden.shape[0] * cap_len
    hidden_rows = work_hidden.reshape(row_count, model_width)
    id_rows = fetched_ids.reshape(row_count)
    vocab_dev = head_weight.shape[1]
    vocab_start = position * vocab_dev
    every_state, every_id = (
        lax.all_gather(hidden_rows, "dp", axis=0, tiled=True),
        lax.all_gather(id_rows, "dp", axis=0, tiled=True),
    )
    logits = jnp.dot(every_state, head_weight, preferred_element_type=jnp.float32)
    local_max = jnp.max(logits, 1)
    local_sum = jnp.sum(jnp.exp(logits - local_max[:, None]), 1)
    target_hit = jnp.arange(vocab_dev)[None, :] == (every_id - vocab_start)[:, None]
    local_pick = jnp.sum(jnp.where(target_hit, logits, 0.0), 1)
    top_all, sum_all, picked_all = merged((local_max, local_sum, local_pick), "dp", merge_totals)
    row_index = row_base[:, None] + jnp.arange(cap_len)[None, :]
    own_top = jnp.take(top_all, row_index)
    own_sum = jnp.take(sum_all, row_index)
    own_picked = jnp.take(picked_all, row_index)
    loglik = own_picked - (own_top + jnp.log(own_sum))
    inside = jnp.arange(cap_len)[None, :] < pair_len[:, None]
    result = jnp.where(inside, loglik, jnp.float32(0.0))
    return result.reshape(img_local, top_count, cap_len)


def local(query_rows, proj_weight, proj_bias, candidates, caption_states, *rest):
    one_each = candidates.shape[0] == 1 and caption_states.shape[0] == 1
    fits = candidates.shape[1] == 2 and caption_states.shape[1] == 4 and query_rows.shape[1] == 32
    plan = paired if lax.axis_size("dp") == 16 and one_each and fits else spread
    return plan(query_rows, proj_weight, proj_bias, candidates, caption_states, *rest)


def solution(mesh):
    in_specs = (
        P(("groups", "dp"), None, None),
        P(),
        P(),
        P(("groups", "dp"), None),
        P(("groups", "dp"), None, None),
        P(("groups", "dp"), None),
        P(("groups", "dp")),
        P(),
        P(None, "dp"),
    )
    out_specs = P(("groups", "dp"), None, None)
    return jax.shard_map(local, mesh=mesh, in_specs=in_specs, out_specs=out_specs, check_vma=False)
```

```python
import functools

import jax
import jax.numpy as jnp
from jax import lax
from jax.experimental import pallas as pl
from jax.experimental.pallas import tpu as pltpu
from jax.sharding import PartitionSpec as P

HEAD_DIM = 64
LANES = 128
TILE = 256
DIGIT = 256
MIB = 1 << 20


score_scale = 0.015625
eps = 1e-06

VMEM = pl.BlockSpec(memory_space=pltpu.VMEM)
SMEM = pl.BlockSpec(memory_space=pltpu.SMEM)
HBM = pl.BlockSpec(memory_space=pltpu.HBM)
ANY = pl.BlockSpec(memory_space=pl.ANY)
ROWS_BY_ROWS = (((1,), (1,)), ((), ()))


def iota(shape, dim):
    return lax.broadcasted_iota(jnp.int32, shape, dim)


def in_hbm(a):
    return pltpu.with_memory_space_constraint(a, pltpu.HBM)


def dot(a, b):
    return jnp.dot(a, b, preferred_element_type=jnp.float32)


def dot_rows(a, b):
    return lax.dot_general(a, b, ROWS_BY_ROWS, preferred_element_type=jnp.float32)


def pack_kernel(cand_hbm, ids_hbm, rows_hbm, states_hbm, out_ref, cand, ids, rows, states, stage, sem):
    copies = [
        pltpu.make_async_copy(src, dst, sem.at[i])
        for i, (src, dst) in enumerate(
            ((cand_hbm, cand), (ids_hbm, ids), (rows_hbm, rows), (states_hbm, states))
        )
    ]
    for copy in copies:
        copy.start()
    for copy in copies:
        copy.wait()
    width = rows.shape[2]
    cap_len, model_width = states.shape[1:]
    pieces = -(-model_width // width)
    held = pieces * cap_len
    values = states[0].astype(jnp.float32)
    for c in range(pieces - 1):
        stage[c * cap_len : (c + 1) * cap_len, :] = values[:, c * width : (c + 1) * width]
    rest = model_width - (pieces - 1) * width
    last = held - cap_len
    stage[last:held, 0:rest] = values[:, model_width - rest :]
    token, lane = iota((cap_len, width - rest), 0), iota((cap_len, width - rest), 1)
    digits = jnp.zeros_like(token)
    for t in range(cap_len):
        digits = jnp.where(token == t, jnp.where(lane == 0, ids[0, t] // DIGIT, ids[0, t] % DIGIT), digits)
    digits = jnp.where(lane < 2, digits, 0)
    for k in range(cand.shape[1]):
        digits = jnp.where(lane == 2 + 2 * k, cand[0, k] // DIGIT, digits)
        digits = jnp.where(lane == 3 + 2 * k, cand[0, k] % DIGIT, digits)
    stage[last:held, rest:] = digits.astype(jnp.float32)
    out_ref[0:held, :] = stage[...].astype(jnp.bfloat16)
    out_ref[held:, :] = rows[0]


def bring_kernel(pos_ref, len_ref, weight_hbm, bias_hbm, gain_hbm, weight_ref, bias_ref, gain_ref, length_ref, bias, sem):
    pairs = ((bias_hbm, bias), (gain_hbm, gain_ref), (weight_hbm, weight_ref))
    copies = [pltpu.make_async_copy(src, dst, sem.at[i]) for i, (src, dst) in enumerate(pairs)]
    for copy in copies:
        copy.start()
    length_ref[...] = jnp.full(length_ref.shape, len_ref[0].astype(jnp.float32))
    copies[0].wait()
    bias_ref[...] = bias[...].astype(jnp.float32).reshape(bias_ref.shape)
    for copy in copies[1:]:
        copy.wait()


def cuts(total, parts):
    piece = -(-total // parts // 16) * 16
    return [(i, min(total, i + piece)) for i in range(0, total, piece)]


def copies_of(src, first, dst, sem):
    return [
        pltpu.make_async_copy(src.at[first + i : first + j], dst.at[i:j], sem.at[n])
        for n, (i, j) in enumerate(cuts(dst.shape[0], sem.shape[0]))
    ]


def bring_head_kernel(after_ref, head_hbm, head_ref, done_ref, sem):
    copies = copies_of(head_hbm, 0, head_ref, sem)
    for copy in copies:
        copy.start()
    done_ref[...] = jnp.zeros_like(done_ref)
    for copy in copies:
        copy.wait()


def collect_kernel(count, *refs):
    msgs, out_ref = refs[:count], refs[-1]
    held = out_ref.shape[0] // count
    for i, msg in enumerate(msgs):
        out_ref[i * held : (i + 1) * held, :] = msg[0:held, :]


def keys_kernel(blocks, *refs):
    msgs, (weight, bias, keys, rows) = refs[:blocks], refs[blocks:]
    prefix = rows.shape[0] // blocks
    for j, msg in enumerate(msgs):
        rows[j * prefix : (j + 1) * prefix, :] = msg[msg.shape[0] - prefix :, :]
    step = 512
    for i in range(0, keys.shape[1], step):
        summed = dot(rows[...], weight[:, i : i + step])
        keys[:, i : i + step] = (summed + bias[:, i : i + step]).astype(jnp.bfloat16)


def hidden_kernel(order, prefix, cap_len, *refs):
    pos_ref, *cap_refs = refs[:5]
    keys, gain_ref, head_hbm, out_ref, head_ref, caps, query, mixed, bias, scores, weights, sem = refs[5:]
    head_copies = copies_of(head_hbm, head_hbm.shape[0] - head_ref.shape[0], head_ref, sem)
    for copy in head_copies:
        copy.start()
    blocks = len(order)
    width = caps.shape[1]
    model_width = mixed.shape[1]
    row_total = query.shape[0]
    held, pair_rows = caps.shape[0] // (2 * blocks), row_total // blocks
    pieces = -(-model_width // width)

    start = 0
    for ref in cap_refs:
        caps[start : start + ref.shape[0], :] = ref[...]
        start += ref.shape[0]
    rest = model_width - (pieces - 1) * width
    last = (pieces - 2) * cap_len
    row, lane = iota((pair_rows, LANES), 0), iota((pair_rows, LANES), 1)
    place = 2 + 2 * (row // cap_len)
    factor = jnp.where(lane == place, float(DIGIT), jnp.where(lane == place + 1, 1.0, 0.0))
    found = []
    for s in range(blocks):
        digits = caps[s * held + last : s * held + last + pair_rows, rest : rest + LANES].astype(jnp.float32)
        digits = jnp.where(row < cap_len, pltpu.roll(digits, cap_len, 0), digits)
        found.append(jnp.sum(digits * factor, 1, keepdims=True))
    found = jnp.concatenate(found, 0)
    away = found.astype(jnp.int32) ^ pos_ref[0]
    block = (away & 1) * blocks
    for s, distance in enumerate(order):
        block += jnp.where(away - (away & 1) == distance, s, 0)
    first = block * held + iota((row_total, 1), 0) % cap_len
    column = iota((row_total, 2 * blocks * held), 1)
    pick = jnp.concatenate(
        [jnp.where(column == first + c * cap_len, 1.0, 0.0).astype(jnp.bfloat16) for c in range(pieces)], 0
    )
    picked = dot(pick, caps[...]).astype(jnp.bfloat16)
    for c in range(pieces):
        part = min(width, query.shape[1] - c * width)
        query[:, c * width : c * width + part] = picked[c * row_total : (c + 1) * row_total, 0:part]

    heads = TILE // HEAD_DIM
    group_rows = bias.shape[0] // heads
    image_keys = bias.shape[1] - group_rows
    lane = iota((group_rows, TILE), 1) // HEAD_DIM
    r, k = iota(bias.shape, 0) % group_rows, iota(bias.shape, 1)
    own = k - image_keys
    allowed = ((k < image_keys) & (k // prefix == r // pair_rows)) | (
        (own >= 0) & (own <= r) & (own // cap_len == r // cap_len)
    )
    bias[...] = jnp.where(allowed, 0.0, -1e30)
    tiles = [
        (g, slice(i * TILE, (i + 1) * TILE))
        for i in range(model_width // TILE)
        for g in range(row_total // group_rows)
    ]

    def keys_of(g, cols):
        q = query[g * group_rows : (g + 1) * group_rows, cols]
        return q, jnp.concatenate([keys[g * image_keys : (g + 1) * image_keys, cols], q], 0)

    for n, (g, cols) in enumerate(tiles):
        q, key = keys_of(g, cols)
        scaled, zero = q * score_scale, jnp.zeros_like(q)
        every = jnp.concatenate([jnp.where(lane == h, scaled, zero) for h in range(heads)], 0)
        scores[n] = dot_rows(every, key)
    for n in range(len(tiles)):
        score = scores[n] + bias[...]
        expo = jnp.exp(score - jnp.max(score, 1, keepdims=True))
        weights[n] = (expo * (1.0 / jnp.sum(expo, 1, keepdims=True))).astype(jnp.bfloat16)
    squares = [jnp.zeros((group_rows, TILE), jnp.float32) for _ in range(row_total // group_rows)]
    for n, (g, cols) in enumerate(tiles):
        q, key = keys_of(g, cols)
        out = dot(weights[n], key)
        value = q.astype(jnp.float32)
        for h in range(heads):
            value += jnp.where(lane == h, out[h * group_rows : (h + 1) * group_rows], 0.0)
        mixed[g * group_rows : (g + 1) * group_rows, cols] = value
        squares[g] += value * value
    square = jnp.concatenate(squares, 0)
    scale = lax.rsqrt(jnp.sum(square, 1, keepdims=True) / model_width + eps)
    out_ref[:, 0:model_width] = (mixed[...] * scale * gain_ref[...]).astype(jnp.bfloat16)
    marks = query[:, model_width:]
    out_ref[:, model_width:] = jnp.where(iota(marks.shape, 1) == 2, found.astype(jnp.bfloat16), marks)
    for copy in head_copies:
        copy.wait()


def logits_kernel(order, pos_ref, mine_ref, other_ref, first_ref, last_ref, length_ref, out_ref, states):
    half = mine_ref.shape[0]
    model_width = states.shape[1]
    row_total = 2 * half
    states[0:half, :] = mine_ref[:, 0:model_width]
    states[half:, :] = other_ref[:, 0:model_width]
    digits = jnp.concatenate(
        [ref[:, model_width:].astype(jnp.float32) for ref in (mine_ref, other_ref)], 0
    ).T
    vocab = first_ref.shape[0] + last_ref.shape[0]
    ids = (digits[0:1] * DIGIT + digits[1:2]).astype(jnp.int32) - pos_ref[0] * vocab
    tops, totals, targets = [], [], []
    before = 0
    for ref in (first_ref, last_ref):
        for i, j in cuts(ref.shape[0], -(-ref.shape[0] // TILE)):
            values = dot_rows(ref[i:j, :], states[...])
            top = jnp.max(values, 0, keepdims=True)
            tops.append(top)
            totals.append(jnp.sum(jnp.exp(values - top), 0, keepdims=True))
            hit = iota(values.shape, 0) == ids - (before + i)
            targets.append(jnp.sum(jnp.where(hit, values, 0.0), 0, keepdims=True))
        before += ref.shape[0]
    top = functools.reduce(jnp.maximum, tops)
    total = sum(t * jnp.exp(m - top) for t, m in zip(totals, tops))
    packed = jnp.concatenate(
        [top, total, sum(targets), length_ref[...], jnp.zeros((LANES - 4, row_total), jnp.float32)], 0
    ).T
    shards, rows = out_ref.shape[:2]
    for j in range(shards):
        away = order[j % len(order)] + j // len(order)
        out_ref[pos_ref[0] ^ away] = packed[j * rows : (j + 1) * rows]


def finish_kernel(stats_ref, mine_ref, out_ref):
    stats = stats_ref[...]
    shards, rows, _ = stats.shape
    cap_len = out_ref.shape[2]
    model_width = mine_ref.shape[1] - LANES
    lane = iota((rows, LANES), 1)
    top = jnp.max(stats, 0)[:, 0:1]
    total = jnp.zeros((rows, 1), jnp.float32)
    target = jnp.zeros((rows, 1), jnp.float32)
    length = jnp.zeros((rows, 1), jnp.float32)
    cand = mine_ref[0:16, model_width:].astype(jnp.float32)[0:rows, 2:3]
    for e in range(shards):
        total += stats[e][:, 1:2] * jnp.exp(stats[e][:, 0:1] - top)
        target += stats[e][:, 2:3]
        length += jnp.where(cand == e, stats[e][:, 3:4], 0.0)
    loglik = target - (top + jnp.log(total))
    token = iota((rows, LANES), 0) % cap_len
    kept = (token == lane) & (token.astype(jnp.float32) < length)
    spread = jnp.where(kept, loglik, 0.0)
    for k in range(out_ref.shape[1]):
        out_ref[0, k : k + 1, :] = jnp.sum(spread[k * cap_len : (k + 1) * cap_len], 0, keepdims=True)[:, 0:cap_len]


def paired(
    query_rows, proj_weight, proj_bias, candidates, caption_states, caption_ids, caption_lengths, norm_gain, head_weight
):
    shards = lax.axis_size("dp")
    blocks = shards // 2
    _, prefix, width = query_rows.shape
    _, cap_len, model_width = caption_states.shape
    top_count = candidates.shape[1]
    pair_rows = top_count * cap_len
    piece_rows = cap_len * -(-model_width // width)
    held = -(-piece_rows // 16) * 16
    row_total = blocks * pair_rows
    vocab = head_weight.shape[1]
    position = lax.axis_index("dp").astype(jnp.int32).reshape(1)
    ahead = vocab * 3 // 8 // TILE * TILE
    heads, group = TILE // HEAD_DIM, LANES // prefix
    score_tiles = model_width // TILE * blocks // group

    def swap(a, away):
        return lax.ppermute(a, "dp", [(i, i ^ away) for i in range(shards)])

    message = pl.pallas_call(
        pack_kernel,
        out_shape=jax.ShapeDtypeStruct((piece_rows + prefix, width), jnp.bfloat16),
        in_specs=[HBM] * 4,
        out_specs=VMEM,
        scratch_shapes=[
            pltpu.SMEM(candidates.shape, jnp.int32),
            pltpu.SMEM(caption_ids.shape, jnp.int32),
            pltpu.VMEM(query_rows.shape, jnp.bfloat16),
            pltpu.VMEM(caption_states.shape, jnp.bfloat16),
            pltpu.VMEM((piece_rows, width), jnp.float32),
            pltpu.SemaphoreType.DMA((4,)),
        ],
        compiler_params=pltpu.CompilerParams(vmem_limit_bytes=2 * MIB),
        name="pack",
    )(*(in_hbm(a) for a in (candidates, caption_ids, query_rows, caption_states)))

    got = {0: message}
    for away in (12, 4, 2):
        got[away] = swap(message, away)
    weight, bias, gain, length = pl.pallas_call(
        bring_kernel,
        out_shape=(
            pltpu.VMEM((width, model_width), jnp.bfloat16),
            pltpu.VMEM((1, model_width), jnp.float32),
            pltpu.VMEM((1, model_width), jnp.float32),
            pltpu.VMEM((1, LANES), jnp.float32),
        ),
        in_specs=[SMEM] * 2 + [HBM] * 3,
        out_specs=(VMEM,) * 4,
        scratch_shapes=[pltpu.VMEM((model_width,), jnp.bfloat16), pltpu.SemaphoreType.DMA((3,))],
        compiler_params=pltpu.CompilerParams(vmem_limit_bytes=2 * MIB),
        cost_estimate=pl.CostEstimate(flops=0, bytes_accessed=4 * width * model_width, transcendentals=0),
        name="bring",
    )(position, caption_lengths, *(in_hbm(a) for a in (proj_weight, proj_bias, norm_gain.reshape(1, -1))))
    got[12], length = lax.optimization_barrier((got[12], length))
    got[8] = swap(got[12], 4)
    for away in (12, 4, 8):
        got[away + 2] = swap(got[away], 2)
    head_weight = in_hbm(head_weight.T)
    head_first, done = pl.pallas_call(
        bring_head_kernel,
        out_shape=(
            pltpu.VMEM((ahead, model_width), jnp.bfloat16),
            pltpu.VMEM((8, LANES), jnp.float32),
        ),
        in_specs=[ANY, HBM],
        out_specs=(VMEM, VMEM),
        scratch_shapes=[pltpu.SemaphoreType.DMA((4,))],
        compiler_params=pltpu.CompilerParams(vmem_limit_bytes=2 * MIB),
        cost_estimate=pl.CostEstimate(flops=0, bytes_accessed=4 * ahead * model_width, transcendentals=0),
        name="bring_head",
    )(got[8], head_weight)
    order = (0, 12, 4, 2, 8, 14, 6, 10)
    mine = [got[away] for away in order]

    def collect(msgs, *after):
        return pl.pallas_call(
            functools.partial(collect_kernel, len(msgs)),
            out_shape=jax.ShapeDtypeStruct((len(msgs) * held, width), jnp.bfloat16),
            in_specs=[VMEM] * len(msgs) + [ANY] * len(after),
            out_specs=VMEM,
            compiler_params=pltpu.CompilerParams(vmem_limit_bytes=2 * MIB),
            name="collect",
        )(*msgs, *after)

    near, far = collect(mine[: blocks // 2]), collect(mine[blocks // 2 :], done)
    other_near, other_far = swap(near, 1), swap(far, 1)

    keys = pl.pallas_call(
        functools.partial(keys_kernel, blocks),
        out_shape=pltpu.VMEM((blocks * prefix, model_width), jnp.bfloat16),
        in_specs=[VMEM] * (blocks + 2),
        out_specs=VMEM,
        scratch_shapes=[pltpu.VMEM((blocks * prefix, width), jnp.bfloat16)],
        compiler_params=pltpu.CompilerParams(vmem_limit_bytes=8 * MIB),
        cost_estimate=pl.CostEstimate(
            flops=2 * blocks * prefix * width * model_width, bytes_accessed=4 * width * model_width, transcendentals=0
        ),
        name="keys",
    )(*mine, weight, bias)

    hidden, head_last = pl.pallas_call(
        functools.partial(hidden_kernel, order, prefix, cap_len),
        out_shape=(
            jax.ShapeDtypeStruct((row_total, model_width + LANES), jnp.bfloat16),
            pltpu.VMEM((vocab - ahead, model_width), jnp.bfloat16),
        ),
        in_specs=[SMEM] + [VMEM] * 6 + [HBM],
        out_specs=(VMEM, VMEM),
        scratch_shapes=[
            pltpu.VMEM((2 * blocks * held, width), jnp.bfloat16),
            pltpu.VMEM((row_total, model_width + LANES), jnp.bfloat16),
            pltpu.VMEM((row_total, model_width), jnp.float32),
            pltpu.VMEM((heads * group * pair_rows, group * (prefix + pair_rows)), jnp.float32),
            pltpu.VMEM((score_tiles, heads * group * pair_rows, group * (prefix + pair_rows)), jnp.float32),
            pltpu.VMEM((score_tiles, heads * group * pair_rows, group * (prefix + pair_rows)), jnp.bfloat16),
            pltpu.SemaphoreType.DMA((8,)),
        ],
        compiler_params=pltpu.CompilerParams(vmem_limit_bytes=24 * MIB),
        name="hidden",
    )(position, near, far, other_near, other_far, keys, gain, head_weight)

    stats = pl.pallas_call(
        functools.partial(logits_kernel, order),
        out_shape=jax.ShapeDtypeStruct((shards, pair_rows, LANES), jnp.float32),
        in_specs=[SMEM] + [VMEM] * 5,
        out_specs=VMEM,
        scratch_shapes=[pltpu.VMEM((2 * row_total, model_width), jnp.bfloat16)],
        compiler_params=pltpu.CompilerParams(vmem_limit_bytes=16 * MIB),
        name="logits",
    )(position, hidden, swap(hidden, 1), head_first, head_last, length)

    stats = lax.all_to_all(stats, "dp", 0, 0, tiled=True)
    return pl.pallas_call(
        finish_kernel,
        out_shape=jax.ShapeDtypeStruct((1, top_count, cap_len), jnp.float32),
        in_specs=[VMEM, VMEM],
        out_specs=VMEM,
        compiler_params=pltpu.CompilerParams(vmem_limit_bytes=2 * MIB),
        name="finish",
    )(stats, hidden)


def merged(part, axis, combine):
    gathered = jax.tree.map(lambda a: lax.all_gather(a, axis), part)

    def take(source):
        return jax.tree.map(lambda a: lax.dynamic_index_in_dim(a, source, 0, False), gathered)

    return lax.fori_loop(
        1, lax.axis_size(axis), lambda source, state: combine(state, take(source)), take(0)
    )


def project(rows, proj_weight, proj_bias):
    row_total, prefix_len, query_width = rows.shape
    summed = jnp.dot(
        rows.reshape(row_total * prefix_len, query_width),
        proj_weight,
        preferred_element_type=jnp.float32,
    )
    projected = (summed + proj_bias.astype(jnp.float32)).astype(jnp.bfloat16)
    return projected.reshape(row_total, prefix_len, proj_weight.shape[1])


def attend(projected, states, norm_gain):
    prefix_len = projected.shape[0]
    cap_len, model_width = states.shape
    heads = model_width // HEAD_DIM
    keys = jnp.concatenate([projected, states], 0)
    query = states.reshape(cap_len, heads, HEAD_DIM)
    keyed = keys.reshape(prefix_len + cap_len, heads, HEAD_DIM)
    scores = (
        jnp.einsum("thd,jhd->htj", query, keyed, preferred_element_type=jnp.float32) * score_scale
    )
    key_pos = jnp.arange(prefix_len + cap_len)[None, :]
    tok_pos = jnp.arange(cap_len)[:, None]
    allowed = (key_pos < prefix_len) | (key_pos - prefix_len <= tok_pos)
    scores = jnp.where(allowed[None], scores, -jnp.inf)
    row_max = jnp.max(scores, -1, keepdims=True)
    expo = jnp.exp(scores - row_max)
    weights = (expo / jnp.sum(expo, -1, keepdims=True)).astype(jnp.bfloat16)
    mixed_out = jnp.einsum(
        "htj,jhd->thd", weights, keyed, preferred_element_type=jnp.float32
    ).reshape(cap_len, model_width)
    mixed = states.astype(jnp.float32) + mixed_out
    normed = mixed * lax.rsqrt(jnp.mean(mixed * mixed, -1, keepdims=True) + eps) * norm_gain
    return normed.astype(jnp.bfloat16)


def merge_totals(first, second):
    larger = jnp.maximum(first[0], second[0])
    summed = first[1] * jnp.exp(first[0] - larger) + second[1] * jnp.exp(second[0] - larger)
    return (larger, summed, first[2] + second[2])


def spread(
    query_rows,
    proj_weight,
    proj_bias,
    candidates,
    caption_states,
    caption_ids,
    caption_lengths,
    norm_gain,
    head_weight,
):
    position = lax.axis_index("dp")
    img_local, top_count = candidates.shape
    pair_count = img_local * top_count
    cap_local, cap_len, model_width = caption_states.shape
    own_cand = candidates.reshape(pair_count)
    all_cand, all_len = (
        lax.all_gather(candidates, "dp", axis=0, tiled=True),
        lax.all_gather(caption_lengths, "dp", axis=0, tiled=True),
    )
    caption_total = all_len.shape[0]
    length_match = own_cand[:, None] == jnp.arange(caption_total)[None, :]
    pair_len = jnp.sum(jnp.where(length_match, all_len[None, :], 0), 1)
    piece_states = lax.all_gather(caption_states, "dp", axis=0, tiled=True)
    piece_ids = lax.all_gather(caption_ids, "dp", axis=0, tiled=True)
    piece_rows = piece_states.shape[0]
    matches = own_cand[:, None] == jnp.arange(piece_rows)[None, :]
    picked = jnp.dot(
        matches.astype(jnp.bfloat16),
        piece_states.reshape(piece_rows, cap_len * model_width),
        preferred_element_type=jnp.float32,
    )
    fetched_ids = jnp.sum(jnp.where(matches[:, :, None], piece_ids[None, :, :], 0), 1).astype(
        jnp.int32
    )
    pair_states = picked.astype(jnp.bfloat16).reshape(pair_count, cap_len, model_width)
    image_proj = project(query_rows, proj_weight, proj_bias)
    pair_proj = jnp.repeat(image_proj, top_count, axis=0)
    work_hidden = jax.vmap(lambda one, two: attend(one, two, norm_gain))(pair_proj, pair_states)
    row_base = (position * pair_count + jnp.arange(pair_count)) * cap_len
    row_count = work_hidden.shape[0] * cap_len
    hidden_rows = work_hidden.reshape(row_count, model_width)
    id_rows = fetched_ids.reshape(row_count)
    vocab_dev = head_weight.shape[1]
    vocab_start = position * vocab_dev
    every_state, every_id = (
        lax.all_gather(hidden_rows, "dp", axis=0, tiled=True),
        lax.all_gather(id_rows, "dp", axis=0, tiled=True),
    )
    logits = jnp.dot(every_state, head_weight, preferred_element_type=jnp.float32)
    local_max = jnp.max(logits, 1)
    local_sum = jnp.sum(jnp.exp(logits - local_max[:, None]), 1)
    target_hit = jnp.arange(vocab_dev)[None, :] == (every_id - vocab_start)[:, None]
    local_pick = jnp.sum(jnp.where(target_hit, logits, 0.0), 1)
    top_all, sum_all, picked_all = merged((local_max, local_sum, local_pick), "dp", merge_totals)
    row_index = row_base[:, None] + jnp.arange(cap_len)[None, :]
    own_top = jnp.take(top_all, row_index)
    own_sum = jnp.take(sum_all, row_index)
    own_picked = jnp.take(picked_all, row_index)
    loglik = own_picked - (own_top + jnp.log(own_sum))
    inside = jnp.arange(cap_len)[None, :] < pair_len[:, None]
    result = jnp.where(inside, loglik, jnp.float32(0.0))
    return result.reshape(img_local, top_count, cap_len)


def local(query_rows, proj_weight, proj_bias, candidates, caption_states, *rest):
    one_each = candidates.shape[0] == 1 and caption_states.shape[0] == 1
    fits = candidates.shape[1] == 2 and caption_states.shape[1] == 4 and query_rows.shape[1] == 32
    plan = paired if lax.axis_size("dp") == 16 and one_each and fits else spread
    return plan(query_rows, proj_weight, proj_bias, candidates, caption_states, *rest)


def solution(mesh):
    in_specs = (
        P(("groups", "dp"), None, None),
        P(),
        P(),
        P(("groups", "dp"), None),
        P(("groups", "dp"), None, None),
        P(("groups", "dp"), None),
        P(("groups", "dp")),
        P(),
        P(None, "dp"),
    )
    out_specs = P(("groups", "dp"), None, None)
    return jax.shard_map(local, mesh=mesh, in_specs=in_specs, out_specs=out_specs, check_vma=False)
```

```python
import functools

import jax
import jax.numpy as jnp
from jax import lax
from jax.experimental import pallas as pl
from jax.experimental.pallas import tpu as pltpu
from jax.sharding import PartitionSpec as P

HEAD_DIM = 64
LANES = 128
SUBLANES = 8
TILE = 256
DIGIT = 256
MIB = 1 << 20


score_scale = 0.015625
eps = 1e-06

VMEM = pl.BlockSpec(memory_space=pltpu.VMEM)
SMEM = pl.BlockSpec(memory_space=pltpu.SMEM)
HBM = pl.BlockSpec(memory_space=pltpu.HBM)
ANY = pl.BlockSpec(memory_space=pl.ANY)
ROWS_BY_ROWS = (((1,), (1,)), ((), ()))


def iota(shape, dim):
    return lax.broadcasted_iota(jnp.int32, shape, dim)


def in_hbm(a):
    return pltpu.with_memory_space_constraint(a, pltpu.HBM)


def dot(a, b):
    return jnp.dot(a, b, preferred_element_type=jnp.float32)


def dot_rows(a, b):
    return lax.dot_general(a, b, ROWS_BY_ROWS, preferred_element_type=jnp.float32)


def pack_kernel(cand_hbm, ids_hbm, rows_hbm, states_hbm, out_ref, cand, ids, rows, states, stage, sem):
    copies = [
        pltpu.make_async_copy(src, dst, sem.at[i])
        for i, (src, dst) in enumerate(
            ((cand_hbm, cand), (ids_hbm, ids), (rows_hbm, rows), (states_hbm, states))
        )
    ]
    for copy in copies:
        copy.start()
    for copy in copies:
        copy.wait()
    width = rows.shape[2]
    cap_len, model_width = states.shape[1:]
    pieces = -(-model_width // width)
    held = pieces * cap_len
    values = states[0].astype(jnp.float32)
    for c in range(pieces - 1):
        stage[c * cap_len : (c + 1) * cap_len, :] = values[:, c * width : (c + 1) * width]
    rest = model_width - (pieces - 1) * width
    last = held - cap_len
    stage[last:held, 0:rest] = values[:, model_width - rest :]
    token, lane = iota((cap_len, width - rest), 0), iota((cap_len, width - rest), 1)
    digits = jnp.zeros_like(token)
    for t in range(cap_len):
        digits = jnp.where(token == t, jnp.where(lane == 0, ids[0, t] // DIGIT, ids[0, t] % DIGIT), digits)
    digits = jnp.where(lane < 2, digits, 0)
    for k in range(cand.shape[1]):
        digits = jnp.where(lane == 2 + 2 * k, cand[0, k] // DIGIT, digits)
        digits = jnp.where(lane == 3 + 2 * k, cand[0, k] % DIGIT, digits)
    stage[last:held, rest:] = digits.astype(jnp.float32)
    out_ref[0:held, :] = stage[...].astype(jnp.bfloat16)
    out_ref[held:, :] = rows[0]


def bring_kernel(pos_ref, len_ref, weight_hbm, bias_hbm, gain_hbm, weight_ref, bias_ref, gain_ref, length_ref, bias, sem):
    pairs = ((bias_hbm, bias), (gain_hbm, gain_ref), (weight_hbm, weight_ref))
    copies = [pltpu.make_async_copy(src, dst, sem.at[i]) for i, (src, dst) in enumerate(pairs)]
    for copy in copies:
        copy.start()
    length_ref[...] = jnp.full(length_ref.shape, len_ref[0].astype(jnp.float32))
    copies[0].wait()
    bias_ref[...] = bias[...].astype(jnp.float32).reshape(bias_ref.shape)
    for copy in copies[1:]:
        copy.wait()


def cuts(total, parts):
    piece = -(-total // parts // 16) * 16
    return [(i, min(total, i + piece)) for i in range(0, total, piece)]


def copies_of(src, first, dst, sem):
    return [
        pltpu.make_async_copy(src.at[first + i : first + j], dst.at[i:j], sem.at[n])
        for n, (i, j) in enumerate(cuts(dst.shape[0], sem.shape[0]))
    ]


def bring_head_kernel(after_ref, head_hbm, head_ref, done_ref, sem):
    copies = copies_of(head_hbm, 0, head_ref, sem)
    for copy in copies:
        copy.start()
    done_ref[...] = jnp.zeros_like(done_ref)
    for copy in copies:
        copy.wait()


def collect_kernel(count, *refs):
    msgs, out_ref = refs[:count], refs[-1]
    held = out_ref.shape[0] // count
    for i, msg in enumerate(msgs):
        out_ref[i * held : (i + 1) * held, :] = msg[0:held, :]


def keys_kernel(blocks, *refs):
    msgs, (weight, bias, keys, rows) = refs[:blocks], refs[blocks:]
    prefix = rows.shape[0] // blocks
    for j, msg in enumerate(msgs):
        rows[j * prefix : (j + 1) * prefix, :] = msg[msg.shape[0] - prefix :, :]
    step = 512
    for i in range(0, keys.shape[1], step):
        summed = dot(rows[...], weight[:, i : i + step])
        keys[:, i : i + step] = (summed + bias[:, i : i + step]).astype(jnp.bfloat16)


def hidden_kernel(order, prefix, cap_len, *refs):
    pos_ref, *cap_refs = refs[:5]
    keys, gain_ref, head_hbm, out_ref, head_ref, caps, query, mixed, bias, scores, weights, sem = refs[5:]
    head_copies = copies_of(head_hbm, head_hbm.shape[0] - head_ref.shape[0], head_ref, sem)
    for copy in head_copies:
        copy.start()
    blocks = len(order)
    width = caps.shape[1]
    model_width = mixed.shape[1]
    row_total = query.shape[0]
    held, pair_rows = caps.shape[0] // (2 * blocks), row_total // blocks
    pieces = -(-model_width // width)

    start = 0
    for ref in cap_refs:
        caps[start : start + ref.shape[0], :] = ref[...]
        start += ref.shape[0]
    rest = model_width - (pieces - 1) * width
    last = (pieces - 2) * cap_len
    row, lane = iota((pair_rows, LANES), 0), iota((pair_rows, LANES), 1)
    place = 2 + 2 * (row // cap_len)
    factor = jnp.where(lane == place, float(DIGIT), jnp.where(lane == place + 1, 1.0, 0.0))
    found = []
    for s in range(blocks):
        digits = caps[s * held + last : s * held + last + pair_rows, rest : rest + LANES].astype(jnp.float32)
        digits = jnp.where(row < cap_len, pltpu.roll(digits, cap_len, 0), digits)
        found.append(jnp.sum(digits * factor, 1, keepdims=True))
    found = jnp.concatenate(found, 0)
    away = found.astype(jnp.int32) ^ pos_ref[0]
    block = (away & 1) * blocks
    for s, distance in enumerate(order):
        block += jnp.where(away - (away & 1) == distance, s, 0)
    first = block * held + iota((row_total, 1), 0) % cap_len
    column = iota((row_total, 2 * blocks * held), 1)
    pick = jnp.concatenate(
        [jnp.where(column == first + c * cap_len, 1.0, 0.0).astype(jnp.bfloat16) for c in range(pieces)], 0
    )
    picked = dot(pick, caps[...]).astype(jnp.bfloat16)
    for c in range(pieces):
        part = min(width, query.shape[1] - c * width)
        query[:, c * width : c * width + part] = picked[c * row_total : (c + 1) * row_total, 0:part]

    heads = TILE // HEAD_DIM
    group_rows = bias.shape[0] // heads
    image_keys = bias.shape[1] - group_rows
    lane = iota((group_rows, TILE), 1) // HEAD_DIM
    r, k = iota(bias.shape, 0) % group_rows, iota(bias.shape, 1)
    own = k - image_keys
    allowed = ((k < image_keys) & (k // prefix == r // pair_rows)) | (
        (own >= 0) & (own <= r) & (own // cap_len == r // cap_len)
    )
    bias[...] = jnp.where(allowed, 0.0, -1e30)
    tiles = [
        (g, slice(i * TILE, (i + 1) * TILE))
        for i in range(model_width // TILE)
        for g in range(row_total // group_rows)
    ]

    def keys_of(g, cols):
        q = query[g * group_rows : (g + 1) * group_rows, cols]
        return q, jnp.concatenate([keys[g * image_keys : (g + 1) * image_keys, cols], q], 0)

    for n, (g, cols) in enumerate(tiles):
        q, key = keys_of(g, cols)
        scaled, zero = q * score_scale, jnp.zeros_like(q)
        every = jnp.concatenate([jnp.where(lane == h, scaled, zero) for h in range(heads)], 0)
        scores[n] = dot_rows(every, key)
    for n in range(len(tiles)):
        score = scores[n] + bias[...]
        expo = jnp.exp(score - jnp.max(score, 1, keepdims=True))
        weights[n] = (expo * (1.0 / jnp.sum(expo, 1, keepdims=True))).astype(jnp.bfloat16)
    squares = [jnp.zeros((group_rows, TILE), jnp.float32) for _ in range(row_total // group_rows)]
    for n, (g, cols) in enumerate(tiles):
        q, key = keys_of(g, cols)
        out = dot(weights[n], key)
        value = q.astype(jnp.float32)
        for h in range(heads):
            value += jnp.where(lane == h, out[h * group_rows : (h + 1) * group_rows], 0.0)
        mixed[g * group_rows : (g + 1) * group_rows, cols] = value
        squares[g] += value * value
    square = jnp.concatenate(squares, 0)
    scale = lax.rsqrt(jnp.sum(square, 1, keepdims=True) / model_width + eps)
    out_ref[:, 0:model_width] = (mixed[...] * scale * gain_ref[...]).astype(jnp.bfloat16)
    marks = query[:, model_width:]
    out_ref[:, model_width:] = jnp.where(iota(marks.shape, 1) == 2, found.astype(jnp.bfloat16), marks)
    for copy in head_copies:
        copy.wait()


def logits_kernel(order, pos_ref, mine_ref, other_ref, first_ref, last_ref, length_ref, out_ref, states):
    half = mine_ref.shape[0]
    model_width = states.shape[1]
    row_total = 2 * half
    states[0:half, :] = mine_ref[:, 0:model_width]
    states[half:, :] = other_ref[:, 0:model_width]
    digits = jnp.concatenate(
        [ref[:, model_width:].astype(jnp.float32) for ref in (mine_ref, other_ref)], 0
    ).T
    vocab = first_ref.shape[0] + last_ref.shape[0]
    ids = (digits[0:1] * DIGIT + digits[1:2]).astype(jnp.int32) - pos_ref[0] * vocab
    tops, totals, targets = [], [], []
    before = 0
    for ref in (first_ref, last_ref):
        for i, j in cuts(ref.shape[0], -(-ref.shape[0] // TILE)):
            values = dot_rows(ref[i:j, :], states[...])
            top = jnp.max(values, 0, keepdims=True)
            tops.append(top)
            totals.append(jnp.sum(jnp.exp(values - top), 0, keepdims=True))
            hit = iota(values.shape, 0) == ids - (before + i)
            targets.append(jnp.sum(jnp.where(hit, values, 0.0), 0, keepdims=True))
        before += ref.shape[0]
    top = functools.reduce(jnp.maximum, tops)
    total = sum(t * jnp.exp(m - top) for t, m in zip(totals, tops))
    shards, _, width = out_ref.shape
    rows = row_total // shards
    field = iota((SUBLANES, width), 1) // rows
    halves = []
    for start in range(0, shards, SUBLANES):
        half = jnp.zeros((SUBLANES, width), jnp.float32)
        for s, values in enumerate((top, total, sum(targets), length_ref[...])):
            shift = (s + 1 + start) * rows % width
            spread = jnp.broadcast_to(pltpu.roll(values, shift, 1) if shift else values, half.shape)
            half = jnp.where(field == s, pltpu.roll(spread, 0, 1, stride=rows, stride_axis=0), half)
        halves.append(half)
    packed = jnp.concatenate(halves, 0)
    for j in range(shards):
        away = order[j % len(order)] + j // len(order)
        out_ref[pos_ref[0] ^ away] = packed[shards - 1 - j : shards - j]


def finish_kernel(stats_ref, mine_ref, out_ref):
    shards, _, width = stats_ref.shape
    _, top_count, cap_len = out_ref.shape
    rows = top_count * cap_len
    tops = jnp.concatenate([stats_ref[e] for e in range(shards)], 0)
    totals, targets, lengths = (pltpu.roll(tops, width - s * rows, 1) for s in (1, 2, 3))
    marks = mine_ref[0:16, mine_ref.shape[1] - width :].astype(jnp.float32)
    cand = jnp.where(iota(marks.shape, 0) == iota(marks.shape, 1), marks[:, 2:3], 0.0)
    cand = jnp.sum(cand, 0, keepdims=True).astype(jnp.int32)
    length = jnp.sum(jnp.where(iota(tops.shape, 0) == cand, lengths, 0.0), 0, keepdims=True)
    top = jnp.max(tops, 0, keepdims=True)
    total = jnp.sum(totals * jnp.exp(tops - top), 0, keepdims=True)
    loglik = jnp.sum(targets, 0, keepdims=True) - (top + jnp.log(total))
    token = (iota(loglik.shape, 1) % cap_len).astype(jnp.float32)
    loglik = jnp.where(token < length, loglik, 0.0)
    for k in range(top_count):
        out_ref[0, k : k + 1, :] = loglik[:, k * cap_len : (k + 1) * cap_len]


def paired(
    query_rows, proj_weight, proj_bias, candidates, caption_states, caption_ids, caption_lengths, norm_gain, head_weight
):
    shards = lax.axis_size("dp")
    blocks = shards // 2
    _, prefix, width = query_rows.shape
    _, cap_len, model_width = caption_states.shape
    top_count = candidates.shape[1]
    pair_rows = top_count * cap_len
    piece_rows = cap_len * -(-model_width // width)
    held = -(-piece_rows // 16) * 16
    row_total = blocks * pair_rows
    vocab = head_weight.shape[1]
    position = lax.axis_index("dp").astype(jnp.int32).reshape(1)
    ahead = vocab // 2 // TILE * TILE + TILE
    heads, group = TILE // HEAD_DIM, LANES // prefix
    score_tiles = model_width // TILE * blocks // group

    def swap(a, away):
        return lax.ppermute(a, "dp", [(i, i ^ away) for i in range(shards)])

    message = pl.pallas_call(
        pack_kernel,
        out_shape=jax.ShapeDtypeStruct((piece_rows + prefix, width), jnp.bfloat16),
        in_specs=[HBM] * 4,
        out_specs=VMEM,
        scratch_shapes=[
            pltpu.SMEM(candidates.shape, jnp.int32),
            pltpu.SMEM(caption_ids.shape, jnp.int32),
            pltpu.VMEM(query_rows.shape, jnp.bfloat16),
            pltpu.VMEM(caption_states.shape, jnp.bfloat16),
            pltpu.VMEM((piece_rows, width), jnp.float32),
            pltpu.SemaphoreType.DMA((4,)),
        ],
        compiler_params=pltpu.CompilerParams(vmem_limit_bytes=2 * MIB),
        name="pack",
    )(*(in_hbm(a) for a in (candidates, caption_ids, query_rows, caption_states)))

    got = {0: message}
    for away in (12, 8, 4, 2):
        got[away] = swap(message, away)
    weight, bias, gain, length = pl.pallas_call(
        bring_kernel,
        out_shape=(
            pltpu.VMEM((width, model_width), jnp.bfloat16),
            pltpu.VMEM((1, model_width), jnp.float32),
            pltpu.VMEM((1, model_width), jnp.float32),
            pltpu.VMEM((1, LANES), jnp.float32),
        ),
        in_specs=[SMEM] * 2 + [HBM] * 3,
        out_specs=(VMEM,) * 4,
        scratch_shapes=[pltpu.VMEM((model_width,), jnp.bfloat16), pltpu.SemaphoreType.DMA((3,))],
        compiler_params=pltpu.CompilerParams(vmem_limit_bytes=2 * MIB),
        cost_estimate=pl.CostEstimate(flops=0, bytes_accessed=4 * width * model_width, transcendentals=0),
        name="bring",
    )(position, caption_lengths, *(in_hbm(a) for a in (proj_weight, proj_bias, norm_gain.reshape(1, -1))))
    got[6] = swap(got[4], 2)
    got[12], length = lax.optimization_barrier((got[12], length))
    for away in (12, 8):
        got[away + 2] = swap(got[away], 2)
    head_weight = in_hbm(head_weight.T)
    head_first, done = pl.pallas_call(
        bring_head_kernel,
        out_shape=(
            pltpu.VMEM((ahead, model_width), jnp.bfloat16),
            pltpu.VMEM((8, LANES), jnp.float32),
        ),
        in_specs=[ANY, HBM],
        out_specs=(VMEM, VMEM),
        scratch_shapes=[pltpu.SemaphoreType.DMA((4,))],
        compiler_params=pltpu.CompilerParams(vmem_limit_bytes=2 * MIB),
        cost_estimate=pl.CostEstimate(flops=0, bytes_accessed=4 * ahead * model_width, transcendentals=0),
        name="bring_head",
    )(got[8], head_weight)
    order = (0, 2, 4, 6, 8, 12, 10, 14)
    mine = [got[away] for away in order]

    def collect(msgs, *after):
        return pl.pallas_call(
            functools.partial(collect_kernel, len(msgs)),
            out_shape=jax.ShapeDtypeStruct((len(msgs) * held, width), jnp.bfloat16),
            in_specs=[VMEM] * len(msgs) + [ANY] * len(after),
            out_specs=VMEM,
            compiler_params=pltpu.CompilerParams(vmem_limit_bytes=2 * MIB),
            name="collect",
        )(*msgs, *after)

    near, far = collect(mine[: blocks // 2]), collect(mine[blocks // 2 :], done)
    other_near, other_far = swap(near, 1), swap(far, 1)

    keys = pl.pallas_call(
        functools.partial(keys_kernel, blocks),
        out_shape=pltpu.VMEM((blocks * prefix, model_width), jnp.bfloat16),
        in_specs=[VMEM] * (blocks + 2),
        out_specs=VMEM,
        scratch_shapes=[pltpu.VMEM((blocks * prefix, width), jnp.bfloat16)],
        compiler_params=pltpu.CompilerParams(vmem_limit_bytes=8 * MIB),
        cost_estimate=pl.CostEstimate(
            flops=2 * blocks * prefix * width * model_width, bytes_accessed=4 * width * model_width, transcendentals=0
        ),
        name="keys",
    )(*mine, weight, bias)

    hidden, head_last = pl.pallas_call(
        functools.partial(hidden_kernel, order, prefix, cap_len),
        out_shape=(
            jax.ShapeDtypeStruct((row_total, model_width + LANES), jnp.bfloat16),
            pltpu.VMEM((vocab - ahead, model_width), jnp.bfloat16),
        ),
        in_specs=[SMEM] + [VMEM] * 6 + [HBM],
        out_specs=(VMEM, VMEM),
        scratch_shapes=[
            pltpu.VMEM((2 * blocks * held, width), jnp.bfloat16),
            pltpu.VMEM((row_total, model_width + LANES), jnp.bfloat16),
            pltpu.VMEM((row_total, model_width), jnp.float32),
            pltpu.VMEM((heads * group * pair_rows, group * (prefix + pair_rows)), jnp.float32),
            pltpu.VMEM((score_tiles, heads * group * pair_rows, group * (prefix + pair_rows)), jnp.float32),
            pltpu.VMEM((score_tiles, heads * group * pair_rows, group * (prefix + pair_rows)), jnp.bfloat16),
            pltpu.SemaphoreType.DMA((8,)),
        ],
        compiler_params=pltpu.CompilerParams(vmem_limit_bytes=24 * MIB),
        name="hidden",
    )(position, near, far, other_near, other_far, keys, gain, head_weight)

    stats = pl.pallas_call(
        functools.partial(logits_kernel, order),
        out_shape=jax.ShapeDtypeStruct((shards, 1, LANES), jnp.float32),
        in_specs=[SMEM] + [VMEM] * 5,
        out_specs=VMEM,
        scratch_shapes=[pltpu.VMEM((2 * row_total, model_width), jnp.bfloat16)],
        compiler_params=pltpu.CompilerParams(vmem_limit_bytes=16 * MIB),
        name="logits",
    )(position, hidden, swap(hidden, 1), head_first, head_last, length)

    stats = lax.all_to_all(stats, "dp", 0, 0, tiled=True)
    return pl.pallas_call(
        finish_kernel,
        out_shape=jax.ShapeDtypeStruct((1, top_count, cap_len), jnp.float32),
        in_specs=[VMEM, VMEM],
        out_specs=VMEM,
        compiler_params=pltpu.CompilerParams(vmem_limit_bytes=2 * MIB),
        name="finish",
    )(stats, hidden)


def merged(part, axis, combine):
    gathered = jax.tree.map(lambda a: lax.all_gather(a, axis), part)

    def take(source):
        return jax.tree.map(lambda a: lax.dynamic_index_in_dim(a, source, 0, False), gathered)

    return lax.fori_loop(
        1, lax.axis_size(axis), lambda source, state: combine(state, take(source)), take(0)
    )


def project(rows, proj_weight, proj_bias):
    row_total, prefix_len, query_width = rows.shape
    summed = jnp.dot(
        rows.reshape(row_total * prefix_len, query_width),
        proj_weight,
        preferred_element_type=jnp.float32,
    )
    projected = (summed + proj_bias.astype(jnp.float32)).astype(jnp.bfloat16)
    return projected.reshape(row_total, prefix_len, proj_weight.shape[1])


def attend(projected, states, norm_gain):
    prefix_len = projected.shape[0]
    cap_len, model_width = states.shape
    heads = model_width // HEAD_DIM
    keys = jnp.concatenate([projected, states], 0)
    query = states.reshape(cap_len, heads, HEAD_DIM)
    keyed = keys.reshape(prefix_len + cap_len, heads, HEAD_DIM)
    scores = (
        jnp.einsum("thd,jhd->htj", query, keyed, preferred_element_type=jnp.float32) * score_scale
    )
    key_pos = jnp.arange(prefix_len + cap_len)[None, :]
    tok_pos = jnp.arange(cap_len)[:, None]
    allowed = (key_pos < prefix_len) | (key_pos - prefix_len <= tok_pos)
    scores = jnp.where(allowed[None], scores, -jnp.inf)
    row_max = jnp.max(scores, -1, keepdims=True)
    expo = jnp.exp(scores - row_max)
    weights = (expo / jnp.sum(expo, -1, keepdims=True)).astype(jnp.bfloat16)
    mixed_out = jnp.einsum(
        "htj,jhd->thd", weights, keyed, preferred_element_type=jnp.float32
    ).reshape(cap_len, model_width)
    mixed = states.astype(jnp.float32) + mixed_out
    normed = mixed * lax.rsqrt(jnp.mean(mixed * mixed, -1, keepdims=True) + eps) * norm_gain
    return normed.astype(jnp.bfloat16)


def merge_totals(first, second):
    larger = jnp.maximum(first[0], second[0])
    summed = first[1] * jnp.exp(first[0] - larger) + second[1] * jnp.exp(second[0] - larger)
    return (larger, summed, first[2] + second[2])


def spread(
    query_rows,
    proj_weight,
    proj_bias,
    candidates,
    caption_states,
    caption_ids,
    caption_lengths,
    norm_gain,
    head_weight,
):
    position = lax.axis_index("dp")
    img_local, top_count = candidates.shape
    pair_count = img_local * top_count
    cap_local, cap_len, model_width = caption_states.shape
    own_cand = candidates.reshape(pair_count)
    all_cand, all_len = (
        lax.all_gather(candidates, "dp", axis=0, tiled=True),
        lax.all_gather(caption_lengths, "dp", axis=0, tiled=True),
    )
    caption_total = all_len.shape[0]
    length_match = own_cand[:, None] == jnp.arange(caption_total)[None, :]
    pair_len = jnp.sum(jnp.where(length_match, all_len[None, :], 0), 1)
    piece_states = lax.all_gather(caption_states, "dp", axis=0, tiled=True)
    piece_ids = lax.all_gather(caption_ids, "dp", axis=0, tiled=True)
    piece_rows = piece_states.shape[0]
    matches = own_cand[:, None] == jnp.arange(piece_rows)[None, :]
    picked = jnp.dot(
        matches.astype(jnp.bfloat16),
        piece_states.reshape(piece_rows, cap_len * model_width),
        preferred_element_type=jnp.float32,
    )
    fetched_ids = jnp.sum(jnp.where(matches[:, :, None], piece_ids[None, :, :], 0), 1).astype(
        jnp.int32
    )
    pair_states = picked.astype(jnp.bfloat16).reshape(pair_count, cap_len, model_width)
    image_proj = project(query_rows, proj_weight, proj_bias)
    pair_proj = jnp.repeat(image_proj, top_count, axis=0)
    work_hidden = jax.vmap(lambda one, two: attend(one, two, norm_gain))(pair_proj, pair_states)
    row_base = (position * pair_count + jnp.arange(pair_count)) * cap_len
    row_count = work_hidden.shape[0] * cap_len
    hidden_rows = work_hidden.reshape(row_count, model_width)
    id_rows = fetched_ids.reshape(row_count)
    vocab_dev = head_weight.shape[1]
    vocab_start = position * vocab_dev
    every_state, every_id = (
        lax.all_gather(hidden_rows, "dp", axis=0, tiled=True),
        lax.all_gather(id_rows, "dp", axis=0, tiled=True),
    )
    logits = jnp.dot(every_state, head_weight, preferred_element_type=jnp.float32)
    local_max = jnp.max(logits, 1)
    local_sum = jnp.sum(jnp.exp(logits - local_max[:, None]), 1)
    target_hit = jnp.arange(vocab_dev)[None, :] == (every_id - vocab_start)[:, None]
    local_pick = jnp.sum(jnp.where(target_hit, logits, 0.0), 1)
    top_all, sum_all, picked_all = merged((local_max, local_sum, local_pick), "dp", merge_totals)
    row_index = row_base[:, None] + jnp.arange(cap_len)[None, :]
    own_top = jnp.take(top_all, row_index)
    own_sum = jnp.take(sum_all, row_index)
    own_picked = jnp.take(picked_all, row_index)
    loglik = own_picked - (own_top + jnp.log(own_sum))
    inside = jnp.arange(cap_len)[None, :] < pair_len[:, None]
    result = jnp.where(inside, loglik, jnp.float32(0.0))
    return result.reshape(img_local, top_count, cap_len)


def local(query_rows, proj_weight, proj_bias, candidates, caption_states, *rest):
    one_each = candidates.shape[0] == 1 and caption_states.shape[0] == 1
    fits = candidates.shape[1] == 2 and caption_states.shape[1] == 4 and query_rows.shape[1] == 32
    plan = paired if lax.axis_size("dp") == 16 and one_each and fits else spread
    return plan(query_rows, proj_weight, proj_bias, candidates, caption_states, *rest)


def solution(mesh):
    in_specs = (
        P(("groups", "dp"), None, None),
        P(),
        P(),
        P(("groups", "dp"), None),
        P(("groups", "dp"), None, None),
        P(("groups", "dp"), None),
        P(("groups", "dp")),
        P(),
        P(None, "dp"),
    )
    out_specs = P(("groups", "dp"), None, None)
    return jax.shard_map(local, mesh=mesh, in_specs=in_specs, out_specs=out_specs, check_vma=False)
```

```python
import functools

import jax
import jax.numpy as jnp
from jax import lax
from jax.experimental import pallas as pl
from jax.experimental.pallas import tpu as pltpu
from jax.sharding import PartitionSpec as P

HEAD_DIM = 64
LANES = 128
SUBLANES = 8
TILE = 256
DIGIT = 256
MIB = 1 << 20


score_scale = 0.015625
eps = 1e-06

VMEM = pl.BlockSpec(memory_space=pltpu.VMEM)
SMEM = pl.BlockSpec(memory_space=pltpu.SMEM)
HBM = pl.BlockSpec(memory_space=pltpu.HBM)
ROWS_BY_ROWS = (((1,), (1,)), ((), ()))


def iota(shape, dim):
    return lax.broadcasted_iota(jnp.int32, shape, dim)


def in_hbm(a):
    return pltpu.with_memory_space_constraint(a, pltpu.HBM)


def in_vmem(a):
    return pltpu.with_memory_space_constraint(a, pltpu.VMEM)


def dot(a, b):
    return jnp.dot(a, b, preferred_element_type=jnp.float32)


def dot_rows(a, b):
    return lax.dot_general(a, b, ROWS_BY_ROWS, preferred_element_type=jnp.float32)


def pack_kernel(cand_hbm, ids_hbm, rows_hbm, states_hbm, out_ref, cand, ids, rows, states, stage, sem):
    copies = [
        pltpu.make_async_copy(src, dst, sem.at[i])
        for i, (src, dst) in enumerate(
            ((cand_hbm, cand), (ids_hbm, ids), (rows_hbm, rows), (states_hbm, states))
        )
    ]
    for copy in copies:
        copy.start()
    for copy in copies:
        copy.wait()
    width = rows.shape[2]
    cap_len, model_width = states.shape[1:]
    pieces = -(-model_width // width)
    held = pieces * cap_len
    values = states[0].astype(jnp.float32)
    for c in range(pieces - 1):
        stage[c * cap_len : (c + 1) * cap_len, :] = values[:, c * width : (c + 1) * width]
    rest = model_width - (pieces - 1) * width
    last = held - cap_len
    stage[last:held, 0:rest] = values[:, model_width - rest :]
    token, lane = iota((cap_len, width - rest), 0), iota((cap_len, width - rest), 1)
    digits = jnp.zeros_like(token)
    for t in range(cap_len):
        digits = jnp.where(token == t, jnp.where(lane == 0, ids[0, t] // DIGIT, ids[0, t] % DIGIT), digits)
    digits = jnp.where(lane < 2, digits, 0)
    for k in range(cand.shape[1]):
        digits = jnp.where(lane == 2 + 2 * k, cand[0, k] // DIGIT, digits)
        digits = jnp.where(lane == 3 + 2 * k, cand[0, k] % DIGIT, digits)
    stage[last:held, rest:] = digits.astype(jnp.float32)
    out_ref[0:held, :] = stage[...].astype(jnp.bfloat16)
    out_ref[held:, :] = rows[0]


def length_kernel(pos_ref, len_ref, *refs):
    length_ref = refs[-1]
    length_ref[...] = jnp.full(length_ref.shape, len_ref[0].astype(jnp.float32))


def cuts(total, parts):
    piece = -(-total // parts // 16) * 16
    return [(i, min(total, i + piece)) for i in range(0, total, piece)]


def collect_kernel(*refs):
    *msgs, out_ref = refs
    held = out_ref.shape[0] // len(msgs)
    for i, msg in enumerate(msgs):
        out_ref[i * held : (i + 1) * held, :] = msg[0:held, :]


def keys_kernel(blocks, *refs):
    msgs, (weight, bias, keys, rows) = refs[:blocks], refs[blocks:]
    prefix = rows.shape[0] // blocks
    for j, msg in enumerate(msgs):
        rows[j * prefix : (j + 1) * prefix, :] = msg[msg.shape[0] - prefix :, :]
    step = 512
    bias = bias[...].astype(jnp.float32).reshape(1, keys.shape[1])
    for i in range(0, keys.shape[1], step):
        summed = dot(rows[...], weight[:, i : i + step])
        keys[:, i : i + step] = (summed + bias[:, i : i + step]).astype(jnp.bfloat16)


def hidden_kernel(order, prefix, cap_len, *refs):
    pos_ref, *cap_refs = refs[:5]
    keys, gain_ref, out_ref, caps, query, mixed, bias, scores, weights = refs[5:]
    blocks = len(order)
    width = caps.shape[1]
    model_width = mixed.shape[1]
    row_total = query.shape[0]
    held, pair_rows = caps.shape[0] // (2 * blocks), row_total // blocks
    pieces = -(-model_width // width)

    start = 0
    for ref in cap_refs:
        caps[start : start + ref.shape[0], :] = ref[...]
        start += ref.shape[0]
    rest = model_width - (pieces - 1) * width
    last = (pieces - 2) * cap_len
    row, lane = iota((pair_rows, LANES), 0), iota((pair_rows, LANES), 1)
    place = 2 + 2 * (row // cap_len)
    factor = jnp.where(lane == place, float(DIGIT), jnp.where(lane == place + 1, 1.0, 0.0))
    found = []
    for s in range(blocks):
        digits = caps[s * held + last : s * held + last + pair_rows, rest : rest + LANES].astype(jnp.float32)
        digits = jnp.where(row < cap_len, pltpu.roll(digits, cap_len, 0), digits)
        found.append(jnp.sum(digits * factor, 1, keepdims=True))
    found = jnp.concatenate(found, 0)
    away = found.astype(jnp.int32) ^ pos_ref[0]
    block = (away & 1) * blocks
    for s, distance in enumerate(order):
        block += jnp.where(away - (away & 1) == distance, s, 0)
    first = block * held + iota((row_total, 1), 0) % cap_len
    column = iota((row_total, 2 * blocks * held), 1)
    pick = jnp.concatenate(
        [jnp.where(column == first + c * cap_len, 1.0, 0.0).astype(jnp.bfloat16) for c in range(pieces)], 0
    )
    picked = dot(pick, caps[...]).astype(jnp.bfloat16)
    for c in range(pieces):
        part = min(width, query.shape[1] - c * width)
        query[:, c * width : c * width + part] = picked[c * row_total : (c + 1) * row_total, 0:part]

    heads = TILE // HEAD_DIM
    group_rows = bias.shape[0] // heads
    image_keys = bias.shape[1] - group_rows
    lane = iota((group_rows, TILE), 1) // HEAD_DIM
    r, k = iota(bias.shape, 0) % group_rows, iota(bias.shape, 1)
    own = k - image_keys
    allowed = ((k < image_keys) & (k // prefix == r // pair_rows)) | (
        (own >= 0) & (own <= r) & (own // cap_len == r // cap_len)
    )
    bias[...] = jnp.where(allowed, 0.0, -1e30)
    tiles = [
        (g, slice(i * TILE, (i + 1) * TILE))
        for i in range(model_width // TILE)
        for g in range(row_total // group_rows)
    ]

    def keys_of(g, cols):
        q = query[g * group_rows : (g + 1) * group_rows, cols]
        return q, jnp.concatenate([keys[g * image_keys : (g + 1) * image_keys, cols], q], 0)

    for n, (g, cols) in enumerate(tiles):
        q, key = keys_of(g, cols)
        scaled, zero = q * score_scale, jnp.zeros_like(q)
        every = jnp.concatenate([jnp.where(lane == h, scaled, zero) for h in range(heads)], 0)
        scores[n] = dot_rows(every, key)
    for n in range(len(tiles)):
        score = scores[n] + bias[...]
        expo = jnp.exp(score - jnp.max(score, 1, keepdims=True))
        weights[n] = (expo * (1.0 / jnp.sum(expo, 1, keepdims=True))).astype(jnp.bfloat16)
    squares = [jnp.zeros((group_rows, TILE), jnp.float32) for _ in range(row_total // group_rows)]
    for n, (g, cols) in enumerate(tiles):
        q, key = keys_of(g, cols)
        out = dot(weights[n], key)
        value = q.astype(jnp.float32)
        for h in range(heads):
            value += jnp.where(lane == h, out[h * group_rows : (h + 1) * group_rows], 0.0)
        mixed[g * group_rows : (g + 1) * group_rows, cols] = value
        squares[g] += value * value
    square = jnp.concatenate(squares, 0)
    scale = lax.rsqrt(jnp.sum(square, 1, keepdims=True) / model_width + eps)
    out_ref[:, 0:model_width] = (mixed[...] * scale * gain_ref[...]).astype(jnp.bfloat16)
    marks = query[:, model_width:]
    out_ref[:, model_width:] = jnp.where(iota(marks.shape, 1) == 2, found.astype(jnp.bfloat16), marks)


def logits_kernel(order, pos_ref, mine_ref, other_ref, head_ref, length_ref, out_ref, states):
    half = mine_ref.shape[0]
    model_width = states.shape[1]
    row_total = 2 * half
    states[0:half, :] = mine_ref[:, 0:model_width]
    states[half:, :] = other_ref[:, 0:model_width]
    digits = jnp.concatenate(
        [ref[:, model_width:].astype(jnp.float32) for ref in (mine_ref, other_ref)], 0
    ).T
    vocab = head_ref.shape[0]
    ids = (digits[0:1] * DIGIT + digits[1:2]).astype(jnp.int32) - pos_ref[0] * vocab
    tops, totals, targets = [], [], []
    for i, j in cuts(vocab, -(-vocab // TILE)):
        values = dot_rows(head_ref[i:j, :], states[...])
        top = jnp.max(values, 0, keepdims=True)
        tops.append(top)
        totals.append(jnp.sum(jnp.exp(values - top), 0, keepdims=True))
        hit = iota(values.shape, 0) == ids - i
        targets.append(jnp.sum(jnp.where(hit, values, 0.0), 0, keepdims=True))
    top = functools.reduce(jnp.maximum, tops)
    total = sum(t * jnp.exp(m - top) for t, m in zip(totals, tops))
    shards, _, width = out_ref.shape
    rows = row_total // shards
    field = iota((SUBLANES, width), 1) // rows
    halves = []
    for start in range(0, shards, SUBLANES):
        half = jnp.zeros((SUBLANES, width), jnp.float32)
        for s, values in enumerate((top, total, sum(targets), length_ref[...])):
            shift = (s + 1 + start) * rows % width
            spread = jnp.broadcast_to(pltpu.roll(values, shift, 1) if shift else values, half.shape)
            half = jnp.where(field == s, pltpu.roll(spread, 0, 1, stride=rows, stride_axis=0), half)
        halves.append(half)
    packed = jnp.concatenate(halves, 0)
    for j in range(shards):
        away = order[j % len(order)] + j // len(order)
        out_ref[pos_ref[0] ^ away] = packed[shards - 1 - j : shards - j]


def finish_kernel(stats_ref, mine_ref, out_ref):
    shards, _, width = stats_ref.shape
    _, top_count, cap_len = out_ref.shape
    rows = top_count * cap_len
    tops = jnp.concatenate([stats_ref[e] for e in range(shards)], 0)
    totals, targets, lengths = (pltpu.roll(tops, width - s * rows, 1) for s in (1, 2, 3))
    marks = mine_ref[0:16, mine_ref.shape[1] - width :].astype(jnp.float32)
    cand = jnp.where(iota(marks.shape, 0) == iota(marks.shape, 1), marks[:, 2:3], 0.0)
    cand = jnp.sum(cand, 0, keepdims=True).astype(jnp.int32)
    length = jnp.sum(jnp.where(iota(tops.shape, 0) == cand, lengths, 0.0), 0, keepdims=True)
    top = jnp.max(tops, 0, keepdims=True)
    total = jnp.sum(totals * jnp.exp(tops - top), 0, keepdims=True)
    loglik = jnp.sum(targets, 0, keepdims=True) - (top + jnp.log(total))
    token = (iota(loglik.shape, 1) % cap_len).astype(jnp.float32)
    loglik = jnp.where(token < length, loglik, 0.0)
    for k in range(top_count):
        out_ref[0, k : k + 1, :] = loglik[:, k * cap_len : (k + 1) * cap_len]


def paired(
    query_rows, proj_weight, proj_bias, candidates, caption_states, caption_ids, caption_lengths, norm_gain, head_weight
):
    shards = lax.axis_size("dp")
    blocks = shards // 2
    _, prefix, width = query_rows.shape
    _, cap_len, model_width = caption_states.shape
    top_count = candidates.shape[1]
    pair_rows = top_count * cap_len
    piece_rows = cap_len * -(-model_width // width)
    held = -(-piece_rows // 16) * 16
    row_total = blocks * pair_rows
    position = lax.axis_index("dp").astype(jnp.int32).reshape(1)
    heads, group = TILE // HEAD_DIM, LANES // prefix
    score_tiles = model_width // TILE * blocks // group

    def swap(a, away):
        return lax.ppermute(a, "dp", [(i, i ^ away) for i in range(shards)])

    message = pl.pallas_call(
        pack_kernel,
        out_shape=jax.ShapeDtypeStruct((piece_rows + prefix, width), jnp.bfloat16),
        in_specs=[HBM] * 4,
        out_specs=VMEM,
        scratch_shapes=[
            pltpu.SMEM(candidates.shape, jnp.int32),
            pltpu.SMEM(caption_ids.shape, jnp.int32),
            pltpu.VMEM(query_rows.shape, jnp.bfloat16),
            pltpu.VMEM(caption_states.shape, jnp.bfloat16),
            pltpu.VMEM((piece_rows, width), jnp.float32),
            pltpu.SemaphoreType.DMA((4,)),
        ],
        compiler_params=pltpu.CompilerParams(vmem_limit_bytes=2 * MIB),
        name="pack",
    )(*(in_hbm(a) for a in (candidates, caption_ids, query_rows, caption_states)))

    got = {0: message}
    for away in (12, 8, 4, 2):
        got[away] = swap(message, away)
    length = pl.pallas_call(
        length_kernel,
        out_shape=jax.ShapeDtypeStruct((1, LANES), jnp.float32),
        in_specs=[SMEM, SMEM] + [HBM] * 3,
        out_specs=VMEM,
        compiler_params=pltpu.CompilerParams(vmem_limit_bytes=MIB),
        name="length",
    )(position, caption_lengths, in_hbm(head_weight.T), in_hbm(head_weight.T), in_hbm(proj_weight))
    got[6] = swap(got[4], 2)
    got[14] = swap(got[12], 2)
    got[8], got[2], got[6], length = lax.optimization_barrier((got[8], got[2], got[6], length))
    got[10] = swap(got[8], 2)
    order = (0, 2, 4, 6, 8, 12, 10, 14)
    mine = [got[away] for away in order]

    def collect(msgs):
        return pl.pallas_call(
            collect_kernel,
            out_shape=jax.ShapeDtypeStruct((len(msgs) * held, width), jnp.bfloat16),
            in_specs=[VMEM] * len(msgs),
            out_specs=VMEM,
            compiler_params=pltpu.CompilerParams(vmem_limit_bytes=2 * MIB),
            name="collect",
        )(*msgs)

    near, far = collect(mine[: blocks // 2]), collect(mine[blocks // 2 :])
    other_near, other_far = swap(near, 1), swap(far, 1)

    keys = pl.pallas_call(
        functools.partial(keys_kernel, blocks),
        out_shape=pltpu.VMEM((blocks * prefix, model_width), jnp.bfloat16),
        in_specs=[VMEM] * (blocks + 2),
        out_specs=VMEM,
        scratch_shapes=[pltpu.VMEM((blocks * prefix, width), jnp.bfloat16)],
        compiler_params=pltpu.CompilerParams(vmem_limit_bytes=8 * MIB),
        cost_estimate=pl.CostEstimate(
            flops=2 * blocks * prefix * width * model_width, bytes_accessed=4 * width * model_width, transcendentals=0
        ),
        name="keys",
    )(*mine, in_vmem(proj_weight), in_vmem(proj_bias))

    hidden = pl.pallas_call(
        functools.partial(hidden_kernel, order, prefix, cap_len),
        out_shape=jax.ShapeDtypeStruct((row_total, model_width + LANES), jnp.bfloat16),
        in_specs=[SMEM] + [VMEM] * 6,
        out_specs=VMEM,
        scratch_shapes=[
            pltpu.VMEM((2 * blocks * held, width), jnp.bfloat16),
            pltpu.VMEM((row_total, model_width + LANES), jnp.bfloat16),
            pltpu.VMEM((row_total, model_width), jnp.float32),
            pltpu.VMEM((heads * group * pair_rows, group * (prefix + pair_rows)), jnp.float32),
            pltpu.VMEM((score_tiles, heads * group * pair_rows, group * (prefix + pair_rows)), jnp.float32),
            pltpu.VMEM((score_tiles, heads * group * pair_rows, group * (prefix + pair_rows)), jnp.bfloat16),
        ],
        compiler_params=pltpu.CompilerParams(vmem_limit_bytes=16 * MIB),
        name="hidden",
    )(position, near, far, other_near, other_far, keys, in_vmem(norm_gain.reshape(1, -1)))

    stats = pl.pallas_call(
        functools.partial(logits_kernel, order),
        out_shape=jax.ShapeDtypeStruct((shards, 1, LANES), jnp.float32),
        in_specs=[SMEM] + [VMEM] * 4,
        out_specs=VMEM,
        scratch_shapes=[pltpu.VMEM((2 * row_total, model_width), jnp.bfloat16)],
        compiler_params=pltpu.CompilerParams(vmem_limit_bytes=16 * MIB),
        name="logits",
    )(position, hidden, swap(hidden, 1), in_vmem(head_weight.T), length)

    stats = lax.all_to_all(stats, "dp", 0, 0, tiled=True)
    return pl.pallas_call(
        finish_kernel,
        out_shape=jax.ShapeDtypeStruct((1, top_count, cap_len), jnp.float32),
        in_specs=[VMEM, VMEM],
        out_specs=VMEM,
        compiler_params=pltpu.CompilerParams(vmem_limit_bytes=2 * MIB),
        name="finish",
    )(stats, hidden)


def merged(part, axis, combine):
    gathered = jax.tree.map(lambda a: lax.all_gather(a, axis), part)

    def take(source):
        return jax.tree.map(lambda a: lax.dynamic_index_in_dim(a, source, 0, False), gathered)

    return lax.fori_loop(
        1, lax.axis_size(axis), lambda source, state: combine(state, take(source)), take(0)
    )


def project(rows, proj_weight, proj_bias):
    row_total, prefix_len, query_width = rows.shape
    summed = jnp.dot(
        rows.reshape(row_total * prefix_len, query_width),
        proj_weight,
        preferred_element_type=jnp.float32,
    )
    projected = (summed + proj_bias.astype(jnp.float32)).astype(jnp.bfloat16)
    return projected.reshape(row_total, prefix_len, proj_weight.shape[1])


def attend(projected, states, norm_gain):
    prefix_len = projected.shape[0]
    cap_len, model_width = states.shape
    heads = model_width // HEAD_DIM
    keys = jnp.concatenate([projected, states], 0)
    query = states.reshape(cap_len, heads, HEAD_DIM)
    keyed = keys.reshape(prefix_len + cap_len, heads, HEAD_DIM)
    scores = (
        jnp.einsum("thd,jhd->htj", query, keyed, preferred_element_type=jnp.float32) * score_scale
    )
    key_pos = jnp.arange(prefix_len + cap_len)[None, :]
    tok_pos = jnp.arange(cap_len)[:, None]
    allowed = (key_pos < prefix_len) | (key_pos - prefix_len <= tok_pos)
    scores = jnp.where(allowed[None], scores, -jnp.inf)
    row_max = jnp.max(scores, -1, keepdims=True)
    expo = jnp.exp(scores - row_max)
    weights = (expo / jnp.sum(expo, -1, keepdims=True)).astype(jnp.bfloat16)
    mixed_out = jnp.einsum(
        "htj,jhd->thd", weights, keyed, preferred_element_type=jnp.float32
    ).reshape(cap_len, model_width)
    mixed = states.astype(jnp.float32) + mixed_out
    normed = mixed * lax.rsqrt(jnp.mean(mixed * mixed, -1, keepdims=True) + eps) * norm_gain
    return normed.astype(jnp.bfloat16)


def merge_totals(first, second):
    larger = jnp.maximum(first[0], second[0])
    summed = first[1] * jnp.exp(first[0] - larger) + second[1] * jnp.exp(second[0] - larger)
    return (larger, summed, first[2] + second[2])


def spread(
    query_rows,
    proj_weight,
    proj_bias,
    candidates,
    caption_states,
    caption_ids,
    caption_lengths,
    norm_gain,
    head_weight,
):
    position = lax.axis_index("dp")
    img_local, top_count = candidates.shape
    pair_count = img_local * top_count
    cap_local, cap_len, model_width = caption_states.shape
    own_cand = candidates.reshape(pair_count)
    all_cand, all_len = (
        lax.all_gather(candidates, "dp", axis=0, tiled=True),
        lax.all_gather(caption_lengths, "dp", axis=0, tiled=True),
    )
    caption_total = all_len.shape[0]
    length_match = own_cand[:, None] == jnp.arange(caption_total)[None, :]
    pair_len = jnp.sum(jnp.where(length_match, all_len[None, :], 0), 1)
    piece_states = lax.all_gather(caption_states, "dp", axis=0, tiled=True)
    piece_ids = lax.all_gather(caption_ids, "dp", axis=0, tiled=True)
    piece_rows = piece_states.shape[0]
    matches = own_cand[:, None] == jnp.arange(piece_rows)[None, :]
    picked = jnp.dot(
        matches.astype(jnp.bfloat16),
        piece_states.reshape(piece_rows, cap_len * model_width),
        preferred_element_type=jnp.float32,
    )
    fetched_ids = jnp.sum(jnp.where(matches[:, :, None], piece_ids[None, :, :], 0), 1).astype(
        jnp.int32
    )
    pair_states = picked.astype(jnp.bfloat16).reshape(pair_count, cap_len, model_width)
    image_proj = project(query_rows, proj_weight, proj_bias)
    pair_proj = jnp.repeat(image_proj, top_count, axis=0)
    work_hidden = jax.vmap(lambda one, two: attend(one, two, norm_gain))(pair_proj, pair_states)
    row_base = (position * pair_count + jnp.arange(pair_count)) * cap_len
    row_count = work_hidden.shape[0] * cap_len
    hidden_rows = work_hidden.reshape(row_count, model_width)
    id_rows = fetched_ids.reshape(row_count)
    vocab_dev = head_weight.shape[1]
    vocab_start = position * vocab_dev
    every_state, every_id = (
        lax.all_gather(hidden_rows, "dp", axis=0, tiled=True),
        lax.all_gather(id_rows, "dp", axis=0, tiled=True),
    )
    logits = jnp.dot(every_state, head_weight, preferred_element_type=jnp.float32)
    local_max = jnp.max(logits, 1)
    local_sum = jnp.sum(jnp.exp(logits - local_max[:, None]), 1)
    target_hit = jnp.arange(vocab_dev)[None, :] == (every_id - vocab_start)[:, None]
    local_pick = jnp.sum(jnp.where(target_hit, logits, 0.0), 1)
    top_all, sum_all, picked_all = merged((local_max, local_sum, local_pick), "dp", merge_totals)
    row_index = row_base[:, None] + jnp.arange(cap_len)[None, :]
    own_top = jnp.take(top_all, row_index)
    own_sum = jnp.take(sum_all, row_index)
    own_picked = jnp.take(picked_all, row_index)
    loglik = own_picked - (own_top + jnp.log(own_sum))
    inside = jnp.arange(cap_len)[None, :] < pair_len[:, None]
    result = jnp.where(inside, loglik, jnp.float32(0.0))
    return result.reshape(img_local, top_count, cap_len)


def local(query_rows, proj_weight, proj_bias, candidates, caption_states, *rest):
    one_each = candidates.shape[0] == 1 and caption_states.shape[0] == 1
    fits = candidates.shape[1] == 2 and caption_states.shape[1] == 4 and query_rows.shape[1] == 32
    plan = paired if lax.axis_size("dp") == 16 and one_each and fits else spread
    return plan(query_rows, proj_weight, proj_bias, candidates, caption_states, *rest)


def solution(mesh):
    in_specs = (
        P(("groups", "dp"), None, None),
        P(),
        P(),
        P(("groups", "dp"), None),
        P(("groups", "dp"), None, None),
        P(("groups", "dp"), None),
        P(("groups", "dp")),
        P(),
        P(None, "dp"),
    )
    out_specs = P(("groups", "dp"), None, None)
    return jax.shard_map(local, mesh=mesh, in_specs=in_specs, out_specs=out_specs, check_vma=False)
```

```python
import functools

import jax
import jax.numpy as jnp
from jax import lax
from jax.experimental import pallas as pl
from jax.experimental.pallas import tpu as pltpu
from jax.sharding import PartitionSpec as P

HEAD_DIM = 64
LANES = 128
SUBLANES = 8
TILE = 256
DIGIT = 256
MIB = 1 << 20


score_scale = 0.015625
eps = 1e-06

VMEM = pl.BlockSpec(memory_space=pltpu.VMEM)
SMEM = pl.BlockSpec(memory_space=pltpu.SMEM)
HBM = pl.BlockSpec(memory_space=pltpu.HBM)
ROWS_BY_ROWS = (((1,), (1,)), ((), ()))


def iota(shape, dim):
    return lax.broadcasted_iota(jnp.int32, shape, dim)


def in_hbm(a):
    return pltpu.with_memory_space_constraint(a, pltpu.HBM)


def in_vmem(a):
    return pltpu.with_memory_space_constraint(a, pltpu.VMEM)


def dot(a, b):
    return jnp.dot(a, b, preferred_element_type=jnp.float32)


def dot_rows(a, b):
    return lax.dot_general(a, b, ROWS_BY_ROWS, preferred_element_type=jnp.float32)


def pack_kernel(cand_hbm, ids_hbm, rows_hbm, states_hbm, out_ref, cand, ids, rows, states, stage, sem):
    copies = [
        pltpu.make_async_copy(src, dst, sem.at[i])
        for i, (src, dst) in enumerate(
            ((cand_hbm, cand), (ids_hbm, ids), (rows_hbm, rows), (states_hbm, states))
        )
    ]
    for copy in copies:
        copy.start()
    for copy in copies:
        copy.wait()
    width = rows.shape[2]
    cap_len, model_width = states.shape[1:]
    pieces = -(-model_width // width)
    held = pieces * cap_len
    values = states[0].astype(jnp.float32)
    for c in range(pieces - 1):
        stage[c * cap_len : (c + 1) * cap_len, :] = values[:, c * width : (c + 1) * width]
    rest = model_width - (pieces - 1) * width
    last = held - cap_len
    stage[last:held, 0:rest] = values[:, model_width - rest :]
    token, lane = iota((cap_len, width - rest), 0), iota((cap_len, width - rest), 1)
    digits = jnp.zeros_like(token)
    for t in range(cap_len):
        digits = jnp.where(token == t, jnp.where(lane == 0, ids[0, t] // DIGIT, ids[0, t] % DIGIT), digits)
    digits = jnp.where(lane < 2, digits, 0)
    for k in range(cand.shape[1]):
        digits = jnp.where(lane == 2 + 2 * k, cand[0, k] // DIGIT, digits)
        digits = jnp.where(lane == 3 + 2 * k, cand[0, k] % DIGIT, digits)
    stage[last:held, rest:] = digits.astype(jnp.float32)
    out_ref[0:held, :] = stage[...].astype(jnp.bfloat16)
    out_ref[held:, :] = rows[0]


def length_kernel(pos_ref, len_ref, *refs):
    length_ref = refs[-1]
    length_ref[...] = jnp.full(length_ref.shape, len_ref[0].astype(jnp.float32))


def cuts(total, parts):
    piece = -(-total // parts // 16) * 16
    return [(i, min(total, i + piece)) for i in range(0, total, piece)]


def collect_kernel(*refs):
    *msgs, out_ref = refs
    held = out_ref.shape[0] // len(msgs)
    for i, msg in enumerate(msgs):
        out_ref[i * held : (i + 1) * held, :] = msg[0:held, :]


def keys_kernel(blocks, *refs):
    msgs, (weight, bias, keys, rows) = refs[:blocks], refs[blocks:]
    prefix = rows.shape[0] // blocks
    for j, msg in enumerate(msgs):
        rows[j * prefix : (j + 1) * prefix, :] = msg[msg.shape[0] - prefix :, :]
    step = 512
    bias = bias[...].astype(jnp.float32).reshape(1, keys.shape[1])
    for i in range(0, keys.shape[1], step):
        summed = dot(rows[...], weight[:, i : i + step])
        keys[:, i : i + step] = (summed + bias[:, i : i + step]).astype(jnp.bfloat16)


def hidden_kernel(order, prefix, cap_len, *refs):
    pos_ref, *cap_refs = refs[:5]
    keys, gain_ref, out_ref, caps, query, mixed, bias, scores, weights = refs[5:]
    blocks = len(order)
    width = caps.shape[1]
    model_width = mixed.shape[1]
    row_total = query.shape[0]
    held, pair_rows = caps.shape[0] // (2 * blocks), row_total // blocks
    pieces = -(-model_width // width)

    start = 0
    for ref in cap_refs:
        caps[start : start + ref.shape[0], :] = ref[...]
        start += ref.shape[0]
    rest = model_width - (pieces - 1) * width
    last = (pieces - 2) * cap_len
    row, lane = iota((pair_rows, LANES), 0), iota((pair_rows, LANES), 1)
    place = 2 + 2 * (row // cap_len)
    factor = jnp.where(lane == place, float(DIGIT), jnp.where(lane == place + 1, 1.0, 0.0))
    found = []
    for s in range(blocks):
        digits = caps[s * held + last : s * held + last + pair_rows, rest : rest + LANES].astype(jnp.float32)
        digits = jnp.where(row < cap_len, pltpu.roll(digits, cap_len, 0), digits)
        found.append(jnp.sum(digits * factor, 1, keepdims=True))
    found = jnp.concatenate(found, 0)
    away = found.astype(jnp.int32) ^ pos_ref[0]
    block = (away & 1) * blocks
    for s, distance in enumerate(order):
        block += jnp.where(away - (away & 1) == distance, s, 0)
    first = block * held + iota((row_total, 1), 0) % cap_len
    column = iota((row_total, 2 * blocks * held), 1)
    pick = jnp.concatenate(
        [jnp.where(column == first + c * cap_len, 1.0, 0.0).astype(jnp.bfloat16) for c in range(pieces)], 0
    )
    picked = dot(pick, caps[...]).astype(jnp.bfloat16)
    for c in range(pieces):
        part = min(width, query.shape[1] - c * width)
        query[:, c * width : c * width + part] = picked[c * row_total : (c + 1) * row_total, 0:part]

    heads = TILE // HEAD_DIM
    group_rows = bias.shape[0] // heads
    image_keys = bias.shape[1] - group_rows
    lane = iota((group_rows, TILE), 1) // HEAD_DIM
    r, k = iota(bias.shape, 0) % group_rows, iota(bias.shape, 1)
    own = k - image_keys
    allowed = ((k < image_keys) & (k // prefix == r // pair_rows)) | (
        (own >= 0) & (own <= r) & (own // cap_len == r // cap_len)
    )
    bias[...] = jnp.where(allowed, 0.0, -1e30)
    tiles = [
        (g, slice(i * TILE, (i + 1) * TILE))
        for i in range(model_width // TILE)
        for g in range(row_total // group_rows)
    ]

    def keys_of(g, cols):
        q = query[g * group_rows : (g + 1) * group_rows, cols]
        return q, jnp.concatenate([keys[g * image_keys : (g + 1) * image_keys, cols], q], 0)

    for n, (g, cols) in enumerate(tiles):
        q, key = keys_of(g, cols)
        scaled, zero = q * score_scale, jnp.zeros_like(q)
        every = jnp.concatenate([jnp.where(lane == h, scaled, zero) for h in range(heads)], 0)
        scores[n] = dot_rows(every, key)
    for n in range(len(tiles)):
        score = scores[n] + bias[...]
        expo = jnp.exp(score - jnp.max(score, 1, keepdims=True))
        weights[n] = (expo * (1.0 / jnp.sum(expo, 1, keepdims=True))).astype(jnp.bfloat16)
    squares = [jnp.zeros((group_rows, TILE), jnp.float32) for _ in range(row_total // group_rows)]
    for n, (g, cols) in enumerate(tiles):
        q, key = keys_of(g, cols)
        out = dot(weights[n], key)
        value = q.astype(jnp.float32)
        for h in range(heads):
            value += jnp.where(lane == h, out[h * group_rows : (h + 1) * group_rows], 0.0)
        mixed[g * group_rows : (g + 1) * group_rows, cols] = value
        squares[g] += value * value
    square = jnp.concatenate(squares, 0)
    scale = lax.rsqrt(jnp.sum(square, 1, keepdims=True) / model_width + eps)
    out_ref[:, 0:model_width] = (mixed[...] * scale * gain_ref[...]).astype(jnp.bfloat16)
    marks = query[:, model_width:]
    out_ref[:, model_width:] = jnp.where(iota(marks.shape, 1) == 2, found.astype(jnp.bfloat16), marks)


def logits_kernel(order, pos_ref, mine_ref, other_ref, head_ref, length_ref, out_ref, states):
    half = mine_ref.shape[0]
    model_width = states.shape[1]
    row_total = 2 * half
    states[0:half, :] = mine_ref[:, 0:model_width]
    states[half:, :] = other_ref[:, 0:model_width]
    digits = jnp.concatenate(
        [ref[:, model_width:].astype(jnp.float32) for ref in (mine_ref, other_ref)], 0
    ).T
    vocab = head_ref.shape[0]
    ids = (digits[0:1] * DIGIT + digits[1:2]).astype(jnp.int32) - pos_ref[0] * vocab
    tops, totals, targets = [], [], []
    for i, j in cuts(vocab, -(-vocab // TILE)):
        values = dot_rows(head_ref[i:j, :], states[...])
        top = jnp.max(values, 0, keepdims=True)
        tops.append(top)
        totals.append(jnp.sum(jnp.exp(values - top), 0, keepdims=True))
        hit = iota(values.shape, 0) == ids - i
        targets.append(jnp.sum(jnp.where(hit, values, 0.0), 0, keepdims=True))
    top = functools.reduce(jnp.maximum, tops)
    total = sum(t * jnp.exp(m - top) for t, m in zip(totals, tops))
    shards, _, width = out_ref.shape
    rows = row_total // shards
    field = iota((SUBLANES, width), 1) // rows
    halves = []
    for start in range(0, shards, SUBLANES):
        half = jnp.zeros((SUBLANES, width), jnp.float32)
        for s, values in enumerate((top, total, sum(targets), length_ref[...])):
            shift = (s + 1 + start) * rows % width
            spread = jnp.broadcast_to(pltpu.roll(values, shift, 1) if shift else values, half.shape)
            half = jnp.where(field == s, pltpu.roll(spread, 0, 1, stride=rows, stride_axis=0), half)
        halves.append(half)
    packed = jnp.concatenate(halves, 0)
    for j in range(shards):
        away = order[j % len(order)] + j // len(order)
        out_ref[pos_ref[0] ^ away] = packed[shards - 1 - j : shards - j]


def finish_kernel(stats_ref, mine_ref, out_ref):
    shards, _, width = stats_ref.shape
    _, top_count, cap_len = out_ref.shape
    rows = top_count * cap_len
    tops = jnp.concatenate([stats_ref[e] for e in range(shards)], 0)
    totals, targets, lengths = (pltpu.roll(tops, width - s * rows, 1) for s in (1, 2, 3))
    marks = mine_ref[0:16, mine_ref.shape[1] - width :].astype(jnp.float32)
    cand = jnp.where(iota(marks.shape, 0) == iota(marks.shape, 1), marks[:, 2:3], 0.0)
    cand = jnp.sum(cand, 0, keepdims=True).astype(jnp.int32)
    length = jnp.sum(jnp.where(iota(tops.shape, 0) == cand, lengths, 0.0), 0, keepdims=True)
    top = jnp.max(tops, 0, keepdims=True)
    total = jnp.sum(totals * jnp.exp(tops - top), 0, keepdims=True)
    loglik = jnp.sum(targets, 0, keepdims=True) - (top + jnp.log(total))
    token = (iota(loglik.shape, 1) % cap_len).astype(jnp.float32)
    loglik = jnp.where(token < length, loglik, 0.0)
    for k in range(top_count):
        out_ref[0, k : k + 1, :] = loglik[:, k * cap_len : (k + 1) * cap_len]


def paired(
    query_rows, proj_weight, proj_bias, candidates, caption_states, caption_ids, caption_lengths, norm_gain, head_weight
):
    shards = lax.axis_size("dp")
    blocks = shards // 2
    _, prefix, width = query_rows.shape
    _, cap_len, model_width = caption_states.shape
    top_count = candidates.shape[1]
    pair_rows = top_count * cap_len
    piece_rows = cap_len * -(-model_width // width)
    held = -(-piece_rows // 16) * 16
    row_total = blocks * pair_rows
    position = lax.axis_index("dp").astype(jnp.int32).reshape(1)
    heads, group = TILE // HEAD_DIM, LANES // prefix
    score_tiles = model_width // TILE * blocks // group

    def swap(a, away):
        return lax.ppermute(a, "dp", [(i, i ^ away) for i in range(shards)])

    message = pl.pallas_call(
        pack_kernel,
        out_shape=jax.ShapeDtypeStruct((piece_rows + prefix, width), jnp.bfloat16),
        in_specs=[HBM] * 4,
        out_specs=VMEM,
        scratch_shapes=[
            pltpu.SMEM(candidates.shape, jnp.int32),
            pltpu.SMEM(caption_ids.shape, jnp.int32),
            pltpu.VMEM(query_rows.shape, jnp.bfloat16),
            pltpu.VMEM(caption_states.shape, jnp.bfloat16),
            pltpu.VMEM((piece_rows, width), jnp.float32),
            pltpu.SemaphoreType.DMA((4,)),
        ],
        compiler_params=pltpu.CompilerParams(vmem_limit_bytes=2 * MIB),
        name="pack",
    )(*(in_hbm(a) for a in (candidates, caption_ids, query_rows, caption_states)))

    got = {0: message}
    for away in (12, 2, 4):
        got[away] = swap(message, away)
    length = pl.pallas_call(
        length_kernel,
        out_shape=jax.ShapeDtypeStruct((1, LANES), jnp.float32),
        in_specs=[SMEM, SMEM] + [HBM] * 3,
        out_specs=VMEM,
        compiler_params=pltpu.CompilerParams(vmem_limit_bytes=MIB),
        name="length",
    )(position, caption_lengths, in_hbm(head_weight.T), in_hbm(head_weight.T), in_hbm(proj_weight))
    got[10] = swap(message, 10)
    got[6] = swap(message, 6)
    got[12], length = lax.optimization_barrier((got[12], length))
    got[8], got[14] = swap(got[12], 4), swap(got[12], 2)
    order = (0, 2, 4, 12, 10, 6, 8, 14)
    mine = [got[away] for away in order]

    def collect(msgs):
        return pl.pallas_call(
            collect_kernel,
            out_shape=jax.ShapeDtypeStruct((len(msgs) * held, width), jnp.bfloat16),
            in_specs=[VMEM] * len(msgs),
            out_specs=VMEM,
            compiler_params=pltpu.CompilerParams(vmem_limit_bytes=2 * MIB),
            name="collect",
        )(*msgs)

    near, far = collect(mine[: blocks // 2]), collect(mine[blocks // 2 :])
    other_near, other_far = swap(near, 1), swap(far, 1)

    keys = pl.pallas_call(
        functools.partial(keys_kernel, blocks),
        out_shape=pltpu.VMEM((blocks * prefix, model_width), jnp.bfloat16),
        in_specs=[VMEM] * (blocks + 2),
        out_specs=VMEM,
        scratch_shapes=[pltpu.VMEM((blocks * prefix, width), jnp.bfloat16)],
        compiler_params=pltpu.CompilerParams(vmem_limit_bytes=8 * MIB),
        cost_estimate=pl.CostEstimate(
            flops=2 * blocks * prefix * width * model_width, bytes_accessed=4 * width * model_width, transcendentals=0
        ),
        name="keys",
    )(*mine, in_vmem(proj_weight), in_vmem(proj_bias))

    hidden = pl.pallas_call(
        functools.partial(hidden_kernel, order, prefix, cap_len),
        out_shape=jax.ShapeDtypeStruct((row_total, model_width + LANES), jnp.bfloat16),
        in_specs=[SMEM] + [VMEM] * 6,
        out_specs=VMEM,
        scratch_shapes=[
            pltpu.VMEM((2 * blocks * held, width), jnp.bfloat16),
            pltpu.VMEM((row_total, model_width + LANES), jnp.bfloat16),
            pltpu.VMEM((row_total, model_width), jnp.float32),
            pltpu.VMEM((heads * group * pair_rows, group * (prefix + pair_rows)), jnp.float32),
            pltpu.VMEM((score_tiles, heads * group * pair_rows, group * (prefix + pair_rows)), jnp.float32),
            pltpu.VMEM((score_tiles, heads * group * pair_rows, group * (prefix + pair_rows)), jnp.bfloat16),
        ],
        compiler_params=pltpu.CompilerParams(vmem_limit_bytes=16 * MIB),
        name="hidden",
    )(position, near, far, other_near, other_far, keys, in_vmem(norm_gain.reshape(1, -1)))

    stats = pl.pallas_call(
        functools.partial(logits_kernel, order),
        out_shape=jax.ShapeDtypeStruct((shards, 1, LANES), jnp.float32),
        in_specs=[SMEM] + [VMEM] * 4,
        out_specs=VMEM,
        scratch_shapes=[pltpu.VMEM((2 * row_total, model_width), jnp.bfloat16)],
        compiler_params=pltpu.CompilerParams(vmem_limit_bytes=16 * MIB),
        name="logits",
    )(position, hidden, swap(hidden, 1), in_vmem(head_weight.T), length)

    stats = lax.all_to_all(stats, "dp", 0, 0, tiled=True)
    return pl.pallas_call(
        finish_kernel,
        out_shape=jax.ShapeDtypeStruct((1, top_count, cap_len), jnp.float32),
        in_specs=[VMEM, VMEM],
        out_specs=VMEM,
        compiler_params=pltpu.CompilerParams(vmem_limit_bytes=2 * MIB),
        name="finish",
    )(stats, hidden)


def merged(part, axis, combine):
    gathered = jax.tree.map(lambda a: lax.all_gather(a, axis), part)

    def take(source):
        return jax.tree.map(lambda a: lax.dynamic_index_in_dim(a, source, 0, False), gathered)

    return lax.fori_loop(
        1, lax.axis_size(axis), lambda source, state: combine(state, take(source)), take(0)
    )


def project(rows, proj_weight, proj_bias):
    row_total, prefix_len, query_width = rows.shape
    summed = jnp.dot(
        rows.reshape(row_total * prefix_len, query_width),
        proj_weight,
        preferred_element_type=jnp.float32,
    )
    projected = (summed + proj_bias.astype(jnp.float32)).astype(jnp.bfloat16)
    return projected.reshape(row_total, prefix_len, proj_weight.shape[1])


def attend(projected, states, norm_gain):
    prefix_len = projected.shape[0]
    cap_len, model_width = states.shape
    heads = model_width // HEAD_DIM
    keys = jnp.concatenate([projected, states], 0)
    query = states.reshape(cap_len, heads, HEAD_DIM)
    keyed = keys.reshape(prefix_len + cap_len, heads, HEAD_DIM)
    scores = (
        jnp.einsum("thd,jhd->htj", query, keyed, preferred_element_type=jnp.float32) * score_scale
    )
    key_pos = jnp.arange(prefix_len + cap_len)[None, :]
    tok_pos = jnp.arange(cap_len)[:, None]
    allowed = (key_pos < prefix_len) | (key_pos - prefix_len <= tok_pos)
    scores = jnp.where(allowed[None], scores, -jnp.inf)
    row_max = jnp.max(scores, -1, keepdims=True)
    expo = jnp.exp(scores - row_max)
    weights = (expo / jnp.sum(expo, -1, keepdims=True)).astype(jnp.bfloat16)
    mixed_out = jnp.einsum(
        "htj,jhd->thd", weights, keyed, preferred_element_type=jnp.float32
    ).reshape(cap_len, model_width)
    mixed = states.astype(jnp.float32) + mixed_out
    normed = mixed * lax.rsqrt(jnp.mean(mixed * mixed, -1, keepdims=True) + eps) * norm_gain
    return normed.astype(jnp.bfloat16)


def merge_totals(first, second):
    larger = jnp.maximum(first[0], second[0])
    summed = first[1] * jnp.exp(first[0] - larger) + second[1] * jnp.exp(second[0] - larger)
    return (larger, summed, first[2] + second[2])


def spread(
    query_rows,
    proj_weight,
    proj_bias,
    candidates,
    caption_states,
    caption_ids,
    caption_lengths,
    norm_gain,
    head_weight,
):
    position = lax.axis_index("dp")
    img_local, top_count = candidates.shape
    pair_count = img_local * top_count
    cap_local, cap_len, model_width = caption_states.shape
    own_cand = candidates.reshape(pair_count)
    all_cand, all_len = (
        lax.all_gather(candidates, "dp", axis=0, tiled=True),
        lax.all_gather(caption_lengths, "dp", axis=0, tiled=True),
    )
    caption_total = all_len.shape[0]
    length_match = own_cand[:, None] == jnp.arange(caption_total)[None, :]
    pair_len = jnp.sum(jnp.where(length_match, all_len[None, :], 0), 1)
    piece_states = lax.all_gather(caption_states, "dp", axis=0, tiled=True)
    piece_ids = lax.all_gather(caption_ids, "dp", axis=0, tiled=True)
    piece_rows = piece_states.shape[0]
    matches = own_cand[:, None] == jnp.arange(piece_rows)[None, :]
    picked = jnp.dot(
        matches.astype(jnp.bfloat16),
        piece_states.reshape(piece_rows, cap_len * model_width),
        preferred_element_type=jnp.float32,
    )
    fetched_ids = jnp.sum(jnp.where(matches[:, :, None], piece_ids[None, :, :], 0), 1).astype(
        jnp.int32
    )
    pair_states = picked.astype(jnp.bfloat16).reshape(pair_count, cap_len, model_width)
    image_proj = project(query_rows, proj_weight, proj_bias)
    pair_proj = jnp.repeat(image_proj, top_count, axis=0)
    work_hidden = jax.vmap(lambda one, two: attend(one, two, norm_gain))(pair_proj, pair_states)
    row_base = (position * pair_count + jnp.arange(pair_count)) * cap_len
    row_count = work_hidden.shape[0] * cap_len
    hidden_rows = work_hidden.reshape(row_count, model_width)
    id_rows = fetched_ids.reshape(row_count)
    vocab_dev = head_weight.shape[1]
    vocab_start = position * vocab_dev
    every_state, every_id = (
        lax.all_gather(hidden_rows, "dp", axis=0, tiled=True),
        lax.all_gather(id_rows, "dp", axis=0, tiled=True),
    )
    logits = jnp.dot(every_state, head_weight, preferred_element_type=jnp.float32)
    local_max = jnp.max(logits, 1)
    local_sum = jnp.sum(jnp.exp(logits - local_max[:, None]), 1)
    target_hit = jnp.arange(vocab_dev)[None, :] == (every_id - vocab_start)[:, None]
    local_pick = jnp.sum(jnp.where(target_hit, logits, 0.0), 1)
    top_all, sum_all, picked_all = merged((local_max, local_sum, local_pick), "dp", merge_totals)
    row_index = row_base[:, None] + jnp.arange(cap_len)[None, :]
    own_top = jnp.take(top_all, row_index)
    own_sum = jnp.take(sum_all, row_index)
    own_picked = jnp.take(picked_all, row_index)
    loglik = own_picked - (own_top + jnp.log(own_sum))
    inside = jnp.arange(cap_len)[None, :] < pair_len[:, None]
    result = jnp.where(inside, loglik, jnp.float32(0.0))
    return result.reshape(img_local, top_count, cap_len)


def local(query_rows, proj_weight, proj_bias, candidates, caption_states, *rest):
    one_each = candidates.shape[0] == 1 and caption_states.shape[0] == 1
    fits = candidates.shape[1] == 2 and caption_states.shape[1] == 4 and query_rows.shape[1] == 32
    plan = paired if lax.axis_size("dp") == 16 and one_each and fits else spread
    return plan(query_rows, proj_weight, proj_bias, candidates, caption_states, *rest)


def solution(mesh):
    in_specs = (
        P(("groups", "dp"), None, None),
        P(),
        P(),
        P(("groups", "dp"), None),
        P(("groups", "dp"), None, None),
        P(("groups", "dp"), None),
        P(("groups", "dp")),
        P(),
        P(None, "dp"),
    )
    out_specs = P(("groups", "dp"), None, None)
    return jax.shard_map(local, mesh=mesh, in_specs=in_specs, out_specs=out_specs, check_vma=False)
```

```python
import functools

import jax
import jax.numpy as jnp
from jax import lax
from jax.experimental import pallas as pl
from jax.experimental.pallas import tpu as pltpu
from jax.sharding import PartitionSpec as P

HEAD_DIM = 64
LANES = 128
SUBLANES = 8
TILE = 256
DIGIT = 256
MIB = 1 << 20


score_scale = 0.015625
eps = 1e-06

VMEM = pl.BlockSpec(memory_space=pltpu.VMEM)
SMEM = pl.BlockSpec(memory_space=pltpu.SMEM)
HBM = pl.BlockSpec(memory_space=pltpu.HBM)
ANY = pl.BlockSpec(memory_space=pl.ANY)
ROWS_BY_ROWS = (((1,), (1,)), ((), ()))


def iota(shape, dim):
    return lax.broadcasted_iota(jnp.int32, shape, dim)


def in_hbm(a):
    return pltpu.with_memory_space_constraint(a, pltpu.HBM)


def in_vmem(a):
    return pltpu.with_memory_space_constraint(a, pltpu.VMEM)


def dot(a, b):
    return jnp.dot(a, b, preferred_element_type=jnp.float32)


def dot_rows(a, b):
    return lax.dot_general(a, b, ROWS_BY_ROWS, preferred_element_type=jnp.float32)


def pack_kernel(cand_hbm, ids_hbm, rows_hbm, states_hbm, out_ref, cand, ids, rows, states, stage, sem):
    copies = [
        pltpu.make_async_copy(src, dst, sem.at[i])
        for i, (src, dst) in enumerate(
            ((cand_hbm, cand), (ids_hbm, ids), (rows_hbm, rows), (states_hbm, states))
        )
    ]
    for copy in copies:
        copy.start()
    for copy in copies:
        copy.wait()
    width = rows.shape[2]
    cap_len, model_width = states.shape[1:]
    pieces = -(-model_width // width)
    held = pieces * cap_len
    values = states[0].astype(jnp.float32)
    for c in range(pieces - 1):
        stage[c * cap_len : (c + 1) * cap_len, :] = values[:, c * width : (c + 1) * width]
    rest = model_width - (pieces - 1) * width
    last = held - cap_len
    stage[last:held, 0:rest] = values[:, model_width - rest :]
    token, lane = iota((cap_len, width - rest), 0), iota((cap_len, width - rest), 1)
    digits = jnp.zeros_like(token)
    for t in range(cap_len):
        digits = jnp.where(token == t, jnp.where(lane == 0, ids[0, t] // DIGIT, ids[0, t] % DIGIT), digits)
    digits = jnp.where(lane < 2, digits, 0)
    for k in range(cand.shape[1]):
        digits = jnp.where(lane == 2 + 2 * k, cand[0, k] // DIGIT, digits)
        digits = jnp.where(lane == 3 + 2 * k, cand[0, k] % DIGIT, digits)
    stage[last:held, rest:] = digits.astype(jnp.float32)
    out_ref[0:held, :] = stage[...].astype(jnp.bfloat16)
    out_ref[held:, :] = rows[0]


def length_kernel(pos_ref, len_ref, *refs):
    length_ref = refs[-1]
    length_ref[...] = jnp.full(length_ref.shape, len_ref[0].astype(jnp.float32))


def cuts(total, parts):
    piece = -(-total // parts // 16) * 16
    return [(i, min(total, i + piece)) for i in range(0, total, piece)]


def collect_kernel(count, *refs):
    msgs, out_ref = refs[:count], refs[-1]
    held = out_ref.shape[0] // count
    for i, msg in enumerate(msgs):
        out_ref[i * held : (i + 1) * held, :] = msg[0:held, :]


def keys_kernel(blocks, *refs):
    msgs, (weight, bias, keys, rows) = refs[:blocks], refs[blocks:]
    prefix = rows.shape[0] // blocks
    for j, msg in enumerate(msgs):
        rows[j * prefix : (j + 1) * prefix, :] = msg[msg.shape[0] - prefix :, :]
    step = 512
    bias = bias[...].astype(jnp.float32).reshape(1, keys.shape[1])
    for i in range(0, keys.shape[1], step):
        summed = dot(rows[...], weight[:, i : i + step])
        keys[:, i : i + step] = (summed + bias[:, i : i + step]).astype(jnp.bfloat16)


def hidden_kernel(order, prefix, cap_len, *refs):
    pos_ref, *cap_refs = refs[:5]
    near_keys, far_keys, gain_ref, out_ref, caps, query, mixed, bias, scores, weights = refs[5:]
    blocks = len(order)
    width = caps.shape[1]
    model_width = mixed.shape[1]
    row_total = query.shape[0]
    held, pair_rows = caps.shape[0] // (2 * blocks), row_total // blocks
    pieces = -(-model_width // width)

    start = 0
    for ref in cap_refs:
        caps[start : start + ref.shape[0], :] = ref[...]
        start += ref.shape[0]
    rest = model_width - (pieces - 1) * width
    last = (pieces - 2) * cap_len
    row, lane = iota((pair_rows, LANES), 0), iota((pair_rows, LANES), 1)
    place = 2 + 2 * (row // cap_len)
    factor = jnp.where(lane == place, float(DIGIT), jnp.where(lane == place + 1, 1.0, 0.0))
    found = []
    for s in range(blocks):
        digits = caps[s * held + last : s * held + last + pair_rows, rest : rest + LANES].astype(jnp.float32)
        digits = jnp.where(row < cap_len, pltpu.roll(digits, cap_len, 0), digits)
        found.append(jnp.sum(digits * factor, 1, keepdims=True))
    found = jnp.concatenate(found, 0)
    away = found.astype(jnp.int32) ^ pos_ref[0]
    block = (away & 1) * blocks
    for s, distance in enumerate(order):
        block += jnp.where(away - (away & 1) == distance, s, 0)
    first = block * held + iota((row_total, 1), 0) % cap_len
    column = iota((row_total, 2 * blocks * held), 1)
    pick = jnp.concatenate(
        [jnp.where(column == first + c * cap_len, 1.0, 0.0).astype(jnp.bfloat16) for c in range(pieces)], 0
    )
    picked = dot(pick, caps[...]).astype(jnp.bfloat16)
    for c in range(pieces):
        part = min(width, query.shape[1] - c * width)
        query[:, c * width : c * width + part] = picked[c * row_total : (c + 1) * row_total, 0:part]

    heads = TILE // HEAD_DIM
    group_rows = bias.shape[0] // heads
    image_keys = bias.shape[1] - group_rows
    lane = iota((group_rows, TILE), 1) // HEAD_DIM
    r, k = iota(bias.shape, 0) % group_rows, iota(bias.shape, 1)
    own = k - image_keys
    allowed = ((k < image_keys) & (k // prefix == r // pair_rows)) | (
        (own >= 0) & (own <= r) & (own // cap_len == r // cap_len)
    )
    bias[...] = jnp.where(allowed, 0.0, -1e30)
    tiles = [
        (g, slice(i * TILE, (i + 1) * TILE))
        for i in range(model_width // TILE)
        for g in range(row_total // group_rows)
    ]

    def keys_of(g, cols):
        q = query[g * group_rows : (g + 1) * group_rows, cols]
        return q, jnp.concatenate([(near_keys, far_keys)[g][:, cols], q], 0)

    for n, (g, cols) in enumerate(tiles):
        q, key = keys_of(g, cols)
        scaled, zero = q * score_scale, jnp.zeros_like(q)
        every = jnp.concatenate([jnp.where(lane == h, scaled, zero) for h in range(heads)], 0)
        scores[n] = dot_rows(every, key)
    for n in range(len(tiles)):
        score = scores[n] + bias[...]
        expo = jnp.exp(score - jnp.max(score, 1, keepdims=True))
        weights[n] = (expo * (1.0 / jnp.sum(expo, 1, keepdims=True))).astype(jnp.bfloat16)
    squares = [jnp.zeros((group_rows, TILE), jnp.float32) for _ in range(row_total // group_rows)]
    for n, (g, cols) in enumerate(tiles):
        q, key = keys_of(g, cols)
        out = dot(weights[n], key)
        value = q.astype(jnp.float32)
        for h in range(heads):
            value += jnp.where(lane == h, out[h * group_rows : (h + 1) * group_rows], 0.0)
        mixed[g * group_rows : (g + 1) * group_rows, cols] = value
        squares[g] += value * value
    square = jnp.concatenate(squares, 0)
    scale = lax.rsqrt(jnp.sum(square, 1, keepdims=True) / model_width + eps)
    out_ref[:, 0:model_width] = (mixed[...] * scale * gain_ref[...]).astype(jnp.bfloat16)
    marks = query[:, model_width:]
    out_ref[:, model_width:] = jnp.where(iota(marks.shape, 1) == 2, found.astype(jnp.bfloat16), marks)


def logits_kernel(order, pos_ref, mine_ref, other_ref, head_ref, length_ref, out_ref, states):
    half = mine_ref.shape[0]
    model_width = states.shape[1]
    row_total = 2 * half
    states[0:half, :] = mine_ref[:, 0:model_width]
    states[half:, :] = other_ref[:, 0:model_width]
    digits = jnp.concatenate(
        [ref[:, model_width:].astype(jnp.float32) for ref in (mine_ref, other_ref)], 0
    ).T
    vocab = head_ref.shape[0]
    ids = (digits[0:1] * DIGIT + digits[1:2]).astype(jnp.int32) - pos_ref[0] * vocab
    tops, totals, targets = [], [], []
    for i, j in cuts(vocab, -(-vocab // TILE)):
        values = dot_rows(head_ref[i:j, :], states[...])
        top = jnp.max(values, 0, keepdims=True)
        tops.append(top)
        totals.append(jnp.sum(jnp.exp(values - top), 0, keepdims=True))
        hit = iota(values.shape, 0) == ids - i
        targets.append(jnp.sum(jnp.where(hit, values, 0.0), 0, keepdims=True))
    top = functools.reduce(jnp.maximum, tops)
    total = sum(t * jnp.exp(m - top) for t, m in zip(totals, tops))
    shards, _, width = out_ref.shape
    rows = row_total // shards
    field = iota((SUBLANES, width), 1) // rows
    halves = []
    for start in range(0, shards, SUBLANES):
        half = jnp.zeros((SUBLANES, width), jnp.float32)
        for s, values in enumerate((top, total, sum(targets), length_ref[...])):
            shift = (s + 1 + start) * rows % width
            spread = jnp.broadcast_to(pltpu.roll(values, shift, 1) if shift else values, half.shape)
            half = jnp.where(field == s, pltpu.roll(spread, 0, 1, stride=rows, stride_axis=0), half)
        halves.append(half)
    packed = jnp.concatenate(halves, 0)
    for j in range(shards):
        away = order[j % len(order)] + j // len(order)
        out_ref[pos_ref[0] ^ away] = packed[shards - 1 - j : shards - j]


def finish_kernel(stats_ref, mine_ref, out_ref):
    shards, _, width = stats_ref.shape
    _, top_count, cap_len = out_ref.shape
    rows = top_count * cap_len
    tops = jnp.concatenate([stats_ref[e] for e in range(shards)], 0)
    totals, targets, lengths = (pltpu.roll(tops, width - s * rows, 1) for s in (1, 2, 3))
    marks = mine_ref[0:16, mine_ref.shape[1] - width :].astype(jnp.float32)
    cand = jnp.where(iota(marks.shape, 0) == iota(marks.shape, 1), marks[:, 2:3], 0.0)
    cand = jnp.sum(cand, 0, keepdims=True).astype(jnp.int32)
    length = jnp.sum(jnp.where(iota(tops.shape, 0) == cand, lengths, 0.0), 0, keepdims=True)
    top = jnp.max(tops, 0, keepdims=True)
    total = jnp.sum(totals * jnp.exp(tops - top), 0, keepdims=True)
    loglik = jnp.sum(targets, 0, keepdims=True) - (top + jnp.log(total))
    token = (iota(loglik.shape, 1) % cap_len).astype(jnp.float32)
    loglik = jnp.where(token < length, loglik, 0.0)
    for k in range(top_count):
        out_ref[0, k : k + 1, :] = loglik[:, k * cap_len : (k + 1) * cap_len]


def paired(
    query_rows, proj_weight, proj_bias, candidates, caption_states, caption_ids, caption_lengths, norm_gain, head_weight
):
    shards = lax.axis_size("dp")
    blocks = shards // 2
    _, prefix, width = query_rows.shape
    _, cap_len, model_width = caption_states.shape
    top_count = candidates.shape[1]
    pair_rows = top_count * cap_len
    piece_rows = cap_len * -(-model_width // width)
    held = -(-piece_rows // 16) * 16
    row_total = blocks * pair_rows
    position = lax.axis_index("dp").astype(jnp.int32).reshape(1)
    heads, group = TILE // HEAD_DIM, LANES // prefix
    score_tiles = model_width // TILE * blocks // group

    def swap(a, away):
        return lax.ppermute(a, "dp", [(i, i ^ away) for i in range(shards)])

    message = pl.pallas_call(
        pack_kernel,
        out_shape=jax.ShapeDtypeStruct((piece_rows + prefix, width), jnp.bfloat16),
        in_specs=[HBM] * 4,
        out_specs=VMEM,
        scratch_shapes=[
            pltpu.SMEM(candidates.shape, jnp.int32),
            pltpu.SMEM(caption_ids.shape, jnp.int32),
            pltpu.VMEM(query_rows.shape, jnp.bfloat16),
            pltpu.VMEM(caption_states.shape, jnp.bfloat16),
            pltpu.VMEM((piece_rows, width), jnp.float32),
            pltpu.SemaphoreType.DMA((4,)),
        ],
        compiler_params=pltpu.CompilerParams(vmem_limit_bytes=2 * MIB),
        name="pack",
    )(*(in_hbm(a) for a in (candidates, caption_ids, query_rows, caption_states)))

    got = {0: message}
    for away in (12, 2, 4):
        got[away] = swap(message, away)
    length = pl.pallas_call(
        length_kernel,
        out_shape=jax.ShapeDtypeStruct((1, LANES), jnp.float32),
        in_specs=[SMEM, SMEM] + [HBM] * 3,
        out_specs=VMEM,
        compiler_params=pltpu.CompilerParams(vmem_limit_bytes=MIB),
        name="length",
    )(position, caption_lengths, in_hbm(head_weight.T), in_hbm(head_weight.T), in_hbm(proj_weight))
    got[10] = swap(message, 10)
    got[6] = swap(message, 6)
    got[12], length = lax.optimization_barrier((got[12], length))
    got[8], got[14] = swap(got[12], 4), swap(got[12], 2)
    order = (0, 2, 4, 12, 6, 10, 14, 8)
    mine = [got[away] for away in order]

    def collect(msgs, *after):
        return pl.pallas_call(
            functools.partial(collect_kernel, len(msgs)),
            out_shape=jax.ShapeDtypeStruct((len(msgs) * held, width), jnp.bfloat16),
            in_specs=[VMEM] * len(msgs) + [ANY] * len(after),
            out_specs=VMEM,
            compiler_params=pltpu.CompilerParams(vmem_limit_bytes=2 * MIB),
            name="collect",
        )(*msgs, *after)


    def keys_of(msgs):
        rows = len(msgs) * prefix
        return pl.pallas_call(
            functools.partial(keys_kernel, len(msgs)),
            out_shape=pltpu.VMEM((rows, model_width), jnp.bfloat16),
            in_specs=[VMEM] * (len(msgs) + 2),
            out_specs=VMEM,
            scratch_shapes=[pltpu.VMEM((rows, width), jnp.bfloat16)],
            compiler_params=pltpu.CompilerParams(vmem_limit_bytes=8 * MIB),
            cost_estimate=pl.CostEstimate(
                flops=2 * rows * width * model_width, bytes_accessed=4 * width * model_width, transcendentals=0
            ),
            name="keys",
        )(*msgs, in_vmem(proj_weight), in_vmem(proj_bias))

    near, near_keys = collect(mine[: blocks // 2]), keys_of(mine[: blocks // 2])
    far, far_keys = collect(mine[blocks // 2 :], near_keys), keys_of(mine[blocks // 2 :])
    other_near, other_far = swap(near, 1), swap(far, 1)

    hidden = pl.pallas_call(
        functools.partial(hidden_kernel, order, prefix, cap_len),
        out_shape=jax.ShapeDtypeStruct((row_total, model_width + LANES), jnp.bfloat16),
        in_specs=[SMEM] + [VMEM] * 7,
        out_specs=VMEM,
        scratch_shapes=[
            pltpu.VMEM((2 * blocks * held, width), jnp.bfloat16),
            pltpu.VMEM((row_total, model_width + LANES), jnp.bfloat16),
            pltpu.VMEM((row_total, model_width), jnp.float32),
            pltpu.VMEM((heads * group * pair_rows, group * (prefix + pair_rows)), jnp.float32),
            pltpu.VMEM((score_tiles, heads * group * pair_rows, group * (prefix + pair_rows)), jnp.float32),
            pltpu.VMEM((score_tiles, heads * group * pair_rows, group * (prefix + pair_rows)), jnp.bfloat16),
        ],
        compiler_params=pltpu.CompilerParams(vmem_limit_bytes=16 * MIB),
        name="hidden",
    )(position, near, far, other_near, other_far, near_keys, far_keys, in_vmem(norm_gain.reshape(1, -1)))

    stats = pl.pallas_call(
        functools.partial(logits_kernel, order),
        out_shape=jax.ShapeDtypeStruct((shards, 1, LANES), jnp.float32),
        in_specs=[SMEM] + [VMEM] * 4,
        out_specs=VMEM,
        scratch_shapes=[pltpu.VMEM((2 * row_total, model_width), jnp.bfloat16)],
        compiler_params=pltpu.CompilerParams(vmem_limit_bytes=16 * MIB),
        name="logits",
    )(position, hidden, swap(hidden, 1), in_vmem(head_weight.T), length)

    stats = lax.all_to_all(stats, "dp", 0, 0, tiled=True)
    return pl.pallas_call(
        finish_kernel,
        out_shape=jax.ShapeDtypeStruct((1, top_count, cap_len), jnp.float32),
        in_specs=[VMEM, VMEM],
        out_specs=VMEM,
        compiler_params=pltpu.CompilerParams(vmem_limit_bytes=2 * MIB),
        name="finish",
    )(stats, hidden)


def merged(part, axis, combine):
    gathered = jax.tree.map(lambda a: lax.all_gather(a, axis), part)

    def take(source):
        return jax.tree.map(lambda a: lax.dynamic_index_in_dim(a, source, 0, False), gathered)

    return lax.fori_loop(
        1, lax.axis_size(axis), lambda source, state: combine(state, take(source)), take(0)
    )


def project(rows, proj_weight, proj_bias):
    row_total, prefix_len, query_width = rows.shape
    summed = jnp.dot(
        rows.reshape(row_total * prefix_len, query_width),
        proj_weight,
        preferred_element_type=jnp.float32,
    )
    projected = (summed + proj_bias.astype(jnp.float32)).astype(jnp.bfloat16)
    return projected.reshape(row_total, prefix_len, proj_weight.shape[1])


def attend(projected, states, norm_gain):
    prefix_len = projected.shape[0]
    cap_len, model_width = states.shape
    heads = model_width // HEAD_DIM
    keys = jnp.concatenate([projected, states], 0)
    query = states.reshape(cap_len, heads, HEAD_DIM)
    keyed = keys.reshape(prefix_len + cap_len, heads, HEAD_DIM)
    scores = (
        jnp.einsum("thd,jhd->htj", query, keyed, preferred_element_type=jnp.float32) * score_scale
    )
    key_pos = jnp.arange(prefix_len + cap_len)[None, :]
    tok_pos = jnp.arange(cap_len)[:, None]
    allowed = (key_pos < prefix_len) | (key_pos - prefix_len <= tok_pos)
    scores = jnp.where(allowed[None], scores, -jnp.inf)
    row_max = jnp.max(scores, -1, keepdims=True)
    expo = jnp.exp(scores - row_max)
    weights = (expo / jnp.sum(expo, -1, keepdims=True)).astype(jnp.bfloat16)
    mixed_out = jnp.einsum(
        "htj,jhd->thd", weights, keyed, preferred_element_type=jnp.float32
    ).reshape(cap_len, model_width)
    mixed = states.astype(jnp.float32) + mixed_out
    normed = mixed * lax.rsqrt(jnp.mean(mixed * mixed, -1, keepdims=True) + eps) * norm_gain
    return normed.astype(jnp.bfloat16)


def merge_totals(first, second):
    larger = jnp.maximum(first[0], second[0])
    summed = first[1] * jnp.exp(first[0] - larger) + second[1] * jnp.exp(second[0] - larger)
    return (larger, summed, first[2] + second[2])


def spread(
    query_rows,
    proj_weight,
    proj_bias,
    candidates,
    caption_states,
    caption_ids,
    caption_lengths,
    norm_gain,
    head_weight,
):
    position = lax.axis_index("dp")
    img_local, top_count = candidates.shape
    pair_count = img_local * top_count
    cap_local, cap_len, model_width = caption_states.shape
    own_cand = candidates.reshape(pair_count)
    all_cand, all_len = (
        lax.all_gather(candidates, "dp", axis=0, tiled=True),
        lax.all_gather(caption_lengths, "dp", axis=0, tiled=True),
    )
    caption_total = all_len.shape[0]
    length_match = own_cand[:, None] == jnp.arange(caption_total)[None, :]
    pair_len = jnp.sum(jnp.where(length_match, all_len[None, :], 0), 1)
    piece_states = lax.all_gather(caption_states, "dp", axis=0, tiled=True)
    piece_ids = lax.all_gather(caption_ids, "dp", axis=0, tiled=True)
    piece_rows = piece_states.shape[0]
    matches = own_cand[:, None] == jnp.arange(piece_rows)[None, :]
    picked = jnp.dot(
        matches.astype(jnp.bfloat16),
        piece_states.reshape(piece_rows, cap_len * model_width),
        preferred_element_type=jnp.float32,
    )
    fetched_ids = jnp.sum(jnp.where(matches[:, :, None], piece_ids[None, :, :], 0), 1).astype(
        jnp.int32
    )
    pair_states = picked.astype(jnp.bfloat16).reshape(pair_count, cap_len, model_width)
    image_proj = project(query_rows, proj_weight, proj_bias)
    pair_proj = jnp.repeat(image_proj, top_count, axis=0)
    work_hidden = jax.vmap(lambda one, two: attend(one, two, norm_gain))(pair_proj, pair_states)
    row_base = (position * pair_count + jnp.arange(pair_count)) * cap_len
    row_count = work_hidden.shape[0] * cap_len
    hidden_rows = work_hidden.reshape(row_count, model_width)
    id_rows = fetched_ids.reshape(row_count)
    vocab_dev = head_weight.shape[1]
    vocab_start = position * vocab_dev
    every_state, every_id = (
        lax.all_gather(hidden_rows, "dp", axis=0, tiled=True),
        lax.all_gather(id_rows, "dp", axis=0, tiled=True),
    )
    logits = jnp.dot(every_state, head_weight, preferred_element_type=jnp.float32)
    local_max = jnp.max(logits, 1)
    local_sum = jnp.sum(jnp.exp(logits - local_max[:, None]), 1)
    target_hit = jnp.arange(vocab_dev)[None, :] == (every_id - vocab_start)[:, None]
    local_pick = jnp.sum(jnp.where(target_hit, logits, 0.0), 1)
    top_all, sum_all, picked_all = merged((local_max, local_sum, local_pick), "dp", merge_totals)
    row_index = row_base[:, None] + jnp.arange(cap_len)[None, :]
    own_top = jnp.take(top_all, row_index)
    own_sum = jnp.take(sum_all, row_index)
    own_picked = jnp.take(picked_all, row_index)
    loglik = own_picked - (own_top + jnp.log(own_sum))
    inside = jnp.arange(cap_len)[None, :] < pair_len[:, None]
    result = jnp.where(inside, loglik, jnp.float32(0.0))
    return result.reshape(img_local, top_count, cap_len)


def local(query_rows, proj_weight, proj_bias, candidates, caption_states, *rest):
    one_each = candidates.shape[0] == 1 and caption_states.shape[0] == 1
    fits = candidates.shape[1] == 2 and caption_states.shape[1] == 4 and query_rows.shape[1] == 32
    plan = paired if lax.axis_size("dp") == 16 and one_each and fits else spread
    return plan(query_rows, proj_weight, proj_bias, candidates, caption_states, *rest)


def solution(mesh):
    in_specs = (
        P(("groups", "dp"), None, None),
        P(),
        P(),
        P(("groups", "dp"), None),
        P(("groups", "dp"), None, None),
        P(("groups", "dp"), None),
        P(("groups", "dp")),
        P(),
        P(None, "dp"),
    )
    out_specs = P(("groups", "dp"), None, None)
    return jax.shard_map(local, mesh=mesh, in_specs=in_specs, out_specs=out_specs, check_vma=False)
```

```python
import functools

import jax
import jax.numpy as jnp
from jax import lax
from jax.experimental import pallas as pl
from jax.experimental.pallas import tpu as pltpu
from jax.sharding import PartitionSpec as P

HEAD_DIM = 64
LANES = 128
SUBLANES = 8
TILE = 256
DIGIT = 256
MIB = 1 << 20


score_scale = 0.015625
eps = 1e-06

VMEM = pl.BlockSpec(memory_space=pltpu.VMEM)
SMEM = pl.BlockSpec(memory_space=pltpu.SMEM)
HBM = pl.BlockSpec(memory_space=pltpu.HBM)
ANY = pl.BlockSpec(memory_space=pl.ANY)
ROWS_BY_ROWS = (((1,), (1,)), ((), ()))


def iota(shape, dim):
    return lax.broadcasted_iota(jnp.int32, shape, dim)


def in_hbm(a):
    return pltpu.with_memory_space_constraint(a, pltpu.HBM)


def in_vmem(a):
    return pltpu.with_memory_space_constraint(a, pltpu.VMEM)


def dot(a, b):
    return jnp.dot(a, b, preferred_element_type=jnp.float32)


def dot_rows(a, b):
    return lax.dot_general(a, b, ROWS_BY_ROWS, preferred_element_type=jnp.float32)


def pack_kernel(cand_hbm, ids_hbm, rows_hbm, states_hbm, out_ref, cand, ids, rows, states, stage, sem):
    copies = [
        pltpu.make_async_copy(src, dst, sem.at[i])
        for i, (src, dst) in enumerate(
            ((cand_hbm, cand), (ids_hbm, ids), (rows_hbm, rows), (states_hbm, states))
        )
    ]
    for copy in copies:
        copy.start()
    for copy in copies:
        copy.wait()
    width = rows.shape[2]
    cap_len, model_width = states.shape[1:]
    pieces = -(-model_width // width)
    held = pieces * cap_len
    values = states[0].astype(jnp.float32)
    for c in range(pieces - 1):
        stage[c * cap_len : (c + 1) * cap_len, :] = values[:, c * width : (c + 1) * width]
    rest = model_width - (pieces - 1) * width
    last = held - cap_len
    stage[last:held, 0:rest] = values[:, model_width - rest :]
    token, lane = iota((cap_len, width - rest), 0), iota((cap_len, width - rest), 1)
    digits = jnp.zeros_like(token)
    for t in range(cap_len):
        digits = jnp.where(token == t, jnp.where(lane == 0, ids[0, t] // DIGIT, ids[0, t] % DIGIT), digits)
    digits = jnp.where(lane < 2, digits, 0)
    for k in range(cand.shape[1]):
        digits = jnp.where(lane == 2 + 2 * k, cand[0, k] // DIGIT, digits)
        digits = jnp.where(lane == 3 + 2 * k, cand[0, k] % DIGIT, digits)
    stage[last:held, rest:] = digits.astype(jnp.float32)
    out_ref[0:held, :] = stage[...].astype(jnp.bfloat16)
    out_ref[held:, :] = rows[0]


def length_kernel(pos_ref, len_ref, *refs):
    length_ref = refs[-1]
    length_ref[...] = jnp.full(length_ref.shape, len_ref[0].astype(jnp.float32))


def cuts(total, parts):
    piece = -(-total // parts // 16) * 16
    return [(i, min(total, i + piece)) for i in range(0, total, piece)]


def collect_kernel(count, *refs):
    msgs, out_ref = refs[:count], refs[-1]
    held = out_ref.shape[0] // count
    for i, msg in enumerate(msgs):
        out_ref[i * held : (i + 1) * held, :] = msg[0:held, :]


def keys_kernel(blocks, *refs):
    msgs, (weight, bias, keys, rows) = refs[:blocks], refs[blocks:]
    prefix = rows.shape[0] // blocks
    for j, msg in enumerate(msgs):
        rows[j * prefix : (j + 1) * prefix, :] = msg[msg.shape[0] - prefix :, :]
    step = 512
    bias = bias[...].astype(jnp.float32).reshape(1, keys.shape[1])
    for i in range(0, keys.shape[1], step):
        summed = dot(rows[...], weight[:, i : i + step])
        keys[:, i : i + step] = (summed + bias[:, i : i + step]).astype(jnp.bfloat16)


def hidden_kernel(order, prefix, cap_len, *refs):
    pos_ref, *cap_refs = refs[:5]
    near_keys, far_keys, gain_ref, out_ref, caps, query, mixed, bias, scores, weights = refs[5:]
    blocks = len(order)
    width = caps.shape[1]
    model_width = mixed.shape[1]
    row_total = query.shape[0]
    held, pair_rows = caps.shape[0] // (2 * blocks), row_total // blocks
    pieces = -(-model_width // width)

    start = 0
    for ref in cap_refs:
        caps[start : start + ref.shape[0], :] = ref[...]
        start += ref.shape[0]
    rest = model_width - (pieces - 1) * width
    last = (pieces - 2) * cap_len
    row, lane = iota((pair_rows, LANES), 0), iota((pair_rows, LANES), 1)
    place = 2 + 2 * (row // cap_len)
    factor = jnp.where(lane == place, float(DIGIT), jnp.where(lane == place + 1, 1.0, 0.0))
    found = []
    for s in range(blocks):
        digits = caps[s * held + last : s * held + last + pair_rows, rest : rest + LANES].astype(jnp.float32)
        digits = jnp.where(row < cap_len, pltpu.roll(digits, cap_len, 0), digits)
        found.append(jnp.sum(digits * factor, 1, keepdims=True))
    found = jnp.concatenate(found, 0)
    away = found.astype(jnp.int32) ^ pos_ref[0]
    block = (away & 1) * blocks
    for s, distance in enumerate(order):
        block += jnp.where(away - (away & 1) == distance, s, 0)
    first = block * held + iota((row_total, 1), 0) % cap_len
    column = iota((row_total, 2 * blocks * held), 1)
    pick = jnp.concatenate(
        [jnp.where(column == first + c * cap_len, 1.0, 0.0).astype(jnp.bfloat16) for c in range(pieces)], 0
    )
    picked = dot(pick, caps[...]).astype(jnp.bfloat16)
    for c in range(pieces):
        part = min(width, query.shape[1] - c * width)
        query[:, c * width : c * width + part] = picked[c * row_total : (c + 1) * row_total, 0:part]

    heads = TILE // HEAD_DIM
    group_rows = bias.shape[0] // heads
    image_keys = bias.shape[1] - group_rows
    lane = iota((group_rows, TILE), 1) // HEAD_DIM
    r, k = iota(bias.shape, 0) % group_rows, iota(bias.shape, 1)
    own = k - image_keys
    allowed = ((k < image_keys) & (k // prefix == r // pair_rows)) | (
        (own >= 0) & (own <= r) & (own // cap_len == r // cap_len)
    )
    bias[...] = jnp.where(allowed, 0.0, -1e30)
    tiles = [
        (g, slice(i * TILE, (i + 1) * TILE))
        for i in range(model_width // TILE)
        for g in range(row_total // group_rows)
    ]

    def keys_of(g, cols):
        q = query[g * group_rows : (g + 1) * group_rows, cols]
        return q, jnp.concatenate([(near_keys, far_keys)[g][:, cols], q], 0)

    for n, (g, cols) in enumerate(tiles):
        q, key = keys_of(g, cols)
        scaled, zero = q * score_scale, jnp.zeros_like(q)
        every = jnp.concatenate([jnp.where(lane == h, scaled, zero) for h in range(heads)], 0)
        scores[n] = dot_rows(every, key)
    for n in range(len(tiles)):
        score = scores[n] + bias[...]
        expo = jnp.exp(score - jnp.max(score, 1, keepdims=True))
        weights[n] = (expo * (1.0 / jnp.sum(expo, 1, keepdims=True))).astype(jnp.bfloat16)
    squares = [jnp.zeros((group_rows, TILE), jnp.float32) for _ in range(row_total // group_rows)]
    for n, (g, cols) in enumerate(tiles):
        q, key = keys_of(g, cols)
        out = dot(weights[n], key)
        value = q.astype(jnp.float32)
        for h in range(heads):
            value += jnp.where(lane == h, out[h * group_rows : (h + 1) * group_rows], 0.0)
        mixed[g * group_rows : (g + 1) * group_rows, cols] = value
        squares[g] += value * value
    square = jnp.concatenate(squares, 0)
    scale = lax.rsqrt(jnp.sum(square, 1, keepdims=True) / model_width + eps)
    out_ref[:, 0:model_width] = (mixed[...] * scale * gain_ref[...]).astype(jnp.bfloat16)
    marks = query[:, model_width:]
    out_ref[:, model_width:] = jnp.where(iota(marks.shape, 1) == 2, found.astype(jnp.bfloat16), marks)


def logits_kernel(order, pos_ref, mine_ref, other_ref, head_ref, length_ref, out_ref, states):
    half = mine_ref.shape[0]
    model_width = states.shape[1]
    row_total = 2 * half
    states[0:half, :] = mine_ref[:, 0:model_width]
    states[half:, :] = other_ref[:, 0:model_width]
    digits = jnp.concatenate(
        [ref[:, model_width:].astype(jnp.float32) for ref in (mine_ref, other_ref)], 0
    ).T
    vocab = head_ref.shape[0]
    ids = (digits[0:1] * DIGIT + digits[1:2]).astype(jnp.int32) - pos_ref[0] * vocab
    tops, totals, targets = [], [], []
    for i, j in cuts(vocab, -(-vocab // TILE)):
        values = dot_rows(head_ref[i:j, :], states[...])
        top = jnp.max(values, 0, keepdims=True)
        tops.append(top)
        totals.append(jnp.sum(jnp.exp(values - top), 0, keepdims=True))
        hit = iota(values.shape, 0) == ids - i
        targets.append(jnp.sum(jnp.where(hit, values, 0.0), 0, keepdims=True))
    top = functools.reduce(jnp.maximum, tops)
    total = sum(t * jnp.exp(m - top) for t, m in zip(totals, tops))
    shards, _, width = out_ref.shape
    rows = row_total // shards
    field = iota((SUBLANES, width), 1) // rows
    halves = []
    for start in range(0, shards, SUBLANES):
        half = jnp.zeros((SUBLANES, width), jnp.float32)
        for s, values in enumerate((top, total, sum(targets), length_ref[...])):
            shift = (s + 1 + start) * rows % width
            spread = jnp.broadcast_to(pltpu.roll(values, shift, 1) if shift else values, half.shape)
            half = jnp.where(field == s, pltpu.roll(spread, 0, 1, stride=rows, stride_axis=0), half)
        halves.append(half)
    packed = jnp.concatenate(halves, 0)
    for j in range(shards):
        away = order[j % len(order)] + j // len(order)
        out_ref[pos_ref[0] ^ away] = packed[shards - 1 - j : shards - j]


def finish_kernel(stats_ref, mine_ref, out_ref):
    shards, _, width = stats_ref.shape
    _, top_count, cap_len = out_ref.shape
    rows = top_count * cap_len
    tops = jnp.concatenate([stats_ref[e] for e in range(shards)], 0)
    totals, targets, lengths = (pltpu.roll(tops, width - s * rows, 1) for s in (1, 2, 3))
    marks = mine_ref[0:16, mine_ref.shape[1] - width :].astype(jnp.float32)
    cand = jnp.where(iota(marks.shape, 0) == iota(marks.shape, 1), marks[:, 2:3], 0.0)
    cand = jnp.sum(cand, 0, keepdims=True).astype(jnp.int32)
    length = jnp.sum(jnp.where(iota(tops.shape, 0) == cand, lengths, 0.0), 0, keepdims=True)
    top = jnp.max(tops, 0, keepdims=True)
    total = jnp.sum(totals * jnp.exp(tops - top), 0, keepdims=True)
    loglik = jnp.sum(targets, 0, keepdims=True) - (top + jnp.log(total))
    token = (iota(loglik.shape, 1) % cap_len).astype(jnp.float32)
    loglik = jnp.where(token < length, loglik, 0.0)
    for k in range(top_count):
        out_ref[0, k : k + 1, :] = loglik[:, k * cap_len : (k + 1) * cap_len]


def paired(
    query_rows, proj_weight, proj_bias, candidates, caption_states, caption_ids, caption_lengths, norm_gain, head_weight
):
    shards = lax.axis_size("dp")
    blocks = shards // 2
    _, prefix, width = query_rows.shape
    _, cap_len, model_width = caption_states.shape
    top_count = candidates.shape[1]
    pair_rows = top_count * cap_len
    piece_rows = cap_len * -(-model_width // width)
    held = -(-piece_rows // 16) * 16
    row_total = blocks * pair_rows
    position = lax.axis_index("dp").astype(jnp.int32).reshape(1)
    heads, group = TILE // HEAD_DIM, LANES // prefix
    score_tiles = model_width // TILE * blocks // group

    def swap(a, away):
        return lax.ppermute(a, "dp", [(i, i ^ away) for i in range(shards)])

    message = pl.pallas_call(
        pack_kernel,
        out_shape=jax.ShapeDtypeStruct((piece_rows + prefix, width), jnp.bfloat16),
        in_specs=[HBM] * 4,
        out_specs=VMEM,
        scratch_shapes=[
            pltpu.SMEM(candidates.shape, jnp.int32),
            pltpu.SMEM(caption_ids.shape, jnp.int32),
            pltpu.VMEM(query_rows.shape, jnp.bfloat16),
            pltpu.VMEM(caption_states.shape, jnp.bfloat16),
            pltpu.VMEM((piece_rows, width), jnp.float32),
            pltpu.SemaphoreType.DMA((4,)),
        ],
        compiler_params=pltpu.CompilerParams(vmem_limit_bytes=2 * MIB),
        name="pack",
    )(*(in_hbm(a) for a in (candidates, caption_ids, query_rows, caption_states)))

    got = {0: message}
    for away in (12, 2, 4):
        got[away] = swap(message, away)
    length = pl.pallas_call(
        length_kernel,
        out_shape=jax.ShapeDtypeStruct((1, LANES), jnp.float32),
        in_specs=[SMEM, SMEM] + [HBM] * 3,
        out_specs=VMEM,
        compiler_params=pltpu.CompilerParams(vmem_limit_bytes=MIB),
        name="length",
    )(position, caption_lengths, in_hbm(head_weight.T), in_hbm(head_weight.T), in_hbm(proj_weight))
    got[10] = swap(message, 10)
    got[6] = swap(got[4], 2)
    got[12], length = lax.optimization_barrier((got[12], length))
    got[8], got[14] = swap(got[12], 4), swap(got[12], 2)
    order = (0, 2, 4, 12, 6, 10, 14, 8)
    mine = [got[away] for away in order]

    def collect(msgs, *after):
        return pl.pallas_call(
            functools.partial(collect_kernel, len(msgs)),
            out_shape=jax.ShapeDtypeStruct((len(msgs) * held, width), jnp.bfloat16),
            in_specs=[VMEM] * len(msgs) + [ANY] * len(after),
            out_specs=VMEM,
            compiler_params=pltpu.CompilerParams(vmem_limit_bytes=2 * MIB),
            name="collect",
        )(*msgs, *after)


    def keys_of(msgs):
        rows = len(msgs) * prefix
        return pl.pallas_call(
            functools.partial(keys_kernel, len(msgs)),
            out_shape=pltpu.VMEM((rows, model_width), jnp.bfloat16),
            in_specs=[VMEM] * (len(msgs) + 2),
            out_specs=VMEM,
            scratch_shapes=[pltpu.VMEM((rows, width), jnp.bfloat16)],
            compiler_params=pltpu.CompilerParams(vmem_limit_bytes=8 * MIB),
            cost_estimate=pl.CostEstimate(
                flops=2 * rows * width * model_width, bytes_accessed=4 * width * model_width, transcendentals=0
            ),
            name="keys",
        )(*msgs, in_vmem(proj_weight), in_vmem(proj_bias))

    near, near_keys = collect(mine[: blocks // 2]), keys_of(mine[: blocks // 2])
    far, far_keys = collect(mine[blocks // 2 :], near_keys), keys_of(mine[blocks // 2 :])
    other_near, other_far = swap(near, 1), swap(far, 1)

    hidden = pl.pallas_call(
        functools.partial(hidden_kernel, order, prefix, cap_len),
        out_shape=jax.ShapeDtypeStruct((row_total, model_width + LANES), jnp.bfloat16),
        in_specs=[SMEM] + [VMEM] * 7,
        out_specs=VMEM,
        scratch_shapes=[
            pltpu.VMEM((2 * blocks * held, width), jnp.bfloat16),
            pltpu.VMEM((row_total, model_width + LANES), jnp.bfloat16),
            pltpu.VMEM((row_total, model_width), jnp.float32),
            pltpu.VMEM((heads * group * pair_rows, group * (prefix + pair_rows)), jnp.float32),
            pltpu.VMEM((score_tiles, heads * group * pair_rows, group * (prefix + pair_rows)), jnp.float32),
            pltpu.VMEM((score_tiles, heads * group * pair_rows, group * (prefix + pair_rows)), jnp.bfloat16),
        ],
        compiler_params=pltpu.CompilerParams(vmem_limit_bytes=16 * MIB),
        name="hidden",
    )(position, near, far, other_near, other_far, near_keys, far_keys, in_vmem(norm_gain.reshape(1, -1)))

    stats = pl.pallas_call(
        functools.partial(logits_kernel, order),
        out_shape=jax.ShapeDtypeStruct((shards, 1, LANES), jnp.float32),
        in_specs=[SMEM] + [VMEM] * 4,
        out_specs=VMEM,
        scratch_shapes=[pltpu.VMEM((2 * row_total, model_width), jnp.bfloat16)],
        compiler_params=pltpu.CompilerParams(vmem_limit_bytes=16 * MIB),
        name="logits",
    )(position, hidden, swap(hidden, 1), in_vmem(head_weight.T), length)

    stats = lax.all_to_all(stats, "dp", 0, 0, tiled=True)
    return pl.pallas_call(
        finish_kernel,
        out_shape=jax.ShapeDtypeStruct((1, top_count, cap_len), jnp.float32),
        in_specs=[VMEM, VMEM],
        out_specs=VMEM,
        compiler_params=pltpu.CompilerParams(vmem_limit_bytes=2 * MIB),
        name="finish",
    )(stats, hidden)


def merged(part, axis, combine):
    gathered = jax.tree.map(lambda a: lax.all_gather(a, axis), part)

    def take(source):
        return jax.tree.map(lambda a: lax.dynamic_index_in_dim(a, source, 0, False), gathered)

    return lax.fori_loop(
        1, lax.axis_size(axis), lambda source, state: combine(state, take(source)), take(0)
    )


def project(rows, proj_weight, proj_bias):
    row_total, prefix_len, query_width = rows.shape
    summed = jnp.dot(
        rows.reshape(row_total * prefix_len, query_width),
        proj_weight,
        preferred_element_type=jnp.float32,
    )
    projected = (summed + proj_bias.astype(jnp.float32)).astype(jnp.bfloat16)
    return projected.reshape(row_total, prefix_len, proj_weight.shape[1])


def attend(projected, states, norm_gain):
    prefix_len = projected.shape[0]
    cap_len, model_width = states.shape
    heads = model_width // HEAD_DIM
    keys = jnp.concatenate([projected, states], 0)
    query = states.reshape(cap_len, heads, HEAD_DIM)
    keyed = keys.reshape(prefix_len + cap_len, heads, HEAD_DIM)
    scores = (
        jnp.einsum("thd,jhd->htj", query, keyed, preferred_element_type=jnp.float32) * score_scale
    )
    key_pos = jnp.arange(prefix_len + cap_len)[None, :]
    tok_pos = jnp.arange(cap_len)[:, None]
    allowed = (key_pos < prefix_len) | (key_pos - prefix_len <= tok_pos)
    scores = jnp.where(allowed[None], scores, -jnp.inf)
    row_max = jnp.max(scores, -1, keepdims=True)
    expo = jnp.exp(scores - row_max)
    weights = (expo / jnp.sum(expo, -1, keepdims=True)).astype(jnp.bfloat16)
    mixed_out = jnp.einsum(
        "htj,jhd->thd", weights, keyed, preferred_element_type=jnp.float32
    ).reshape(cap_len, model_width)
    mixed = states.astype(jnp.float32) + mixed_out
    normed = mixed * lax.rsqrt(jnp.mean(mixed * mixed, -1, keepdims=True) + eps) * norm_gain
    return normed.astype(jnp.bfloat16)


def merge_totals(first, second):
    larger = jnp.maximum(first[0], second[0])
    summed = first[1] * jnp.exp(first[0] - larger) + second[1] * jnp.exp(second[0] - larger)
    return (larger, summed, first[2] + second[2])


def spread(
    query_rows,
    proj_weight,
    proj_bias,
    candidates,
    caption_states,
    caption_ids,
    caption_lengths,
    norm_gain,
    head_weight,
):
    position = lax.axis_index("dp")
    img_local, top_count = candidates.shape
    pair_count = img_local * top_count
    cap_local, cap_len, model_width = caption_states.shape
    own_cand = candidates.reshape(pair_count)
    all_cand, all_len = (
        lax.all_gather(candidates, "dp", axis=0, tiled=True),
        lax.all_gather(caption_lengths, "dp", axis=0, tiled=True),
    )
    caption_total = all_len.shape[0]
    length_match = own_cand[:, None] == jnp.arange(caption_total)[None, :]
    pair_len = jnp.sum(jnp.where(length_match, all_len[None, :], 0), 1)
    piece_states = lax.all_gather(caption_states, "dp", axis=0, tiled=True)
    piece_ids = lax.all_gather(caption_ids, "dp", axis=0, tiled=True)
    piece_rows = piece_states.shape[0]
    matches = own_cand[:, None] == jnp.arange(piece_rows)[None, :]
    picked = jnp.dot(
        matches.astype(jnp.bfloat16),
        piece_states.reshape(piece_rows, cap_len * model_width),
        preferred_element_type=jnp.float32,
    )
    fetched_ids = jnp.sum(jnp.where(matches[:, :, None], piece_ids[None, :, :], 0), 1).astype(
        jnp.int32
    )
    pair_states = picked.astype(jnp.bfloat16).reshape(pair_count, cap_len, model_width)
    image_proj = project(query_rows, proj_weight, proj_bias)
    pair_proj = jnp.repeat(image_proj, top_count, axis=0)
    work_hidden = jax.vmap(lambda one, two: attend(one, two, norm_gain))(pair_proj, pair_states)
    row_base = (position * pair_count + jnp.arange(pair_count)) * cap_len
    row_count = work_hidden.shape[0] * cap_len
    hidden_rows = work_hidden.reshape(row_count, model_width)
    id_rows = fetched_ids.reshape(row_count)
    vocab_dev = head_weight.shape[1]
    vocab_start = position * vocab_dev
    every_state, every_id = (
        lax.all_gather(hidden_rows, "dp", axis=0, tiled=True),
        lax.all_gather(id_rows, "dp", axis=0, tiled=True),
    )
    logits = jnp.dot(every_state, head_weight, preferred_element_type=jnp.float32)
    local_max = jnp.max(logits, 1)
    local_sum = jnp.sum(jnp.exp(logits - local_max[:, None]), 1)
    target_hit = jnp.arange(vocab_dev)[None, :] == (every_id - vocab_start)[:, None]
    local_pick = jnp.sum(jnp.where(target_hit, logits, 0.0), 1)
    top_all, sum_all, picked_all = merged((local_max, local_sum, local_pick), "dp", merge_totals)
    row_index = row_base[:, None] + jnp.arange(cap_len)[None, :]
    own_top = jnp.take(top_all, row_index)
    own_sum = jnp.take(sum_all, row_index)
    own_picked = jnp.take(picked_all, row_index)
    loglik = own_picked - (own_top + jnp.log(own_sum))
    inside = jnp.arange(cap_len)[None, :] < pair_len[:, None]
    result = jnp.where(inside, loglik, jnp.float32(0.0))
    return result.reshape(img_local, top_count, cap_len)


def local(query_rows, proj_weight, proj_bias, candidates, caption_states, *rest):
    one_each = candidates.shape[0] == 1 and caption_states.shape[0] == 1
    fits = candidates.shape[1] == 2 and caption_states.shape[1] == 4 and query_rows.shape[1] == 32
    plan = paired if lax.axis_size("dp") == 16 and one_each and fits else spread
    return plan(query_rows, proj_weight, proj_bias, candidates, caption_states, *rest)


def solution(mesh):
    in_specs = (
        P(("groups", "dp"), None, None),
        P(),
        P(),
        P(("groups", "dp"), None),
        P(("groups", "dp"), None, None),
        P(("groups", "dp"), None),
        P(("groups", "dp")),
        P(),
        P(None, "dp"),
    )
    out_specs = P(("groups", "dp"), None, None)
    return jax.shard_map(local, mesh=mesh, in_specs=in_specs, out_specs=out_specs, check_vma=False)
```

```python
import functools

import jax
import jax.numpy as jnp
from jax import lax
from jax.experimental import pallas as pl
from jax.experimental.pallas import tpu as pltpu
from jax.sharding import PartitionSpec as P

HEAD_DIM = 64
LANES = 128
SUBLANES = 8
TILE = 256
DIGIT = 256
MIB = 1 << 20


score_scale = 0.015625
eps = 1e-06

VMEM = pl.BlockSpec(memory_space=pltpu.VMEM)
SMEM = pl.BlockSpec(memory_space=pltpu.SMEM)
HBM = pl.BlockSpec(memory_space=pltpu.HBM)
ANY = pl.BlockSpec(memory_space=pl.ANY)
ROWS_BY_ROWS = (((1,), (1,)), ((), ()))


def iota(shape, dim):
    return lax.broadcasted_iota(jnp.int32, shape, dim)


def in_hbm(a):
    return pltpu.with_memory_space_constraint(a, pltpu.HBM)


def in_vmem(a):
    return pltpu.with_memory_space_constraint(a, pltpu.VMEM)


def dot(a, b):
    return jnp.dot(a, b, preferred_element_type=jnp.float32)


def dot_rows(a, b):
    return lax.dot_general(a, b, ROWS_BY_ROWS, preferred_element_type=jnp.float32)


def pack_kernel(cand_hbm, ids_hbm, rows_hbm, states_hbm, out_ref, cand, ids, rows, states, stage, sem):
    copies = [
        pltpu.make_async_copy(src, dst, sem.at[i])
        for i, (src, dst) in enumerate(
            ((cand_hbm, cand), (ids_hbm, ids), (rows_hbm, rows), (states_hbm, states))
        )
    ]
    for copy in copies:
        copy.start()
    for copy in copies:
        copy.wait()
    width = rows.shape[2]
    cap_len, model_width = states.shape[1:]
    pieces = -(-model_width // width)
    held = pieces * cap_len
    values = states[0].astype(jnp.float32)
    for c in range(pieces - 1):
        stage[c * cap_len : (c + 1) * cap_len, :] = values[:, c * width : (c + 1) * width]
    rest = model_width - (pieces - 1) * width
    last = held - cap_len
    stage[last:held, 0:rest] = values[:, model_width - rest :]
    token, lane = iota((cap_len, width - rest), 0), iota((cap_len, width - rest), 1)
    digits = jnp.zeros_like(token)
    for t in range(cap_len):
        digits = jnp.where(token == t, jnp.where(lane == 0, ids[0, t] // DIGIT, ids[0, t] % DIGIT), digits)
    digits = jnp.where(lane < 2, digits, 0)
    for k in range(cand.shape[1]):
        digits = jnp.where(lane == 2 + 2 * k, cand[0, k] // DIGIT, digits)
        digits = jnp.where(lane == 3 + 2 * k, cand[0, k] % DIGIT, digits)
    stage[last:held, rest:] = digits.astype(jnp.float32)
    out_ref[0:held, :] = stage[...].astype(jnp.bfloat16)
    out_ref[held:, :] = rows[0]


def length_kernel(pos_ref, len_ref, *refs):
    length_ref = refs[-1]
    length_ref[...] = jnp.full(length_ref.shape, len_ref[0].astype(jnp.float32))


def cuts(total, parts):
    piece = -(-total // parts // 16) * 16
    return [(i, min(total, i + piece)) for i in range(0, total, piece)]


def collect_kernel(count, *refs):
    msgs, out_ref = refs[:count], refs[-1]
    held = out_ref.shape[0] // count
    for i, msg in enumerate(msgs):
        out_ref[i * held : (i + 1) * held, :] = msg[0:held, :]


def keys_kernel(blocks, *refs):
    msgs, (weight, bias, keys, rows) = refs[:blocks], refs[blocks:]
    prefix = rows.shape[0] // blocks
    for j, msg in enumerate(msgs):
        rows[j * prefix : (j + 1) * prefix, :] = msg[msg.shape[0] - prefix :, :]
    step = 512
    bias = bias[...].astype(jnp.float32).reshape(1, keys.shape[1])
    for i in range(0, keys.shape[1], step):
        summed = dot(rows[...], weight[:, i : i + step])
        keys[:, i : i + step] = (summed + bias[:, i : i + step]).astype(jnp.bfloat16)


def hidden_kernel(order, prefix, cap_len, *refs):
    pos_ref, *cap_refs = refs[:5]
    near_keys, far_keys, gain_ref, out_ref, caps, query, mixed, bias, scores, weights = refs[5:]
    blocks = len(order)
    width = caps.shape[1]
    model_width = mixed.shape[1]
    row_total = query.shape[0]
    held, pair_rows = caps.shape[0] // (2 * blocks), row_total // blocks
    pieces = -(-model_width // width)

    start = 0
    for ref in cap_refs:
        caps[start : start + ref.shape[0], :] = ref[...]
        start += ref.shape[0]
    rest = model_width - (pieces - 1) * width
    last = (pieces - 2) * cap_len
    row, lane = iota((pair_rows, LANES), 0), iota((pair_rows, LANES), 1)
    place = 2 + 2 * (row // cap_len)
    factor = jnp.where(lane == place, float(DIGIT), jnp.where(lane == place + 1, 1.0, 0.0))
    found = []
    for s in range(blocks):
        digits = caps[s * held + last : s * held + last + pair_rows, rest : rest + LANES].astype(jnp.float32)
        digits = jnp.where(row < cap_len, pltpu.roll(digits, cap_len, 0), digits)
        found.append(jnp.sum(digits * factor, 1, keepdims=True))
    found = jnp.concatenate(found, 0)
    away = found.astype(jnp.int32) ^ pos_ref[0]
    block = (away & 1) * blocks
    for s, distance in enumerate(order):
        block += jnp.where(away - (away & 1) == distance, s, 0)
    first = block * held + iota((row_total, 1), 0) % cap_len
    column = iota((row_total, 2 * blocks * held), 1)
    pick = jnp.concatenate(
        [jnp.where(column == first + c * cap_len, 1.0, 0.0).astype(jnp.bfloat16) for c in range(pieces)], 0
    )
    picked = dot(pick, caps[...]).astype(jnp.bfloat16)
    for c in range(pieces):
        part = min(width, query.shape[1] - c * width)
        query[:, c * width : c * width + part] = picked[c * row_total : (c + 1) * row_total, 0:part]

    heads = TILE // HEAD_DIM
    group_rows = bias.shape[0] // heads
    image_keys = bias.shape[1] - group_rows
    lane = iota((group_rows, TILE), 1) // HEAD_DIM
    r, k = iota(bias.shape, 0) % group_rows, iota(bias.shape, 1)
    own = k - image_keys
    allowed = ((k < image_keys) & (k // prefix == r // pair_rows)) | (
        (own >= 0) & (own <= r) & (own // cap_len == r // cap_len)
    )
    bias[...] = jnp.where(allowed, 0.0, -1e30)
    tiles = [
        (g, slice(i * TILE, (i + 1) * TILE))
        for i in range(model_width // TILE)
        for g in range(row_total // group_rows)
    ]

    def keys_of(g, cols):
        q = query[g * group_rows : (g + 1) * group_rows, cols]
        return q, jnp.concatenate([(near_keys, far_keys)[g][:, cols], q], 0)

    for n, (g, cols) in enumerate(tiles):
        q, key = keys_of(g, cols)
        scaled, zero = q * score_scale, jnp.zeros_like(q)
        every = jnp.concatenate([jnp.where(lane == h, scaled, zero) for h in range(heads)], 0)
        scores[n] = dot_rows(every, key)
    for n in range(len(tiles)):
        score = scores[n] + bias[...]
        expo = jnp.exp(score - jnp.max(score, 1, keepdims=True))
        weights[n] = (expo * (1.0 / jnp.sum(expo, 1, keepdims=True))).astype(jnp.bfloat16)
    squares = [jnp.zeros((group_rows, TILE), jnp.float32) for _ in range(row_total // group_rows)]
    for n, (g, cols) in enumerate(tiles):
        q, key = keys_of(g, cols)
        out = dot(weights[n], key)
        mine = out[0:group_rows]
        for h in range(1, heads):
            mine = jnp.where(lane == h, out[h * group_rows : (h + 1) * group_rows], mine)
        value = q.astype(jnp.float32) + mine
        mixed[g * group_rows : (g + 1) * group_rows, cols] = value
        squares[g] += value * value
    square = jnp.concatenate(squares, 0)
    scale = lax.rsqrt(jnp.sum(square, 1, keepdims=True) / model_width + eps)
    out_ref[:, 0:model_width] = (mixed[...] * scale * gain_ref[...]).astype(jnp.bfloat16)
    marks = query[:, model_width:]
    out_ref[:, model_width:] = jnp.where(iota(marks.shape, 1) == 2, found.astype(jnp.bfloat16), marks)


def logits_kernel(order, pos_ref, mine_ref, other_ref, head_ref, length_ref, out_ref, states):
    half = mine_ref.shape[0]
    model_width = states.shape[1]
    row_total = 2 * half
    states[0:half, :] = mine_ref[:, 0:model_width]
    states[half:, :] = other_ref[:, 0:model_width]
    digits = jnp.concatenate(
        [ref[:, model_width:].astype(jnp.float32) for ref in (mine_ref, other_ref)], 0
    ).T
    vocab = head_ref.shape[0]
    ids = (digits[0:1] * DIGIT + digits[1:2]).astype(jnp.int32) - pos_ref[0] * vocab
    tops, totals, targets = [], [], []
    for i, j in cuts(vocab, -(-vocab // TILE)):
        values = dot_rows(head_ref[i:j, :], states[...])
        top = jnp.max(values, 0, keepdims=True)
        tops.append(top)
        totals.append(jnp.sum(jnp.exp(values - top), 0, keepdims=True))
        hit = iota(values.shape, 0) == ids - i
        targets.append(jnp.sum(jnp.where(hit, values, 0.0), 0, keepdims=True))
    top = functools.reduce(jnp.maximum, tops)
    total = sum(t * jnp.exp(m - top) for t, m in zip(totals, tops))
    shards, _, width = out_ref.shape
    rows = row_total // shards
    field = iota((SUBLANES, width), 1) // rows
    halves = []
    for start in range(0, shards, SUBLANES):
        half = jnp.zeros((SUBLANES, width), jnp.float32)
        for s, values in enumerate((top, total, sum(targets), length_ref[...])):
            shift = (s + 1 + start) * rows % width
            spread = jnp.broadcast_to(pltpu.roll(values, shift, 1) if shift else values, half.shape)
            half = jnp.where(field == s, pltpu.roll(spread, 0, 1, stride=rows, stride_axis=0), half)
        halves.append(half)
    packed = jnp.concatenate(halves, 0)
    for j in range(shards):
        away = order[j % len(order)] + j // len(order)
        out_ref[pos_ref[0] ^ away] = packed[shards - 1 - j : shards - j]


def finish_kernel(stats_ref, mine_ref, out_ref):
    shards, _, width = stats_ref.shape
    _, top_count, cap_len = out_ref.shape
    rows = top_count * cap_len
    tops = jnp.concatenate([stats_ref[e] for e in range(shards)], 0)
    totals, targets, lengths = (pltpu.roll(tops, width - s * rows, 1) for s in (1, 2, 3))
    marks = mine_ref[0:16, mine_ref.shape[1] - width :].astype(jnp.float32)
    cand = jnp.where(iota(marks.shape, 0) == iota(marks.shape, 1), marks[:, 2:3], 0.0)
    cand = jnp.sum(cand, 0, keepdims=True).astype(jnp.int32)
    length = jnp.sum(jnp.where(iota(tops.shape, 0) == cand, lengths, 0.0), 0, keepdims=True)
    top = jnp.max(tops, 0, keepdims=True)
    total = jnp.sum(totals * jnp.exp(tops - top), 0, keepdims=True)
    loglik = jnp.sum(targets, 0, keepdims=True) - (top + jnp.log(total))
    token = (iota(loglik.shape, 1) % cap_len).astype(jnp.float32)
    loglik = jnp.where(token < length, loglik, 0.0)
    for k in range(top_count):
        out_ref[0, k : k + 1, :] = loglik[:, k * cap_len : (k + 1) * cap_len]


def paired(
    query_rows, proj_weight, proj_bias, candidates, caption_states, caption_ids, caption_lengths, norm_gain, head_weight
):
    shards = lax.axis_size("dp")
    blocks = shards // 2
    _, prefix, width = query_rows.shape
    _, cap_len, model_width = caption_states.shape
    top_count = candidates.shape[1]
    pair_rows = top_count * cap_len
    piece_rows = cap_len * -(-model_width // width)
    held = -(-piece_rows // 16) * 16
    row_total = blocks * pair_rows
    position = lax.axis_index("dp").astype(jnp.int32).reshape(1)
    heads, group = TILE // HEAD_DIM, LANES // prefix
    score_tiles = model_width // TILE * blocks // group

    def swap(a, away):
        return lax.ppermute(a, "dp", [(i, i ^ away) for i in range(shards)])

    message = pl.pallas_call(
        pack_kernel,
        out_shape=jax.ShapeDtypeStruct((piece_rows + prefix, width), jnp.bfloat16),
        in_specs=[HBM] * 4,
        out_specs=VMEM,
        scratch_shapes=[
            pltpu.SMEM(candidates.shape, jnp.int32),
            pltpu.SMEM(caption_ids.shape, jnp.int32),
            pltpu.VMEM(query_rows.shape, jnp.bfloat16),
            pltpu.VMEM(caption_states.shape, jnp.bfloat16),
            pltpu.VMEM((piece_rows, width), jnp.float32),
            pltpu.SemaphoreType.DMA((4,)),
        ],
        compiler_params=pltpu.CompilerParams(vmem_limit_bytes=2 * MIB),
        name="pack",
    )(*(in_hbm(a) for a in (candidates, caption_ids, query_rows, caption_states)))

    got = {0: message}
    for away in (12, 2, 4):
        got[away] = swap(message, away)
    length = pl.pallas_call(
        length_kernel,
        out_shape=jax.ShapeDtypeStruct((1, LANES), jnp.float32),
        in_specs=[SMEM, SMEM] + [HBM] * 3,
        out_specs=VMEM,
        compiler_params=pltpu.CompilerParams(vmem_limit_bytes=MIB),
        name="length",
    )(position, caption_lengths, in_hbm(head_weight.T), in_hbm(head_weight.T), in_hbm(proj_weight))
    got[10] = swap(message, 10)
    got[6] = swap(got[4], 2)
    got[12], length = lax.optimization_barrier((got[12], length))
    got[8], got[14] = swap(got[12], 4), swap(got[12], 2)
    order = (0, 2, 4, 12, 6, 10, 14, 8)
    mine = [got[away] for away in order]

    def collect(msgs, *after):
        return pl.pallas_call(
            functools.partial(collect_kernel, len(msgs)),
            out_shape=jax.ShapeDtypeStruct((len(msgs) * held, width), jnp.bfloat16),
            in_specs=[VMEM] * len(msgs) + [ANY] * len(after),
            out_specs=VMEM,
            compiler_params=pltpu.CompilerParams(vmem_limit_bytes=2 * MIB),
            name="collect",
        )(*msgs, *after)


    def keys_of(msgs):
        rows = len(msgs) * prefix
        return pl.pallas_call(
            functools.partial(keys_kernel, len(msgs)),
            out_shape=pltpu.VMEM((rows, model_width), jnp.bfloat16),
            in_specs=[VMEM] * (len(msgs) + 2),
            out_specs=VMEM,
            scratch_shapes=[pltpu.VMEM((rows, width), jnp.bfloat16)],
            compiler_params=pltpu.CompilerParams(vmem_limit_bytes=8 * MIB),
            cost_estimate=pl.CostEstimate(
                flops=2 * rows * width * model_width, bytes_accessed=4 * width * model_width, transcendentals=0
            ),
            name="keys",
        )(*msgs, in_vmem(proj_weight), in_vmem(proj_bias))

    near, near_keys = collect(mine[: blocks // 2]), keys_of(mine[: blocks // 2])
    far, far_keys = collect(mine[blocks // 2 :], near_keys), keys_of(mine[blocks // 2 :])
    other_near, other_far = swap(near, 1), swap(far, 1)

    hidden = pl.pallas_call(
        functools.partial(hidden_kernel, order, prefix, cap_len),
        out_shape=jax.ShapeDtypeStruct((row_total, model_width + LANES), jnp.bfloat16),
        in_specs=[SMEM] + [VMEM] * 7,
        out_specs=VMEM,
        scratch_shapes=[
            pltpu.VMEM((2 * blocks * held, width), jnp.bfloat16),
            pltpu.VMEM((row_total, model_width + LANES), jnp.bfloat16),
            pltpu.VMEM((row_total, model_width), jnp.float32),
            pltpu.VMEM((heads * group * pair_rows, group * (prefix + pair_rows)), jnp.float32),
            pltpu.VMEM((score_tiles, heads * group * pair_rows, group * (prefix + pair_rows)), jnp.float32),
            pltpu.VMEM((score_tiles, heads * group * pair_rows, group * (prefix + pair_rows)), jnp.bfloat16),
        ],
        compiler_params=pltpu.CompilerParams(vmem_limit_bytes=16 * MIB),
        name="hidden",
    )(position, near, far, other_near, other_far, near_keys, far_keys, in_vmem(norm_gain.reshape(1, -1)))

    stats = pl.pallas_call(
        functools.partial(logits_kernel, order),
        out_shape=jax.ShapeDtypeStruct((shards, 1, LANES), jnp.float32),
        in_specs=[SMEM] + [VMEM] * 4,
        out_specs=VMEM,
        scratch_shapes=[pltpu.VMEM((2 * row_total, model_width), jnp.bfloat16)],
        compiler_params=pltpu.CompilerParams(vmem_limit_bytes=16 * MIB),
        name="logits",
    )(position, hidden, swap(hidden, 1), in_vmem(head_weight.T), length)

    stats = lax.all_to_all(stats, "dp", 0, 0, tiled=True)
    return pl.pallas_call(
        finish_kernel,
        out_shape=jax.ShapeDtypeStruct((1, top_count, cap_len), jnp.float32),
        in_specs=[VMEM, VMEM],
        out_specs=VMEM,
        compiler_params=pltpu.CompilerParams(vmem_limit_bytes=2 * MIB),
        name="finish",
    )(stats, hidden)


def merged(part, axis, combine):
    gathered = jax.tree.map(lambda a: lax.all_gather(a, axis), part)

    def take(source):
        return jax.tree.map(lambda a: lax.dynamic_index_in_dim(a, source, 0, False), gathered)

    return lax.fori_loop(
        1, lax.axis_size(axis), lambda source, state: combine(state, take(source)), take(0)
    )


def project(rows, proj_weight, proj_bias):
    row_total, prefix_len, query_width = rows.shape
    summed = jnp.dot(
        rows.reshape(row_total * prefix_len, query_width),
        proj_weight,
        preferred_element_type=jnp.float32,
    )
    projected = (summed + proj_bias.astype(jnp.float32)).astype(jnp.bfloat16)
    return projected.reshape(row_total, prefix_len, proj_weight.shape[1])


def attend(projected, states, norm_gain):
    prefix_len = projected.shape[0]
    cap_len, model_width = states.shape
    heads = model_width // HEAD_DIM
    keys = jnp.concatenate([projected, states], 0)
    query = states.reshape(cap_len, heads, HEAD_DIM)
    keyed = keys.reshape(prefix_len + cap_len, heads, HEAD_DIM)
    scores = (
        jnp.einsum("thd,jhd->htj", query, keyed, preferred_element_type=jnp.float32) * score_scale
    )
    key_pos = jnp.arange(prefix_len + cap_len)[None, :]
    tok_pos = jnp.arange(cap_len)[:, None]
    allowed = (key_pos < prefix_len) | (key_pos - prefix_len <= tok_pos)
    scores = jnp.where(allowed[None], scores, -jnp.inf)
    row_max = jnp.max(scores, -1, keepdims=True)
    expo = jnp.exp(scores - row_max)
    weights = (expo / jnp.sum(expo, -1, keepdims=True)).astype(jnp.bfloat16)
    mixed_out = jnp.einsum(
        "htj,jhd->thd", weights, keyed, preferred_element_type=jnp.float32
    ).reshape(cap_len, model_width)
    mixed = states.astype(jnp.float32) + mixed_out
    normed = mixed * lax.rsqrt(jnp.mean(mixed * mixed, -1, keepdims=True) + eps) * norm_gain
    return normed.astype(jnp.bfloat16)


def merge_totals(first, second):
    larger = jnp.maximum(first[0], second[0])
    summed = first[1] * jnp.exp(first[0] - larger) + second[1] * jnp.exp(second[0] - larger)
    return (larger, summed, first[2] + second[2])


def spread(
    query_rows,
    proj_weight,
    proj_bias,
    candidates,
    caption_states,
    caption_ids,
    caption_lengths,
    norm_gain,
    head_weight,
):
    position = lax.axis_index("dp")
    img_local, top_count = candidates.shape
    pair_count = img_local * top_count
    cap_local, cap_len, model_width = caption_states.shape
    own_cand = candidates.reshape(pair_count)
    all_cand, all_len = (
        lax.all_gather(candidates, "dp", axis=0, tiled=True),
        lax.all_gather(caption_lengths, "dp", axis=0, tiled=True),
    )
    caption_total = all_len.shape[0]
    length_match = own_cand[:, None] == jnp.arange(caption_total)[None, :]
    pair_len = jnp.sum(jnp.where(length_match, all_len[None, :], 0), 1)
    piece_states = lax.all_gather(caption_states, "dp", axis=0, tiled=True)
    piece_ids = lax.all_gather(caption_ids, "dp", axis=0, tiled=True)
    piece_rows = piece_states.shape[0]
    matches = own_cand[:, None] == jnp.arange(piece_rows)[None, :]
    picked = jnp.dot(
        matches.astype(jnp.bfloat16),
        piece_states.reshape(piece_rows, cap_len * model_width),
        preferred_element_type=jnp.float32,
    )
    fetched_ids = jnp.sum(jnp.where(matches[:, :, None], piece_ids[None, :, :], 0), 1).astype(
        jnp.int32
    )
    pair_states = picked.astype(jnp.bfloat16).reshape(pair_count, cap_len, model_width)
    image_proj = project(query_rows, proj_weight, proj_bias)
    pair_proj = jnp.repeat(image_proj, top_count, axis=0)
    work_hidden = jax.vmap(lambda one, two: attend(one, two, norm_gain))(pair_proj, pair_states)
    row_base = (position * pair_count + jnp.arange(pair_count)) * cap_len
    row_count = work_hidden.shape[0] * cap_len
    hidden_rows = work_hidden.reshape(row_count, model_width)
    id_rows = fetched_ids.reshape(row_count)
    vocab_dev = head_weight.shape[1]
    vocab_start = position * vocab_dev
    every_state, every_id = (
        lax.all_gather(hidden_rows, "dp", axis=0, tiled=True),
        lax.all_gather(id_rows, "dp", axis=0, tiled=True),
    )
    logits = jnp.dot(every_state, head_weight, preferred_element_type=jnp.float32)
    local_max = jnp.max(logits, 1)
    local_sum = jnp.sum(jnp.exp(logits - local_max[:, None]), 1)
    target_hit = jnp.arange(vocab_dev)[None, :] == (every_id - vocab_start)[:, None]
    local_pick = jnp.sum(jnp.where(target_hit, logits, 0.0), 1)
    top_all, sum_all, picked_all = merged((local_max, local_sum, local_pick), "dp", merge_totals)
    row_index = row_base[:, None] + jnp.arange(cap_len)[None, :]
    own_top = jnp.take(top_all, row_index)
    own_sum = jnp.take(sum_all, row_index)
    own_picked = jnp.take(picked_all, row_index)
    loglik = own_picked - (own_top + jnp.log(own_sum))
    inside = jnp.arange(cap_len)[None, :] < pair_len[:, None]
    result = jnp.where(inside, loglik, jnp.float32(0.0))
    return result.reshape(img_local, top_count, cap_len)


def local(query_rows, proj_weight, proj_bias, candidates, caption_states, *rest):
    one_each = candidates.shape[0] == 1 and caption_states.shape[0] == 1
    fits = candidates.shape[1] == 2 and caption_states.shape[1] == 4 and query_rows.shape[1] == 32
    plan = paired if lax.axis_size("dp") == 16 and one_each and fits else spread
    return plan(query_rows, proj_weight, proj_bias, candidates, caption_states, *rest)


def solution(mesh):
    in_specs = (
        P(("groups", "dp"), None, None),
        P(),
        P(),
        P(("groups", "dp"), None),
        P(("groups", "dp"), None, None),
        P(("groups", "dp"), None),
        P(("groups", "dp")),
        P(),
        P(None, "dp"),
    )
    out_specs = P(("groups", "dp"), None, None)
    return jax.shard_map(local, mesh=mesh, in_specs=in_specs, out_specs=out_specs, check_vma=False)
```
